32 devices in a mesh: res: 16 (over z, y, x), nbr: 2 (over core).
Axes of the slice: x: 2, y: 2, z: 4, core: 2. Of those that a mesh axis runs over, the one named last changes fastest.
Arguments:
- nodes: bfloat16 [16384, 512], P(('res', 'nbr')), may hold values from -6 to 6
- edges: bfloat16 [16384, 60, 192], P('res', 'nbr'), may hold values from -6 to 6
- neighbours: int32 [16384, 60], P('res', 'nbr'), may hold values from 0 to 16383, as said below
- lengths: int32 [16], replicated, may hold values from 60 to 1024, as said below
- message_receiver_weight: bfloat16 [512, 512], replicated, may hold values from -0.15625 to 0.15625
- message_neighbour_weight: bfloat16 [512, 512], replicated, may hold values from -0.15625 to 0.15625
- message_edge_weight: bfloat16 [192, 512], replicated, may hold values from -0.15625 to 0.15625
- message_hidden_bias: float32 [512], replicated, may hold values from -3 to 3
- message_output_weight: bfloat16 [512, 512], replicated, may hold values from -1 to 1
- gain_one: float32 [512], replicated, may hold values from 0.25 to 1.75
- ffn_in: bfloat16 [512, 2048], replicated, may hold values from -0.25 to 0.25
- ffn_bias: float32 [2048], replicated, may hold values from -3 to 3
- ffn_out: bfloat16 [2048, 512], replicated, may hold values from -0.125 to 0.125
- gain_two: float32 [512], replicated, may hold values from 0.25 to 1.75
- edge_update_residue_weight: bfloat16 [512, 192], replicated, may hold values from -0.15625 to 0.15625
- edge_update_neighbour_weight: bfloat16 [512, 192], replicated, may hold values from -0.15625 to 0.15625
- edge_update_edge_weight: bfloat16 [192, 192], replicated, may hold values from -0.15625 to 0.15625
- edge_update_bias: float32 [192], replicated, may hold values from -3 to 3
- edge_out: bfloat16 [192, 192], replicated, may hold values from -0.4375 to 0.4375
- gain_three: float32 [192], replicated, may hold values from 0.25 to 1.75
- node_cot: bfloat16 [16384, 512], P(('res', 'nbr')), may hold values from -6 to 6
- edge_cot: bfloat16 [16384, 60, 192], P('res', 'nbr'), may hold values from -6 to 6
Outputs:
- node_out: bfloat16 [16384, 512], P(('res', 'nbr'))
- edge_new: bfloat16 [16384, 60, 192], P('res', 'nbr')
- node_grad: float32 [16384, 512], P(('res', 'nbr'))
- edge_grad: float32 [16384, 60, 192], P('res', 'nbr')
- grad_msg_self: float32 [512, 512], replicated
- grad_msg_nbr: float32 [512, 512], replicated
- grad_msg_edge: float32 [192, 512], replicated
- grad_msg_bias: float32 [512], replicated
- grad_msg_out: float32 [512, 512], replicated
- grad_gain_one: float32 [512], replicated
- grad_ffn_in: float32 [512, 2048], replicated
- grad_ffn_bias: float32 [2048], replicated
- grad_ffn_out: float32 [2048, 512], replicated
- grad_gain_two: float32 [512], replicated
- grad_edge_self: float32 [512, 192], replicated
- grad_edge_nbr: float32 [512, 192], replicated
- grad_edge_edge: float32 [192, 192], replicated
- grad_edge_bias: float32 [192], replicated
- grad_edge_out: float32 [192, 192], replicated
- grad_gain_three: float32 [192], replicated
The draws below stay inside these ranges and needn't reach their ends.
Inputs may be any that keep to these rules, and one draw needn't show every extreme that they name: `neighbours`: every entry names a slot of the residue's own bucket, slots b * 1024 to (b + 1) * 1024 - 1 for bucket b. Even-numbered entries lie within 30 positions of the residue, inside its protein where the residue is a real one; odd-numbered entries lie anywhere in the bucket, padding slots included. `lengths`: the last bucket holds a protein of 1024 residues; the others vary.
All inputs are finite; a program needn't handle non-finite values.
Results may differ from the reference program's by a relative error of at most 0.014.
Values may be sent and summed in bfloat16 or wider, within the bound.
No kernel may reach another device: no remote copies, remote signals or barrier semaphores. Data moves between devices by JAX's collectives and lax.ppermute only.
A program may use at most 576 MiB of HBM per device.

```python
import math
import jax
import jax.numpy as jnp
from jax import lax

D = 512
E = 192
K = 60
FF = 2048
SPAN = 1024
MIN_LEN = 60
BUCKETS = 16
NODES = 16384


def protein_lengths(key):
    key = jax.random.fold_in(key, 101)
    drawn_len = jax.random.randint(jax.random.fold_in(key, 2), (BUCKETS,), MIN_LEN, SPAN + 1)
    return jnp.where(jnp.arange(BUCKETS) == BUCKETS - 1, SPAN, drawn_len).astype(jnp.int32)


def draw_lengths(key, part):
    return protein_lengths(key)


def draw_neighbours(key, part):
    true_lengths = protein_lengths(key)
    key = jax.random.fold_in(key, 7)
    slot_ids = jnp.arange(NODES, dtype=jnp.int32)
    position = slot_ids % SPAN
    bucket = slot_ids // SPAN
    true_len = true_lengths[bucket]
    reach_max = K // 2
    step_size = jax.random.randint(jax.random.fold_in(key, 1), (NODES, K), 1, reach_max + 1)
    sign_flip = 2 * jax.random.randint(jax.random.fold_in(key, 2), (NODES, K), 0, 2) - 1
    upper_end = (jnp.where(position < true_len, true_len, SPAN) - 1)[:, None]
    near_pos = jnp.clip(position[:, None] + sign_flip * step_size, 0, upper_end)
    far_pos = jax.random.randint(jax.random.fold_in(key, 3), (NODES, K), 0, SPAN)
    column = jnp.arange(K, dtype=jnp.int32)
    chosen = jnp.where(column[None, :] % 2 == 0, near_pos, far_pos)
    return (bucket[:, None] * SPAN + chosen).astype(jnp.int32)


def levels(stream_key, extent, pieces, least, largest):
    gain, own = 1.0, jax.random.fold_in(stream_key, 6)
    for dim, shards_of in pieces:
        steps = jnp.exp(jax.random.uniform(jax.random.fold_in(own, dim), (shards_of,), jnp.float32, least / len(pieces), largest / len(pieces)))
        gain = gain * jnp.repeat(steps, extent[dim] // shards_of).reshape([-1 if axis == dim else 1 for axis in range(len(extent))])
    return gain


def bell_draw(own_key, dims, width, most, shards=(), kind=jnp.bfloat16):
    entries = jax.random.normal(own_key, dims, jnp.float32) * width
    if len(shards) > 0:
        entries = levels(own_key, dims, shards, -0.22, 0.18) * entries
    return jnp.clip(entries, min=-most, max=most).astype(kind)


def setup_inputs(seed: int = 0) -> dict:
    streams_of = jax.random.split(jax.random.key(seed), 23)
    return {
        "nodes": bell_draw(streams_of[0], (NODES, D), 1.0, 6.0, ((0, 32),)),
        "edges": bell_draw(streams_of[1], (NODES, K, E), 1.0, 6.0, ((0, 16), (1, 2))),
        "neighbours": draw_neighbours(jax.random.fold_in(streams_of[22], 71), 0),
        "lengths": draw_lengths(jax.random.fold_in(streams_of[22], 71), 0),
        "message_receiver_weight": bell_draw(streams_of[4], (D, D), (2 * D + E) ** -0.5, 0.15625),
        "message_neighbour_weight": bell_draw(streams_of[5], (D, D), (2 * D + E) ** -0.5, 0.15625),
        "message_edge_weight": bell_draw(streams_of[6], (E, D), (2 * D + E) ** -0.5, 0.15625),
        "message_hidden_bias": bell_draw(streams_of[7], (D,), 0.5, 3.0, (), jnp.float32),
        "message_output_weight": bell_draw(streams_of[8], (D, D), (4 * D // K) ** -0.5, 1.0),
        "gain_one": jnp.clip(1.0 + 0.15 * jax.random.normal(streams_of[9], (D,), jnp.float32), 0.25, 1.75),
        "ffn_in": bell_draw(streams_of[10], (D, FF), D ** -0.5, 0.25),
        "ffn_bias": bell_draw(streams_of[11], (FF,), 0.5, 3.0, (), jnp.float32),
        "ffn_out": bell_draw(streams_of[12], (FF, D), FF ** -0.5, 0.125),
        "gain_two": jnp.clip(1.0 + 0.15 * jax.random.normal(streams_of[13], (D,), jnp.float32), 0.25, 1.75),
        "edge_update_residue_weight": bell_draw(streams_of[14], (D, E), (2 * D + E) ** -0.5, 0.15625),
        "edge_update_neighbour_weight": bell_draw(streams_of[15], (D, E), (2 * D + E) ** -0.5, 0.15625),
        "edge_update_edge_weight": bell_draw(streams_of[16], (E, E), (2 * D + E) ** -0.5, 0.15625),
        "edge_update_bias": bell_draw(streams_of[17], (E,), 0.5, 3.0, (), jnp.float32),
        "edge_out": bell_draw(streams_of[18], (E, E), E ** -0.5, 0.4375),
        "gain_three": jnp.clip(1.0 + 0.15 * jax.random.normal(streams_of[19], (E,), jnp.float32), 0.25, 1.75),
        "node_cot": bell_draw(streams_of[20], (NODES, D), 1.0, 6.0, ((0, 32),)),
        "edge_cot": bell_draw(streams_of[21], (NODES, K, E), 1.0, 6.0, ((0, 16), (1, 2))),
    }


@jax.custom_vjp
def low(v):
    return lax.optimization_barrier(v.astype(jnp.bfloat16)).astype(jnp.float32)

@jax.custom_vjp
def low_back(v):
    return v

def low_keep(v):
    return (low(v), None)

def low_pass(kept, grad):
    return (grad,)

def back_keep(v):
    return (v, None)

def back_low(kept, grad):
    return (low(grad),)
low.defvjp(low_keep, low_pass)
low_back.defvjp(back_keep, back_low)
highest_precision = lax.Precision.HIGHEST
epsilon = 1e-05

def layer_norm(values, gain_vec):
    mean_val = lax.optimization_barrier(jnp.mean(values, -1, keepdims=True))
    centered = values - mean_val
    variance = lax.optimization_barrier(jnp.mean(centered * centered, -1, keepdims=True))
    return centered * lax.rsqrt(variance + epsilon) * gain_vec

def valid_of(slot_ids, lengths):
    return (slot_ids % SPAN < lengths[slot_ids // SPAN]).astype(jnp.float32)

def exact_gelu(values):
    return jax.nn.gelu(values, approximate=False)

def forward(nodes, edges, message_receiver_weight, message_neighbour_weight, message_edge_weight, message_hidden_bias, message_output_weight, gain_one, ffn_in, ffn_bias, ffn_out, gain_two, edge_update_residue_weight, edge_update_neighbour_weight, edge_update_edge_weight, edge_update_bias, edge_out, gain_three, neighbours, lengths):
    block_size = math.gcd(NODES, 256)
    count_blocks = NODES // block_size
    valid_all = valid_of(jnp.arange(NODES, dtype=jnp.int32), lengths)

    def message_block(block_index):
        start_row = (block_index * block_size).astype(jnp.int32)
        residue_rows = lax.dynamic_slice_in_dim(nodes, start_row, block_size, 0)
        residue_edges = lax.dynamic_slice_in_dim(edges, start_row, block_size, 0)
        near_ids = lax.dynamic_slice_in_dim(neighbours, start_row, block_size, 0)
        neighbour_rows = jnp.take(nodes, near_ids, axis=0)
        preactivation_value = jnp.dot(residue_rows, message_receiver_weight, precision=highest_precision)[:, None, :] + jnp.einsum('wjt,tz->wjz', neighbour_rows, message_neighbour_weight, precision=highest_precision) + jnp.einsum('zlu,uo->zlo', residue_edges, message_edge_weight, precision=highest_precision) + message_hidden_bias
        preactivation_value = low_back(preactivation_value)
        nonlinear_output = low(exact_gelu(preactivation_value))
        message_value = low_back(jnp.einsum('wjt,tz->wjz', nonlinear_output, message_output_weight, precision=highest_precision))
        edge_weight = lax.dynamic_slice_in_dim(valid_all, start_row, block_size, 0)[:, None] * valid_all[near_ids]
        weighted = lax.optimization_barrier(jnp.sum(edge_weight[:, :, None] * message_value, axis=1))
        count_row = jnp.maximum(lax.optimization_barrier(jnp.sum(edge_weight, axis=1)), 1.0)
        return weighted / count_row[:, None]
    update = lax.map(jax.checkpoint(message_block), jnp.arange(count_blocks, dtype=jnp.int32)).reshape(NODES, D)
    first_sum = nodes + update
    first_norm = layer_norm(first_sum, gain_one)
    pre_ffn = low_back(jnp.dot(low(first_norm), ffn_in, precision=highest_precision) + ffn_bias)
    hidden = low(exact_gelu(pre_ffn))
    second_sum = first_norm + low_back(jnp.dot(hidden, ffn_out, precision=highest_precision))
    node_state = layer_norm(second_sum, gain_two)
    state_low = low(node_state)

    def edge_block(block_index):
        start_row = (block_index * block_size).astype(jnp.int32)
        residue_rows = lax.dynamic_slice_in_dim(state_low, start_row, block_size, 0)
        residue_edges = lax.dynamic_slice_in_dim(edges, start_row, block_size, 0)
        near_ids = lax.dynamic_slice_in_dim(neighbours, start_row, block_size, 0)
        neighbour_rows = jnp.take(state_low, near_ids, axis=0)
        preactivation_value = jnp.dot(residue_rows, edge_update_residue_weight, precision=highest_precision)[:, None, :] + jnp.einsum('wjt,tz->wjz', neighbour_rows, edge_update_neighbour_weight, precision=highest_precision) + jnp.einsum('zlu,uo->zlo', residue_edges, edge_update_edge_weight, precision=highest_precision) + edge_update_bias
        preactivation_value = low_back(preactivation_value)
        nonlinear_output = low(exact_gelu(preactivation_value))
        branch = low_back(jnp.einsum('zlu,uo->zlo', nonlinear_output, edge_out, precision=highest_precision))
        return layer_norm(residue_edges + branch, gain_three)
    new_edges = lax.map(jax.checkpoint(edge_block), jnp.arange(count_blocks, dtype=jnp.int32)).reshape(NODES, K, E)
    return (node_state, new_edges)

def reference(nodes, edges, neighbours, lengths, message_receiver_weight, message_neighbour_weight, message_edge_weight, message_hidden_bias, message_output_weight, gain_one, ffn_in, ffn_bias, ffn_out, gain_two, edge_update_residue_weight, edge_update_neighbour_weight, edge_update_edge_weight, edge_update_bias, edge_out, gain_three, node_cot, edge_cot):
    floats = [value.astype(jnp.float32) for value in (nodes, edges, message_receiver_weight, message_neighbour_weight, message_edge_weight, message_hidden_bias, message_output_weight, gain_one, ffn_in, ffn_bias, ffn_out, gain_two, edge_update_residue_weight, edge_update_neighbour_weight, edge_update_edge_weight, edge_update_bias, edge_out, gain_three)]

    def wrapped(*values):
        return forward(*values, neighbours, lengths)
    outputs, pullback = jax.vjp(wrapped, *floats)
    gradients = pullback((node_cot.astype(jnp.float32), edge_cot.astype(jnp.float32)))
    return (outputs[0].astype(jnp.bfloat16), outputs[1].astype(jnp.bfloat16), gradients[0], gradients[1], gradients[2], gradients[3], gradients[4], gradients[5], gradients[6], gradients[7], gradients[8], gradients[9], gradients[10], gradients[11], gradients[12], gradients[13], gradients[14], gradients[15], gradients[16], gradients[17])
```

```python
import functools

import jax
import jax.numpy as jnp
from jax import lax
from jax.experimental import pallas as pl
from jax.experimental.pallas import tpu as pltpu
from jax.sharding import PartitionSpec as P

SPAN = 1024
REACH = 64
TILE = 128
WINDOW = TILE + 2 * REACH
VMEM_BYTES = 60 * 2**20

epsilon = 1e-05
root_half = 0.7071067811865476
inv_root_two_pi = 0.3989422804014327
half_log2_e = 0.7213475204444817

bf16 = jnp.bfloat16
f32 = jnp.float32


def swapped(value, level):
    mask = 2**level
    devices = lax.axis_size("res") * lax.axis_size("nbr")
    pairs = [(source, source ^ mask) for source in range(devices)]
    return lax.ppermute(value, ("res", "nbr"), pairs)


def nn(left_op, right_op):
    return jnp.dot(left_op, right_op, preferred_element_type=f32)


def nt(left_op, right_op):
    return lax.dot_general(
        left_op, right_op, (((1,), (1,)), ((), ())), preferred_element_type=f32
    )


def tn(left_op, right_op):
    return lax.dot_general(
        left_op, right_op, (((0,), (0,)), ((), ())), preferred_element_type=f32
    )


def split(values):
    high = values.astype(bf16)
    return high, (values - high.astype(f32)).astype(bf16)


def gelu_and_slope(values):
    below = 0.5 + 0.5 * lax.erf(values * root_half)
    density = jnp.exp2(values * values * -half_log2_e)
    return values * below, below + values * density * inv_root_two_pi


def selector(rows, ids):
    places = lax.broadcasted_iota(jnp.int32, (rows, ids.shape[1]), 0)
    return (places == ids).astype(bf16)


def near_selector(ids, tile, local_first):
    first = local_first + tile * TILE
    return selector(WINDOW, ids[:, tile * TILE : (tile + 1) * TILE] - (first - REACH))


def window_of(tile, local_first):
    return pl.ds(pl.multiple_of(local_first + tile * TILE, TILE), WINDOW)


def repeat_lanes(column, width):
    return jnp.concatenate([column] * (width // column.shape[1]), axis=1)


def padded_rows(table):
    zeros = jnp.zeros((REACH, table.shape[1]), table.dtype)
    return jnp.concatenate([zeros, table, zeros], axis=0)


def whole(shape):
    return pl.BlockSpec(shape, lambda *_: (0,) * len(shape))


def params():
    return pltpu.CompilerParams(vmem_limit_bytes=VMEM_BYTES)


smem = pl.BlockSpec(memory_space=pltpu.SMEM)


def message_forward_kernel(
    static_first,
    meta,
    own,
    other,
    ids,
    edges,
    receiver,
    neighbour,
    edge_weight_t,
    bias,
    out_weight,
    table,
    slope,
    sums,
    packed,
    far_table,
    near_table,
    base,
    counts,
):
    step = pl.program_id(0)
    rows = base.shape[1]
    half = own.shape[0]
    local_first = pl.multiple_of(meta[1], TILE) if static_first is None else static_first

    @pl.when(step == 0)
    def _():
        high = meta[0]
        table[pl.ds(pl.multiple_of(high * half, half), half), :] = own[...]
        table[pl.ds(pl.multiple_of((1 - high) * half, half), half), :] = other[...]
        neighbour_t = neighbour[...].T
        nodes = table[...]
        far_table[...] = nt(neighbour_t, nodes).astype(bf16)
        near_table[...] = nt(neighbour_t, padded_rows(nodes)).astype(bf16)
        block = table[pl.ds(local_first, rows), :]
        base[...] = nt(receiver[...].T, block) + repeat_lanes(bias[...], rows)
        sums[...] = jnp.zeros_like(sums)
        counts[...] = jnp.zeros_like(counts)

    positions = lax.broadcasted_iota(jnp.int32, (1, rows), 1) + local_first
    for side in range(2):
        near = ids[pl.ds(2 * step + side, 1), :] - meta[2]
        valid = ((near < meta[3]) & (positions < meta[3])).astype(f32)
        counts[...] += valid
        if side == 0:
            picked = jnp.concatenate(
                [
                    nn(near_table[:, window_of(tile, local_first)], near_selector(near, tile, local_first))
                    for tile in range(rows // TILE)
                ],
                axis=1,
            )
        else:
            picked = nn(far_table[...], selector(SPAN, near))
        value = picked + nn(edge_weight_t[...], edges[side]) + base[...]
        act, grad = gelu_and_slope(value)
        sums[...] += act * valid
        slope[side] = (grad * valid).astype(bf16)

    @pl.when(step == pl.num_programs(0) - 1)
    def _():
        high_part, low_part = split(sums[...])
        message = tn(high_part, out_weight[...]) + tn(low_part, out_weight[...])
        width = message.shape[1]
        packed[:, :width] = message.astype(bf16)
        packed[:, width:] = jnp.broadcast_to(counts[...], (128, rows)).T.astype(bf16)


def message_forward(meta, own, other, ids, edges, receiver, neighbour, edge_weight, bias, out_weight, local_first):
    pairs = edges.shape[0] // 2
    width, rows = edges.shape[1:]
    model = own.shape[1]
    return pl.pallas_call(
        functools.partial(message_forward_kernel, local_first),
        name="message_forward",
        grid=(pairs,),
        in_specs=[
            smem,
            whole(own.shape),
            whole(other.shape),
            whole(ids.shape),
            pl.BlockSpec((2, width, rows), lambda i: (i, 0, 0)),
            whole(receiver.shape),
            whole(neighbour.shape),
            whole((model, width)),
            whole((model, 128)),
            whole(out_weight.shape),
        ],
        out_specs=[
            whole((SPAN, model)),
            pl.BlockSpec((2, model, rows), lambda i: (i, 0, 0)),
            whole((model, rows)),
            whole((rows, model + 128)),
        ],
        out_shape=[
            jax.ShapeDtypeStruct((SPAN, model), bf16),
            jax.ShapeDtypeStruct((2 * pairs, model, rows), bf16),
            jax.ShapeDtypeStruct((model, rows), f32),
            jax.ShapeDtypeStruct((rows, model + 128), bf16),
        ],
        scratch_shapes=[
            pltpu.VMEM((model, SPAN), bf16),
            pltpu.VMEM((model, SPAN + 2 * REACH), bf16),
            pltpu.VMEM((model, rows), f32),
            pltpu.VMEM((1, rows), f32),
        ],
        compiler_params=params(),
    )(
        meta,
        own,
        other,
        ids,
        edges,
        receiver,
        neighbour,
        edge_weight.T,
        jnp.broadcast_to(bias[:, None], (model, 128)),
        out_weight,
    )


def normed(values):
    mean_val = jnp.mean(values, -1, keepdims=True)
    centered = values - mean_val
    inv_std = lax.rsqrt(jnp.mean(centered * centered, -1, keepdims=True) + epsilon)
    return centered * inv_std, inv_std


def node_forward_kernel(
    nodes, mine, theirs, gain_one, ffn_in, ffn_bias, ffn_out, gain_two, state, ffn_input, act, slope, first, second, stats
):
    width = nodes.shape[1]
    total = mine[...].astype(f32) + theirs[...].astype(f32)
    divisor = jnp.maximum(total[:, width:], 1.0)
    ratio = 1.0 / divisor
    first_sum = nodes[...].astype(f32) + total[:, :width] * repeat_lanes(ratio, width)
    first_unit, first_inv = normed(first_sum)
    first[...] = first_unit
    first_norm = first_unit * gain_one[...]
    low = first_norm.astype(bf16)
    ffn_input[...] = low
    hidden, grad = gelu_and_slope(nn(low, ffn_in[...]) + ffn_bias[...])
    hidden = hidden.astype(bf16)
    act[...] = hidden
    slope[...] = grad.astype(bf16)
    second_unit, second_inv = normed(first_norm + nn(hidden, ffn_out[...]))
    second[...] = second_unit
    state[...] = (second_unit * gain_two[...]).astype(bf16)
    stats[:, :128] = ratio
    stats[:, 128:256] = jnp.broadcast_to(first_inv, ratio.shape)
    stats[:, 256:] = jnp.broadcast_to(second_inv, ratio.shape)


def node_forward(nodes, mine, theirs, gain_one, ffn_in, ffn_bias, ffn_out, gain_two):
    rows, model = nodes.shape
    hidden = ffn_in.shape[1]
    chunk = min(rows, 256)

    def by_rows(width):
        return pl.BlockSpec((chunk, width), lambda i: (i, 0))

    return pl.pallas_call(
        node_forward_kernel,
        name="node_forward",
        grid=(rows // chunk,),
        in_specs=[
            by_rows(model),
            by_rows(model + 128),
            by_rows(model + 128),
            whole((1, model)),
            whole(ffn_in.shape),
            whole((1, hidden)),
            whole(ffn_out.shape),
            whole((1, model)),
        ],
        out_specs=[
            by_rows(model),
            by_rows(model),
            by_rows(hidden),
            by_rows(hidden),
            by_rows(model),
            by_rows(model),
            by_rows(384),
        ],
        out_shape=[
            jax.ShapeDtypeStruct((rows, model), bf16),
            jax.ShapeDtypeStruct((rows, model), bf16),
            jax.ShapeDtypeStruct((rows, hidden), bf16),
            jax.ShapeDtypeStruct((rows, hidden), bf16),
            jax.ShapeDtypeStruct((rows, model), f32),
            jax.ShapeDtypeStruct((rows, model), f32),
            jax.ShapeDtypeStruct((rows, 384), f32),
        ],
        compiler_params=params(),
    )(nodes, mine, theirs, gain_one[None], ffn_in, ffn_bias[None], ffn_out, gain_two[None])


def edge_kernel(
    static_first,
    meta,
    states,
    ids,
    edges,
    cots,
    residue_t,
    neighbour_t,
    edge_weight,
    edge_weight_t,
    bias,
    out_weight,
    out_weight_t,
    gain,
    new_edges,
    partial,
    back_table,
    grads,
    vectors,
    far_table,
    near_table,
    base,
    far_sum,
    near_sum,
    own_sum,
    gain_sum,
    grad_edge,
    grad_out,
):
    step = pl.program_id(0)
    width, rows = base.shape
    local_first = pl.multiple_of(meta[1], TILE) if static_first is None else static_first

    @pl.when(step == 0)
    def _():
        nodes = states[...]
        far_table[...] = nt(neighbour_t[...], nodes).astype(bf16)
        near_table[...] = nt(neighbour_t[...], padded_rows(nodes)).astype(bf16)
        block = states[pl.ds(local_first, rows), :]
        base[...] = nt(residue_t[...], block) + repeat_lanes(bias[...], rows)
        for total in (far_sum, near_sum, own_sum, gain_sum, grad_edge, grad_out):
            total[...] = jnp.zeros_like(total)

    gains = repeat_lanes(gain[...], rows)
    for side in range(2):
        near = ids[pl.ds(2 * step + side, 1), :] - meta[2]
        if side == 0:
            chosen = [near_selector(near, tile, local_first) for tile in range(rows // TILE)]
            picked = jnp.concatenate(
                [
                    nn(near_table[:, window_of(tile, local_first)], pick)
                    for tile, pick in enumerate(chosen)
                ],
                axis=1,
            )
        else:
            chosen = selector(SPAN, near)
            picked = nn(far_table[...], chosen)
        edge = edges[side]
        value = picked + nn(edge_weight_t[...], edge) + base[...]
        act, slope = gelu_and_slope(value)
        act = act.astype(bf16)
        third = edge.astype(f32) + nn(out_weight_t[...], act)
        centered = third - jnp.mean(third, 0, keepdims=True)
        inv_std = lax.rsqrt(jnp.mean(centered * centered, 0, keepdims=True) + epsilon)
        unit = centered * inv_std
        new_edges[side] = (unit * gains).astype(bf16)
        cot = cots[side].astype(f32)
        gain_sum[...] += cot * unit
        scaled = cot * gains
        grad_third = inv_std * (
            scaled
            - jnp.mean(scaled, 0, keepdims=True)
            - unit * jnp.mean(scaled * unit, 0, keepdims=True)
        )
        branch = grad_third.astype(bf16)
        grad_out[...] += nt(act, branch)
        grad_value = (nn(out_weight[...], branch) * slope).astype(bf16)
        own_sum[...] += grad_value.astype(f32)
        grad_edge[...] += nt(edge, grad_value)
        partial[side] = grad_third + nn(edge_weight[...], grad_value)
        if side == 0:
            for tile, pick in enumerate(chosen):
                near_sum[:, window_of(tile, local_first)] += nt(
                    grad_value[:, tile * TILE : (tile + 1) * TILE], pick
                )
        else:
            far_sum[...] += nt(grad_value, chosen)

    @pl.when(step == pl.num_programs(0) - 1)
    def _():
        shifted = pltpu.roll(near_sum[...], SPAN + REACH, 1)
        table_sum = far_sum[...] + shifted[:, :SPAN]
        table_high, table_low = split(table_sum)
        own_high, own_low = split(own_sum[...])
        back = tn(table_high, neighbour_t[...]) + tn(table_low, neighbour_t[...])
        own_back = tn(own_high, residue_t[...]) + tn(own_low, residue_t[...])
        if rows == SPAN:
            back_table[...] = (back + own_back).astype(bf16)
        else:
            near_sum_rows = pl.ds(pl.multiple_of(local_first, TILE), rows)
            back_table[...] = back.astype(bf16)
            back_table[near_sum_rows, :] = (
                back_table[near_sum_rows, :].astype(f32) + own_back
            ).astype(bf16)
        block = states[pl.ds(local_first, rows), :]
        grads[:width, :] = nn(own_high, block) + nn(own_low, block)
        grads[width : 2 * width, :] = nn(table_high, states[...]) + nn(table_low, states[...])
        grads[2 * width :, :width] = grad_edge[...]
        grads[2 * width :, 256 : 256 + width] = grad_out[...]
        vectors[:, :1] = jnp.sum(own_sum[...], axis=1, keepdims=True)
        vectors[:, 1:2] = jnp.sum(gain_sum[...], axis=1, keepdims=True)


def edge_layer(
    meta, states, ids, edges, cots, residue, neighbour, edge_weight, bias, out_weight, gain, local_first
):
    pairs = edges.shape[0] // 2
    width, rows = edges.shape[1:]
    model = states.shape[1]
    by_pair = pl.BlockSpec((2, width, rows), lambda i: (i, 0, 0))
    square = whole((width, width))
    return pl.pallas_call(
        functools.partial(edge_kernel, local_first),
        name="edge_layer",
        grid=(pairs,),
        in_specs=[
            smem,
            whole(states.shape),
            whole(ids.shape),
            by_pair,
            by_pair,
            whole((width, model)),
            whole((width, model)),
            square,
            square,
            whole((width, 128)),
            square,
            square,
            whole((width, 128)),
        ],
        out_specs=[
            by_pair,
            by_pair,
            whole((SPAN, model)),
            whole((3 * width, model)),
            whole((width, 128)),
        ],
        out_shape=[
            jax.ShapeDtypeStruct(edges.shape, bf16),
            jax.ShapeDtypeStruct(edges.shape, f32),
            jax.ShapeDtypeStruct((SPAN, model), bf16),
            jax.ShapeDtypeStruct((3 * width, model), f32),
            jax.ShapeDtypeStruct((width, 128), f32),
        ],
        scratch_shapes=[
            pltpu.VMEM((width, SPAN), bf16),
            pltpu.VMEM((width, SPAN + 2 * REACH), bf16),
            pltpu.VMEM((width, rows), f32),
            pltpu.VMEM((width, SPAN), f32),
            pltpu.VMEM((width, SPAN + 2 * REACH), f32),
            pltpu.VMEM((width, rows), f32),
            pltpu.VMEM((width, rows), f32),
            pltpu.VMEM((width, width), f32),
            pltpu.VMEM((width, width), f32),
        ],
        compiler_params=params(),
    )(
        meta,
        states,
        ids,
        edges,
        cots,
        residue.T,
        neighbour.T,
        edge_weight,
        edge_weight.T,
        jnp.broadcast_to(bias[:, None], (width, 128)),
        out_weight,
        out_weight.T,
        jnp.broadcast_to(gain[:, None], (width, 128)),
    )


def norm_back(unit, inv_std, gain, grad_out):
    grad_gain = jnp.sum(grad_out * unit, axis=0, keepdims=True)
    scaled = grad_out * gain
    grad_in = inv_std * (
        scaled
        - jnp.mean(scaled, -1, keepdims=True)
        - unit * jnp.mean(scaled * unit, -1, keepdims=True)
    )
    return grad_in, grad_gain


def node_backward_kernel(
    meta,
    own_cot,
    other_cot,
    mine,
    theirs,
    first,
    second,
    stats,
    ffn_input,
    act,
    slope,
    gain_one,
    ffn_in,
    ffn_out,
    gain_two,
    grad_first_ref,
    message_cot,
    weights,
    vectors,
    sum_out,
    sum_in,
):
    step = pl.program_id(0)
    chunk, model = first.shape
    hidden = act.shape[1]
    core = meta[4]
    half = own_cot.shape[0]

    @pl.when(step == 0)
    def _():
        vectors[...] = jnp.zeros_like(vectors)
        sum_out[...] = jnp.zeros_like(sum_out)
        sum_in[...] = jnp.zeros_like(sum_in)

    row = step * chunk
    inside = pl.ds(pl.multiple_of(lax.rem(row, half), chunk), chunk)
    cot = jnp.where(row // half == core, own_cot[inside, :], other_cot[inside, :])
    total = cot.astype(f32) + (mine[...].astype(f32) + theirs[...].astype(f32))
    second_inv = stats[:, 256:257]
    first_inv = stats[:, 128:129]
    grad_second, gain_two_part = norm_back(second[...], second_inv, gain_two[...], total)
    top = grad_second.astype(bf16)
    grad_hidden = (nt(top, ffn_out[...]) * slope[...].astype(f32)).astype(bf16)
    out_columns = pl.ds(pl.multiple_of(core * (hidden // 2), 128), hidden // 2)
    in_columns = pl.ds(pl.multiple_of(core * (model // 2), 128), model // 2)
    sum_out[...] += tn(act[:, out_columns], top)
    sum_in[...] += tn(ffn_input[:, in_columns], grad_hidden)
    bias_part = jnp.sum(grad_hidden.astype(f32), axis=0, keepdims=True)
    grad_norm = grad_second + nt(grad_hidden, ffn_in[...])
    grad_first, gain_one_part = norm_back(first[...], first_inv, gain_one[...], grad_norm)
    grad_first_ref[...] = grad_first
    message_cot[...] = (grad_first * stats[:, :1]).astype(bf16)
    vectors[0:1, :] += gain_one_part
    vectors[1:2, :] += gain_two_part
    for part in range(hidden // model):
        vectors[2 + part : 3 + part, :] += bias_part[:, part * model : (part + 1) * model]

    @pl.when(step == pl.num_programs(0) - 1)
    def _():
        weights[: hidden // 2, :] = sum_out[...].astype(bf16)
        for part in range(hidden // model):
            start = hidden // 2 + part * (model // 2)
            weights[start : start + model // 2, :] = sum_in[
                :, part * model : (part + 1) * model
            ].astype(bf16)


def node_backward(
    meta, own_cot, other_cot, mine, theirs, first, second, stats, ffn_input, act, slope, gain_one, ffn_in, ffn_out, gain_two
):
    rows, model = first.shape
    hidden = act.shape[1]
    chunk = min(own_cot.shape[0], 256)

    def by_rows(width):
        return pl.BlockSpec((chunk, width), lambda i: (i, 0))

    return pl.pallas_call(
        node_backward_kernel,
        name="node_backward",
        grid=(rows // chunk,),
        in_specs=[
            smem,
            whole(own_cot.shape),
            whole(other_cot.shape),
            by_rows(model),
            by_rows(model),
            by_rows(model),
            by_rows(model),
            by_rows(384),
            by_rows(model),
            by_rows(hidden),
            by_rows(hidden),
            whole((1, model)),
            whole(ffn_in.shape),
            whole(ffn_out.shape),
            whole((1, model)),
        ],
        out_specs=[by_rows(model), by_rows(model), whole((hidden, model)), whole((8, model))],
        out_shape=[
            jax.ShapeDtypeStruct((rows, model), f32),
            jax.ShapeDtypeStruct((rows, model), bf16),
            jax.ShapeDtypeStruct((hidden, model), bf16),
            jax.ShapeDtypeStruct((8, model), f32),
        ],
        scratch_shapes=[
            pltpu.VMEM((hidden // 2, model), f32),
            pltpu.VMEM((model // 2, hidden), f32),
        ],
        compiler_params=params(),
    )(
        meta,
        own_cot,
        other_cot,
        mine,
        theirs,
        first,
        second,
        stats,
        ffn_input,
        act,
        slope,
        gain_one[None],
        ffn_in,
        ffn_out,
        gain_two[None],
    )


def message_backward_kernel(
    static_first,
    meta,
    table,
    cot,
    sums,
    ids,
    edges,
    slope,
    receiver,
    neighbour,
    out_weight,
    keep,
    send,
    grad_self,
    grad_near,
    grad_edge,
    grad_out,
    grad_bias,
    spread,
    far_sum,
    near_sum,
    own_sum,
):
    step = pl.program_id(0)
    rows = spread.shape[1]
    half = keep.shape[0]
    local_first = pl.multiple_of(meta[1], TILE) if static_first is None else static_first

    @pl.when(step == 0)
    def _():
        spread[...] = nt(out_weight[...], cot[...])
        grad_out[...] = nn(sums[...].astype(bf16), cot[...])
        grad_edge[...] = jnp.zeros_like(grad_edge)
        for total in (far_sum, near_sum, own_sum):
            total[...] = jnp.zeros_like(total)

    for side in range(2):
        near = ids[pl.ds(2 * step + side, 1), :] - meta[2]
        grad_value = (spread[...] * slope[side].astype(f32)).astype(bf16)
        own_sum[...] += grad_value.astype(f32)
        grad_edge[...] += nt(edges[side], grad_value)
        if side == 0:
            for tile in range(rows // TILE):
                near_sum[:, window_of(tile, local_first)] += nt(
                    grad_value[:, tile * TILE : (tile + 1) * TILE],
                    near_selector(near, tile, local_first),
                )
        else:
            far_sum[...] += nt(grad_value, selector(SPAN, near))

    @pl.when(step == pl.num_programs(0) - 1)
    def _():
        shifted = pltpu.roll(near_sum[...], SPAN + REACH, 1)
        table_high, table_low = split(far_sum[...] + shifted[:, :SPAN])
        own_high, own_low = split(own_sum[...])
        nodes = table[...]
        block = table[pl.ds(local_first, rows), :]
        grad_near[...] = (nn(table_high, nodes) + nn(table_low, nodes)).T
        grad_self[...] = (nn(own_high, block) + nn(own_low, block)).T
        grad_bias[...] = jnp.sum(own_sum[...].T, axis=0, keepdims=True)
        back = nn(neighbour[...], table_high) + nn(neighbour[...], table_low)
        own_back = nn(receiver[...], own_high) + nn(receiver[...], own_low)
        if rows == SPAN:
            far_sum[...] = back + own_back
        else:
            far_sum[...] = back
            far_sum[:, pl.ds(pl.multiple_of(local_first, TILE), rows)] += own_back
        high = meta[0]
        keep[...] = far_sum[:, pl.ds(pl.multiple_of(high * half, half), half)].T
        send[...] = far_sum[:, pl.ds(pl.multiple_of((1 - high) * half, half), half)].T.astype(bf16)


def message_backward(meta, table, cot, sums, ids, edges, slope, receiver, neighbour, out_weight, local_first):
    pairs = edges.shape[0] // 2
    width, rows = edges.shape[1:]
    model = table.shape[1]
    square = whole((model, model))
    return pl.pallas_call(
        functools.partial(message_backward_kernel, local_first),
        name="message_backward",
        grid=(pairs,),
        in_specs=[
            smem,
            whole(table.shape),
            whole(cot.shape),
            whole(sums.shape),
            whole(ids.shape),
            pl.BlockSpec((2, width, rows), lambda i: (i, 0, 0)),
            pl.BlockSpec((2, model, rows), lambda i: (i, 0, 0)),
            square,
            square,
            square,
        ],
        out_specs=[
            whole((SPAN // 2, model)),
            whole((SPAN // 2, model)),
            square,
            square,
            whole((width, model)),
            square,
            whole((1, model)),
            whole((model, rows)),
        ],
        out_shape=[
            jax.ShapeDtypeStruct((SPAN // 2, model), f32),
            jax.ShapeDtypeStruct((SPAN // 2, model), bf16),
            jax.ShapeDtypeStruct((model, model), f32),
            jax.ShapeDtypeStruct((model, model), f32),
            jax.ShapeDtypeStruct((width, model), f32),
            jax.ShapeDtypeStruct((model, model), f32),
            jax.ShapeDtypeStruct((1, model), f32),
            jax.ShapeDtypeStruct((model, rows), f32),
        ],
        scratch_shapes=[
            pltpu.VMEM((model, SPAN), f32),
            pltpu.VMEM((model, SPAN + 2 * REACH), f32),
            pltpu.VMEM((model, rows), f32),
        ],
        compiler_params=params(),
    )(meta, table, cot, sums, ids, edges, slope, receiver, neighbour, out_weight)


def edge_gradient_kernel(partial, slope, spread, edge_weight, out):
    for side in range(partial.shape[0]):
        grad_value = (spread[...] * slope[side].astype(f32)).astype(bf16)
        out[side] = partial[side] + nn(edge_weight[...], grad_value)


def edge_gradient(partial, slope, spread, edge_weight):
    columns, width, rows = partial.shape
    model = spread.shape[0]
    by_pair = pl.BlockSpec((2, width, rows), lambda i: (i, 0, 0))
    return pl.pallas_call(
        edge_gradient_kernel,
        name="edge_gradient",
        grid=(columns // 2,),
        in_specs=[
            by_pair,
            pl.BlockSpec((2, model, rows), lambda i: (i, 0, 0)),
            whole(spread.shape),
            whole(edge_weight.shape),
        ],
        out_specs=by_pair,
        out_shape=jax.ShapeDtypeStruct(partial.shape, f32),
        compiler_params=params(),
    )(partial, slope, spread, edge_weight)


def joined(table, other, high_side):
    return jnp.where(
        high_side, jnp.concatenate([other, table], axis=0), jnp.concatenate([table, other], axis=0)
    )


def halves(table, high_side):
    half = table.shape[0] // 2
    lower, upper = (table[:half], table[half:])
    return (jnp.where(high_side, upper, lower), jnp.where(high_side, lower, upper))


def sum_blocks(table, device, level):
    keep, send = halves(table, device >> level & 1 == 1)
    return keep + swapped(send.astype(bf16), level).astype(keep.dtype)


def on_device(
    nodes,
    edges,
    neighbours,
    lengths,
    message_receiver_weight,
    message_neighbour_weight,
    message_edge_weight,
    message_hidden_bias,
    message_output_weight,
    gain_one,
    ffn_in,
    ffn_bias,
    ffn_out,
    gain_two,
    edge_update_residue_weight,
    edge_update_neighbour_weight,
    edge_update_edge_weight,
    edge_update_bias,
    edge_out,
    gain_three,
    node_cot,
    edge_cot,
):
    rows, half_k, edge_width = edges.shape
    own_rows, model = nodes.shape
    hidden = ffn_in.shape[1]
    levels = (SPAN // own_rows).bit_length() - 1
    core = lax.axis_index("nbr")
    device = lax.axis_index("res") * lax.axis_size("nbr") + core
    first_row = lax.axis_index("res") * rows
    bucket = first_row // SPAN
    group_start = bucket * SPAN
    local_first = 0 if rows == SPAN else None
    length = jnp.sum(jnp.where(jnp.arange(lengths.shape[0]) == bucket, lengths, 0))
    top = device >> (levels - 1) & 1
    meta = jnp.stack(
        [top, first_row - group_start, group_start, length, core, 0, 0, 0]
    ).astype(jnp.int32)

    ids = neighbours.T
    edges_t = edges.transpose(1, 2, 0)
    cot_t = edge_cot.transpose(1, 2, 0)

    table = nodes
    for level in range(levels - 1):
        table = joined(table, swapped(table, level), device >> level & 1 == 1)
    other_table = swapped(table, levels - 1)
    other_cot = swapped(node_cot, 0)

    node_table, slope, sums, packed = message_forward(
        meta,
        table,
        other_table,
        ids,
        edges_t,
        message_receiver_weight,
        message_neighbour_weight,
        message_edge_weight,
        message_hidden_bias,
        message_output_weight,
        local_first,
    )
    block = node_table
    if rows < SPAN:
        block = lax.dynamic_slice_in_dim(node_table, first_row - group_start, rows, 0)
    state, ffn_input, act, ffn_slope, first, second, stats = node_forward(
        block, packed, swapped(packed, 0), gain_one, ffn_in, ffn_bias, ffn_out, gain_two
    )
    states = state
    for level in range(1, levels):
        states = joined(states, swapped(states, level), device >> level & 1 == 1)
    new_edges, partial, back, edge_grads, edge_vectors = edge_layer(
        meta,
        states,
        ids,
        edges_t,
        cot_t,
        edge_update_residue_weight,
        edge_update_neighbour_weight,
        edge_update_edge_weight,
        edge_update_bias,
        edge_out,
        gain_three,
        local_first,
    )
    for level in reversed(range(1, levels)):
        back = sum_blocks(back, device, level)
    grad_first, message_cot, ffn_grads, node_vectors = node_backward(
        meta,
        node_cot,
        other_cot,
        back,
        swapped(back, 0),
        first,
        second,
        stats,
        ffn_input,
        act,
        ffn_slope,
        gain_one,
        ffn_in,
        ffn_out,
        gain_two,
    )
    (
        keep,
        send,
        grad_msg_self,
        grad_msg_nbr,
        grad_msg_edge,
        grad_msg_out,
        grad_msg_bias,
        spread,
    ) = message_backward(
        meta,
        node_table,
        message_cot,
        sums,
        ids,
        edges_t,
        slope,
        message_receiver_weight,
        message_neighbour_weight,
        message_output_weight,
        local_first,
    )
    edge_grad = edge_gradient(partial, slope, spread, message_edge_weight)
    kept = keep + swapped(send, levels - 1).astype(f32)
    for level in reversed(range(levels - 1)):
        kept = sum_blocks(kept, device, level)
    own_first = lax.dynamic_slice_in_dim(grad_first, core * own_rows, own_rows, 0)
    node_grad = own_first + kept
    node_out = lax.dynamic_slice_in_dim(state, core * own_rows, own_rows, 0)

    halved = node_vectors * 0.5
    small = lax.psum(
        (
            grad_msg_self,
            grad_msg_nbr,
            grad_msg_edge,
            grad_msg_bias,
            grad_msg_out,
            edge_grads,
            edge_vectors[:, :2],
            halved,
        ),
        ("res", "nbr"),
    )
    grad_msg_self, grad_msg_nbr, grad_msg_edge, grad_msg_bias, grad_msg_out, edge_grads, edge_vectors, vectors = small
    ffn_grads = lax.psum(ffn_grads.astype(f32), "res")
    both = lax.all_gather(ffn_grads, "nbr", axis=0)
    grad_ffn_out = jnp.concatenate([both[0, : hidden // 2], both[1, : hidden // 2]], axis=0)
    parts = [
        both[:, hidden // 2 + part * (model // 2) : hidden // 2 + (part + 1) * (model // 2)].reshape(model, model)
        for part in range(hidden // model)
    ]
    grad_ffn_in = jnp.concatenate(parts, axis=1)
    return (
        node_out,
        new_edges.transpose(2, 0, 1),
        node_grad,
        edge_grad.transpose(2, 0, 1),
        grad_msg_self,
        grad_msg_nbr,
        grad_msg_edge,
        grad_msg_bias[0],
        grad_msg_out,
        vectors[0],
        grad_ffn_in,
        vectors[2 : 2 + hidden // model].reshape(-1),
        grad_ffn_out,
        vectors[1],
        edge_grads[:edge_width].T,
        edge_grads[edge_width : 2 * edge_width].T,
        edge_grads[2 * edge_width :, :edge_width],
        edge_vectors[:, 0],
        edge_grads[2 * edge_width :, 256 : 256 + edge_width],
        edge_vectors[:, 1],
    )


def solution(mesh):
    rows = P(("res", "nbr"), None)
    pairs = P("res", "nbr", None)
    placed = (rows, pairs, P("res", "nbr")) + (P(),) * 17 + (rows, pairs)
    return jax.shard_map(
        on_device,
        mesh=mesh,
        in_specs=placed,
        out_specs=(rows, pairs, rows, pairs) + (P(),) * 16,
        check_vma=False,
    )
```

```python
import functools

import jax
import jax.numpy as jnp
from jax import lax
from jax.experimental import pallas as pl
from jax.experimental.pallas import tpu as pltpu
from jax.sharding import PartitionSpec as P

SPAN = 1024
REACH = 32
MASKED = -16384.0
VMEM_BYTES = 60 * 2**20

epsilon = 1e-05
root_half = 0.7071067811865476
inv_root_two_pi = 0.3989422804014327
half_log2_e = 0.7213475204444817

bf16 = jnp.bfloat16
f32 = jnp.float32


def swapped(value, level):
    mask = 2**level
    devices = lax.axis_size("res") * lax.axis_size("nbr")
    pairs = [(source, source ^ mask) for source in range(devices)]
    return lax.ppermute(value, ("res", "nbr"), pairs)


def nn(left_op, right_op):
    return jnp.dot(left_op, right_op, preferred_element_type=f32)


def nt(left_op, right_op):
    return lax.dot_general(
        left_op, right_op, (((1,), (1,)), ((), ())), preferred_element_type=f32
    )


def tn(left_op, right_op):
    return lax.dot_general(
        left_op, right_op, (((0,), (0,)), ((), ())), preferred_element_type=f32
    )


def split(values):
    high = values.astype(bf16)
    return high, (values - high.astype(f32)).astype(bf16)


def twice_gelu_and_slope(values):
    below = 1.0 + lax.erf(values * root_half)
    density = jnp.exp2(values * values * -half_log2_e)
    return values * below, below + values * density * (2.0 * inv_root_two_pi)


def selector(rows, ids):
    places = lax.broadcasted_iota(jnp.int32, (rows, ids.shape[1]), 0)
    return (places == ids).astype(bf16)


def tile_of(rows):
    return min(rows, 256)


def window_of(rows):
    return tile_of(rows) + 2 * REACH


def far_rows(ids, edge):
    return jnp.concatenate([selector(SPAN, ids), edge], axis=0)


def near_rows(ids, edge, first):
    return jnp.concatenate([selector(ids.shape[1] + 2 * REACH, ids - (first - REACH)), edge], axis=0)


def tiles(rows):
    width = tile_of(rows)
    return [(tile, slice(tile * width, (tile + 1) * width)) for tile in range(rows // width)]


def window_rows(local_first, rows, tile):
    start = local_first + tile * tile_of(rows)
    if not isinstance(start, int):
        start = pl.multiple_of(start, 128)
    return pl.ds(start, window_of(rows))


def repeat_lanes(column, width):
    return jnp.concatenate([column] * (width // column.shape[1]), axis=1)


def whole(shape):
    return pl.BlockSpec(shape, lambda *_: (0,) * len(shape))


def params():
    return pltpu.CompilerParams(vmem_limit_bytes=VMEM_BYTES)


smem = pl.BlockSpec(memory_space=pltpu.SMEM)


def message_forward_kernel(
    static_first,
    meta,
    own,
    other,
    ids,
    edges,
    receiver,
    neighbour,
    edge_weight,
    bias,
    table,
    slope,
    packed,
    padded,
    far_table,
    near_table,
    base,
    sums,
    counts,
):
    step = pl.program_id(0)
    rows = base.shape[1]
    half = own.shape[0]
    local_first = pl.multiple_of(meta[1], 128) if static_first is None else static_first

    @pl.when(step == 0)
    def _():
        high = meta[0]
        table[pl.ds(pl.multiple_of(high * half, half), half), :] = own[...]
        table[pl.ds(pl.multiple_of((1 - high) * half, half), half), :] = other[...]
        places = lax.broadcasted_iota(jnp.int32, (SPAN, 1), 0)
        hidden = jnp.where(places < meta[3], 0.0, MASKED)
        projected = (nn(table[...], neighbour[...]) + hidden).astype(bf16)
        far_table[...] = jnp.concatenate([projected, edge_weight[...]], axis=0).T
        padded[...] = jnp.zeros_like(padded)
        padded[REACH : REACH + SPAN, :] = projected
        for tile, _ in tiles(rows):
            window = padded[window_rows(local_first, rows, tile), :]
            near_table[tile] = jnp.concatenate([window, edge_weight[...]], axis=0).T
        block = table[pl.ds(local_first, rows), :]
        places = lax.broadcasted_iota(jnp.int32, (rows, 1), 0) + local_first
        hidden = jnp.where(places < meta[3], 0.0, MASKED)
        base[...] = (nn(block, receiver[...]) + (bias[...] + hidden)).T
        sums[...] = jnp.zeros_like(sums)
        counts[...] = jnp.zeros_like(counts)

    positions = lax.broadcasted_iota(jnp.int32, (1, rows), 1) + local_first
    near, far = (ids[pl.ds(2 * step + side, 1), :] - meta[2] for side in range(2))
    counts[...] += jnp.where(positions < meta[3], 1.0, 0.0) * (
        jnp.where(near < meta[3], 1.0, 0.0) + jnp.where(far < meta[3], 1.0, 0.0)
    )
    for tile, lanes in tiles(rows):
        near_part = near_rows(near[:, lanes], edges[0, :, lanes], local_first + lanes.start)
        far_part = far_rows(far[:, lanes], edges[1, :, lanes])
        far_value = nn(far_table[...], far_part)
        near_value = nn(near_table[tile], near_part)
        far_act, far_slope = twice_gelu_and_slope(far_value + base[:, lanes])
        slope[1, :, lanes] = far_slope.astype(bf16)
        near_act, near_slope = twice_gelu_and_slope(near_value + base[:, lanes])
        slope[0, :, lanes] = near_slope.astype(bf16)
        sums[:, lanes] += far_act + near_act

    @pl.when(step == pl.num_programs(0) - 1)
    def _():
        width = sums.shape[0]
        packed[:width, :] = (0.5 * sums[...]).astype(bf16)
        packed[width:, :] = jnp.broadcast_to(counts[...], (16, rows)).astype(bf16)


def message_forward(meta, own, other, ids, edges, receiver, neighbour, edge_weight, bias, local_first):
    pairs = edges.shape[0] // 2
    width, rows = edges.shape[1:]
    model = own.shape[1]
    return pl.pallas_call(
        functools.partial(message_forward_kernel, local_first),
        name="message_forward",
        grid=(pairs,),
        in_specs=[
            smem,
            whole(own.shape),
            whole(other.shape),
            whole(ids.shape),
            pl.BlockSpec((2, width, rows), lambda i: (i, 0, 0)),
            whole(receiver.shape),
            whole(neighbour.shape),
            whole(edge_weight.shape),
            whole((1, model)),
        ],
        out_specs=[
            whole((SPAN, model)),
            pl.BlockSpec((2, model, rows), lambda i: (i, 0, 0)),
            whole((model + 16, rows)),
        ],
        out_shape=[
            jax.ShapeDtypeStruct((SPAN, model), bf16),
            jax.ShapeDtypeStruct((2 * pairs, model, rows), bf16),
            jax.ShapeDtypeStruct((model + 16, rows), bf16),
        ],
        scratch_shapes=[
            pltpu.VMEM((SPAN + 2 * REACH, model), bf16),
            pltpu.VMEM((model, SPAN + width), bf16),
            pltpu.VMEM((rows // tile_of(rows), model, window_of(rows) + width), bf16),
            pltpu.VMEM((model, rows), f32),
            pltpu.VMEM((model, rows), f32),
            pltpu.VMEM((1, rows), f32),
        ],
        compiler_params=params(),
    )(meta, own, other, ids, edges, receiver, neighbour, edge_weight, bias[None])


def normed(values):
    mean_val = jnp.mean(values, -1, keepdims=True)
    centered = values - mean_val
    inv_std = lax.rsqrt(jnp.mean(centered * centered, -1, keepdims=True) + epsilon)
    return centered * inv_std, inv_std


def node_forward_kernel(
    nodes,
    mine,
    theirs,
    out_weight,
    gain_one,
    ffn_in,
    ffn_bias,
    ffn_out,
    gain_two,
    state,
    ffn_input,
    act,
    slope,
    first,
    second,
    stats,
    sums,
):
    rows, width = nodes.shape
    total = mine[...].astype(f32) + theirs[...].astype(f32)
    count = jnp.maximum(total[width : width + 1, :], 1.0)
    ratio = 1.0 / jnp.broadcast_to(count, (128, rows)).T
    high, low = split(total[:width, :])
    sums[...] = high
    message = tn(high, out_weight[...]) + tn(low, out_weight[...])
    first_sum = nodes[...].astype(f32) + message * repeat_lanes(ratio, width)
    first_unit, first_inv = normed(first_sum)
    first[...] = first_unit
    first_norm = first_unit * gain_one[...]
    low = first_norm.astype(bf16)
    ffn_input[...] = low
    hidden, grad = twice_gelu_and_slope(nn(low, ffn_in[...]) + ffn_bias[...])
    hidden = (0.5 * hidden).astype(bf16)
    act[...] = hidden
    slope[...] = (0.5 * grad).astype(bf16)
    second_unit, second_inv = normed(first_norm + nn(hidden, ffn_out[...]))
    second[...] = second_unit
    state[...] = (second_unit * gain_two[...]).astype(bf16)
    stats[:, :128] = ratio
    stats[:, 128:256] = jnp.broadcast_to(first_inv, ratio.shape)
    stats[:, 256:] = jnp.broadcast_to(second_inv, ratio.shape)


def node_forward(nodes, mine, theirs, out_weight, gain_one, ffn_in, ffn_bias, ffn_out, gain_two):
    rows, model = nodes.shape
    hidden = ffn_in.shape[1]
    chunk = min(rows, 256)

    def by_rows(width):
        return pl.BlockSpec((chunk, width), lambda i: (i, 0))

    return pl.pallas_call(
        node_forward_kernel,
        name="node_forward",
        grid=(rows // chunk,),
        in_specs=[
            by_rows(model),
            pl.BlockSpec((model + 16, chunk), lambda i: (0, i)),
            pl.BlockSpec((model + 16, chunk), lambda i: (0, i)),
            whole(out_weight.shape),
            whole((1, model)),
            whole(ffn_in.shape),
            whole((1, hidden)),
            whole(ffn_out.shape),
            whole((1, model)),
        ],
        out_specs=[
            by_rows(model),
            by_rows(model),
            by_rows(hidden),
            by_rows(hidden),
            by_rows(model),
            by_rows(model),
            by_rows(384),
            pl.BlockSpec((model, chunk), lambda i: (0, i)),
        ],
        out_shape=[
            jax.ShapeDtypeStruct((rows, model), bf16),
            jax.ShapeDtypeStruct((rows, model), bf16),
            jax.ShapeDtypeStruct((rows, hidden), bf16),
            jax.ShapeDtypeStruct((rows, hidden), bf16),
            jax.ShapeDtypeStruct((rows, model), f32),
            jax.ShapeDtypeStruct((rows, model), f32),
            jax.ShapeDtypeStruct((rows, 384), f32),
            jax.ShapeDtypeStruct((model, rows), bf16),
        ],
        compiler_params=params(),
    )(
        nodes, mine, theirs, out_weight, gain_one[None], ffn_in, ffn_bias[None], ffn_out, gain_two[None]
    )


def edge_kernel(
    static_first,
    meta,
    states,
    ids,
    edges,
    cots,
    residue_t,
    neighbour_t,
    edge_weight,
    bias,
    out_weight,
    out_weight_t,
    gain,
    new_edges,
    partial,
    back_table,
    grads,
    vectors,
    padded,
    far_table,
    near_table,
    base,
    gains,
    far_sum,
    near_sum,
    own_sum,
    gain_sum,
    grad_edge,
    grad_out,
):
    step = pl.program_id(0)
    width, rows = base.shape
    window = window_of(rows)
    local_first = pl.multiple_of(meta[1], 128) if static_first is None else static_first

    @pl.when(step == 0)
    def _():
        fill = jnp.zeros((width, 256 - width), bf16)
        weight = jnp.concatenate([edge_weight[...], fill], axis=1)
        projected = nt(states[...], neighbour_t[...]).astype(bf16)
        projected = jnp.concatenate([projected, jnp.zeros((SPAN, 256 - width), bf16)], axis=1)
        far_table[...] = jnp.concatenate([projected, weight], axis=0).T[:width, :]
        padded[...] = jnp.zeros_like(padded)
        padded[REACH : REACH + SPAN, :] = projected
        for tile, _ in tiles(rows):
            part = padded[window_rows(local_first, rows, tile), :]
            near_table[tile] = jnp.concatenate([part, weight], axis=0).T[:width, :]
        block = states[pl.ds(local_first, rows), :]
        base[...] = nt(residue_t[...], block) + repeat_lanes(bias[...], rows)
        gains[...] = repeat_lanes(gain[...], rows)
        for total in (far_sum, near_sum, own_sum, gain_sum, grad_edge, grad_out):
            total[...] = jnp.zeros_like(total)

    for side in range(2):
        near = ids[pl.ds(2 * step + side, 1), :] - meta[2]
        edge = edges[side]
        if side == 0:
            chosen = [
                near_rows(near[:, lanes], edges[0, :, lanes], local_first + lanes.start)
                for _, lanes in tiles(rows)
            ]
            value = jnp.concatenate(
                [nn(near_table[tile], part) for tile, part in enumerate(chosen)], axis=1
            )
        else:
            chosen = far_rows(near, edge)
            value = nn(far_table[...], chosen)
        act, slope = twice_gelu_and_slope(value + base[...])
        act = act.astype(bf16)
        third = edge.astype(f32) + nn(out_weight_t[...], act)
        centered = third - jnp.mean(third, 0, keepdims=True)
        inv_std = lax.rsqrt(jnp.mean(centered * centered, 0, keepdims=True) + epsilon)
        unit = centered * inv_std
        new_edges[side] = (unit * gains[...]).astype(bf16)
        cot = cots[side].astype(f32)
        gain_sum[...] += cot * unit
        scaled = cot * gains[...]
        grad_third = inv_std * (
            scaled
            - jnp.mean(scaled, 0, keepdims=True)
            - unit * jnp.mean(scaled * unit, 0, keepdims=True)
        )
        branch = grad_third.astype(bf16)
        grad_out[...] += nt(act, branch)
        grad_value = (nn(out_weight[...], branch) * slope).astype(bf16)
        own_sum[...] += grad_value.astype(f32)
        partial[side] = grad_third + nn(edge_weight[...], grad_value)
        if side == 0:
            for tile, lanes in tiles(rows):
                found = nt(chosen[tile], grad_value[:, lanes])
                near_sum[window_rows(local_first, rows, tile), :] += found[:window, :]
                grad_edge[...] += found[window:, :]
        else:
            far_sum[...] += nt(chosen, grad_value)

    @pl.when(step == pl.num_programs(0) - 1)
    def _():
        table_high, table_low = split(far_sum[:SPAN, :] + near_sum[REACH : REACH + SPAN, :])
        own_high, own_low = split(own_sum[...])
        back = nn(table_high, neighbour_t[...]) + nn(table_low, neighbour_t[...])
        own_back = tn(own_high, residue_t[...]) + tn(own_low, residue_t[...])
        if rows == SPAN:
            back_table[...] = (back + own_back).astype(bf16)
        else:
            own_rows = pl.ds(local_first, rows)
            back_table[...] = back.astype(bf16)
            back_table[own_rows, :] = (back_table[own_rows, :].astype(f32) + own_back).astype(bf16)
        block = states[pl.ds(local_first, rows), :]
        grads[:width, :] = nn(own_high, block) + nn(own_low, block)
        grads[width : 2 * width, :] = tn(table_high, states[...]) + tn(table_low, states[...])
        grads[2 * width :, :width] = grad_edge[...] + far_sum[SPAN:, :]
        grads[2 * width :, 256 : 256 + width] = 0.5 * grad_out[...]
        ones = jnp.ones((16, rows), bf16)
        gain_high, gain_low = split(gain_sum[...])
        vectors[0:1, :width] = (nt(ones, own_high) + nt(ones, own_low))[:1]
        vectors[1:2, :width] = (nt(ones, gain_high) + nt(ones, gain_low))[:1]


def edge_layer(
    meta, states, ids, edges, cots, residue, neighbour, edge_weight, bias, out_weight, gain, local_first
):
    pairs = edges.shape[0] // 2
    width, rows = edges.shape[1:]
    model = states.shape[1]
    by_pair = pl.BlockSpec((2, width, rows), lambda i: (i, 0, 0))
    square = whole((width, width))
    return pl.pallas_call(
        functools.partial(edge_kernel, local_first),
        name="edge_layer",
        grid=(pairs,),
        in_specs=[
            smem,
            whole(states.shape),
            whole(ids.shape),
            by_pair,
            by_pair,
            whole((width, model)),
            whole((width, model)),
            square,
            whole((width, 128)),
            square,
            square,
            whole((width, 128)),
        ],
        out_specs=[
            by_pair,
            by_pair,
            whole((SPAN, model)),
            whole((3 * width, model)),
            whole((8, model)),
        ],
        out_shape=[
            jax.ShapeDtypeStruct(edges.shape, bf16),
            jax.ShapeDtypeStruct(edges.shape, f32),
            jax.ShapeDtypeStruct((SPAN, model), bf16),
            jax.ShapeDtypeStruct((3 * width, model), f32),
            jax.ShapeDtypeStruct((8, model), f32),
        ],
        scratch_shapes=[
            pltpu.VMEM((SPAN + 2 * REACH, 256), bf16),
            pltpu.VMEM((width, SPAN + width), bf16),
            pltpu.VMEM((rows // tile_of(rows), width, window_of(rows) + width), bf16),
            pltpu.VMEM((width, rows), f32),
            pltpu.VMEM((width, rows), f32),
            pltpu.VMEM((SPAN + width, width), f32),
            pltpu.VMEM((SPAN + 2 * REACH, width), f32),
            pltpu.VMEM((width, rows), f32),
            pltpu.VMEM((width, rows), f32),
            pltpu.VMEM((width, width), f32),
            pltpu.VMEM((width, width), f32),
        ],
        compiler_params=params(),
    )(
        meta,
        states,
        ids,
        edges,
        cots,
        residue.T,
        neighbour.T,
        edge_weight,
        jnp.broadcast_to(bias[:, None], (width, 128)),
        out_weight * 0.5,
        out_weight.T * 0.5,
        jnp.broadcast_to(gain[:, None], (width, 128)),
    )


def norm_back(unit, inv_std, gain, grad_out):
    grad_gain = jnp.sum(grad_out * unit, axis=0, keepdims=True)
    scaled = grad_out * gain
    grad_in = inv_std * (
        scaled
        - jnp.mean(scaled, -1, keepdims=True)
        - unit * jnp.mean(scaled * unit, -1, keepdims=True)
    )
    return grad_in, grad_gain


def node_backward_kernel(
    meta,
    own_cot,
    other_cot,
    mine,
    theirs,
    first,
    second,
    stats,
    ffn_input,
    act,
    slope,
    sums,
    gain_one,
    ffn_in,
    ffn_out,
    gain_two,
    grad_first_ref,
    message_cot,
    weights,
    vectors,
    sum_out,
    sum_in,
    sum_message,
):
    step = pl.program_id(0)
    chunk, model = first.shape
    hidden = act.shape[1]
    core = meta[4]
    half = own_cot.shape[0]

    @pl.when(step == 0)
    def _():
        vectors[...] = jnp.zeros_like(vectors)
        sum_out[...] = jnp.zeros_like(sum_out)
        sum_in[...] = jnp.zeros_like(sum_in)
        sum_message[...] = jnp.zeros_like(sum_message)

    if chunk > half:
        mine_first = core == 0
        lower = jnp.where(mine_first, own_cot[...], other_cot[...])
        cot = jnp.concatenate([lower, jnp.where(mine_first, other_cot[...], own_cot[...])], axis=0)
    else:
        row = step * chunk
        inside = pl.ds(pl.multiple_of(lax.rem(row, half), chunk), chunk)
        cot = jnp.where(row // half == core, own_cot[inside, :], other_cot[inside, :])
    total = cot.astype(f32) + (mine[...].astype(f32) + theirs[...].astype(f32))
    second_inv = stats[:, 256:257]
    first_inv = stats[:, 128:129]
    grad_second, gain_two_part = norm_back(second[...], second_inv, gain_two[...], total)
    top = grad_second.astype(bf16)
    grad_hidden = (nt(top, ffn_out[...]) * slope[...].astype(f32)).astype(bf16)
    out_columns = pl.ds(pl.multiple_of(core * (hidden // 2), 128), hidden // 2)
    in_columns = pl.ds(pl.multiple_of(core * (model // 2), 128), model // 2)
    sum_out[...] += tn(act[:, out_columns], top)
    sum_in[...] += tn(ffn_input[:, in_columns], grad_hidden)
    bias_part = jnp.sum(grad_hidden.astype(f32), axis=0, keepdims=True)
    grad_norm = grad_second + nt(grad_hidden, ffn_in[...])
    grad_first, gain_one_part = norm_back(first[...], first_inv, gain_one[...], grad_norm)
    grad_first_ref[...] = grad_first
    spread = (grad_first * stats[:, :1]).astype(bf16)
    message_cot[...] = spread
    sum_message[...] += nn(sums[pl.ds(pl.multiple_of(core * (model // 2), 16), model // 2), :], spread)
    vectors[0:1, :] += gain_one_part
    vectors[1:2, :] += gain_two_part
    for part in range(hidden // model):
        vectors[2 + part : 3 + part, :] += bias_part[:, part * model : (part + 1) * model]

    @pl.when(step == pl.num_programs(0) - 1)
    def _():
        weights[: hidden // 2, :] = sum_out[...].astype(bf16)
        for part in range(hidden // model):
            start = hidden // 2 + part * (model // 2)
            weights[start : start + model // 2, :] = sum_in[
                :, part * model : (part + 1) * model
            ].astype(bf16)
        weights[hidden:, :] = sum_message[...].astype(bf16)


def node_backward(
    meta, own_cot, other_cot, mine, theirs, first, second, stats, ffn_input, act, slope, sums, gain_one, ffn_in, ffn_out, gain_two
):
    rows, model = first.shape
    hidden = act.shape[1]
    chunk = min(rows, 256)

    def by_rows(width):
        return pl.BlockSpec((chunk, width), lambda i: (i, 0))

    return pl.pallas_call(
        node_backward_kernel,
        name="node_backward",
        grid=(rows // chunk,),
        in_specs=[
            smem,
            whole(own_cot.shape),
            whole(other_cot.shape),
            by_rows(model),
            by_rows(model),
            by_rows(model),
            by_rows(model),
            by_rows(384),
            by_rows(model),
            by_rows(hidden),
            by_rows(hidden),
            pl.BlockSpec((model, chunk), lambda i: (0, i)),
            whole((1, model)),
            whole(ffn_in.shape),
            whole(ffn_out.shape),
            whole((1, model)),
        ],
        out_specs=[
            by_rows(model),
            by_rows(model),
            whole((hidden + model // 2, model)),
            whole((8, model)),
        ],
        out_shape=[
            jax.ShapeDtypeStruct((rows, model), f32),
            jax.ShapeDtypeStruct((rows, model), bf16),
            jax.ShapeDtypeStruct((hidden + model // 2, model), bf16),
            jax.ShapeDtypeStruct((8, model), f32),
        ],
        scratch_shapes=[
            pltpu.VMEM((hidden // 2, model), f32),
            pltpu.VMEM((model // 2, hidden), f32),
            pltpu.VMEM((model // 2, model), f32),
        ],
        compiler_params=params(),
    )(
        meta,
        own_cot,
        other_cot,
        mine,
        theirs,
        first,
        second,
        stats,
        ffn_input,
        act,
        slope,
        sums,
        gain_one[None],
        ffn_in,
        ffn_out,
        gain_two[None],
    )


def message_backward_kernel(
    static_first,
    meta,
    table,
    cot,
    ids,
    edges,
    slope,
    receiver,
    neighbour,
    out_weight,
    edge_grads,
    edge_vectors,
    node_vectors,
    keep,
    send,
    keep_weights,
    send_weights,
    spread,
    far_sum,
    near_sum,
    own_sum,
    weights,
):
    step = pl.program_id(0)
    model, rows = spread.shape
    width = edges.shape[1]
    half = keep.shape[0]
    local_first = pl.multiple_of(meta[1], 128) if static_first is None else static_first

    @pl.when(step == 0)
    def _():
        spread[...] = 0.5 * nt(out_weight[...], cot[...])
        for total in (far_sum, near_sum, own_sum, weights):
            total[...] = jnp.zeros_like(total)

    window = window_of(rows)
    edge_rows = slice(2 * model, 2 * model + width)
    near, far = (ids[pl.ds(2 * step + side, 1), :] - meta[2] for side in range(2))
    far_grad = (spread[...] * slope[1].astype(f32)).astype(bf16)
    near_grad = (spread[...] * slope[0].astype(f32)).astype(bf16)
    own_sum[...] += far_grad.astype(f32) + near_grad.astype(f32)
    far_sum[...] += nt(far_rows(far, edges[1]), far_grad)
    for tile, lanes in tiles(rows):
        part = near_rows(near[:, lanes], edges[0, :, lanes], local_first + lanes.start)
        found = nt(part, near_grad[:, lanes])
        near_sum[window_rows(local_first, rows, tile), :] += found[:window, :]
        weights[edge_rows, :] += found[window:, :]

    @pl.when(step == pl.num_programs(0) - 1)
    def _():
        table_sum = far_sum[:SPAN, :] + near_sum[REACH : REACH + SPAN, :]
        own_rows = own_sum[...].T
        table_high, table_low = split(table_sum)
        own_high, own_low = split(own_rows)
        nodes_t = table[...].T
        block_t = nodes_t
        if rows < SPAN:
            block_t = table[pl.ds(local_first, rows), :].T
        weights[:model, :] = nn(block_t, own_high) + nn(block_t, own_low)
        weights[model : 2 * model, :] = nn(nodes_t, table_high) + nn(nodes_t, table_low)
        weights[edge_rows, :] += far_sum[SPAN:, :]
        start = edge_rows.stop
        weights[start : start + 3 * width, :] = edge_grads[...]
        start += 3 * width
        weights[start : start + 8, :] = edge_vectors[...]
        weights[start + 8 : start + 16, :] = 0.5 * node_vectors[...]
        weights[start + 16 : start + 17, :] = jnp.sum(own_rows, axis=0, keepdims=True)
        core = meta[4]
        split_rows = keep_weights.shape[0]
        mine = pl.multiple_of(core * split_rows, split_rows)
        keep_weights[...] = weights[pl.ds(mine, split_rows), :]
        send_weights[...] = weights[pl.ds(split_rows - mine, split_rows), :].astype(bf16)
        back = nt(table_high, neighbour[...]) + nt(table_low, neighbour[...])
        own_back = nt(own_high, receiver[...]) + nt(own_low, receiver[...])
        if rows == SPAN:
            far_sum[:SPAN, :] = back + own_back
        else:
            far_sum[:SPAN, :] = back
            far_sum[pl.ds(local_first, rows), :] += own_back
        high = meta[0]
        keep[...] = far_sum[pl.ds(pl.multiple_of(high * half, half), half), :]
        send[...] = far_sum[pl.ds(pl.multiple_of((1 - high) * half, half), half), :].astype(bf16)


def message_backward(
    meta, table, cot, ids, edges, slope, receiver, neighbour, out_weight, edge_grads, edge_vectors, node_vectors, local_first
):
    pairs = edges.shape[0] // 2
    width, rows = edges.shape[1:]
    model = table.shape[1]
    square = whole((model, model))
    used = 2 * model + 4 * width + 24
    split_rows = -(-used // 512) * 256
    return pl.pallas_call(
        functools.partial(message_backward_kernel, local_first),
        name="message_backward",
        grid=(pairs,),
        in_specs=[
            smem,
            whole(table.shape),
            whole(cot.shape),
            whole(ids.shape),
            pl.BlockSpec((2, width, rows), lambda i: (i, 0, 0)),
            pl.BlockSpec((2, model, rows), lambda i: (i, 0, 0)),
            square,
            square,
            square,
            whole(edge_grads.shape),
            whole(edge_vectors.shape),
            whole(node_vectors.shape),
        ],
        out_specs=[
            whole((SPAN // 2, model)),
            whole((SPAN // 2, model)),
            whole((split_rows, model)),
            whole((split_rows, model)),
            whole((model, rows)),
        ],
        out_shape=[
            jax.ShapeDtypeStruct((SPAN // 2, model), f32),
            jax.ShapeDtypeStruct((SPAN // 2, model), bf16),
            jax.ShapeDtypeStruct((split_rows, model), f32),
            jax.ShapeDtypeStruct((split_rows, model), bf16),
            jax.ShapeDtypeStruct((model, rows), f32),
        ],
        scratch_shapes=[
            pltpu.VMEM((SPAN + width, model), f32),
            pltpu.VMEM((SPAN + 2 * REACH, model), f32),
            pltpu.VMEM((model, rows), f32),
            pltpu.VMEM((2 * split_rows, model), f32),
        ],
        compiler_params=params(),
    )(
        meta,
        table,
        cot,
        ids,
        edges,
        slope,
        receiver,
        neighbour,
        out_weight,
        edge_grads,
        edge_vectors,
        node_vectors,
    )


def edge_gradient_kernel(partial, slope, spread, edge_weight, out):
    for side in range(partial.shape[0]):
        grad_value = (spread[...] * slope[side].astype(f32)).astype(bf16)
        out[side] = partial[side] + nn(edge_weight[...], grad_value)


def edge_gradient(first, count, values, slope, spread, edge_weight):
    width, rows = values.shape[1:]
    model = spread.shape[0]
    by_pair = pl.BlockSpec((2, width, rows), lambda i: (first + i, 0, 0))
    return pl.pallas_call(
        edge_gradient_kernel,
        name="edge_gradient",
        grid=(count,),
        in_specs=[
            by_pair,
            pl.BlockSpec((2, model, rows), lambda i: (first + i, 0, 0)),
            whole(spread.shape),
            whole(edge_weight.shape),
        ],
        out_specs=by_pair,
        out_shape=jax.ShapeDtypeStruct(values.shape, f32),
        input_output_aliases={0: 0},
        compiler_params=params(),
    )(values, slope, spread, edge_weight)


def sum_to_slots_kernel(shift, meta, *refs):
    parts, outs, total = refs[:-5], refs[-5:-1], refs[-1]
    total[...] = parts[0][...].astype(f32)
    for part in parts[1:]:
        total[...] += part[...].astype(f32)
    place = meta[5] >> shift & 3
    rows = outs[0].shape[0]
    for slot, out in enumerate(outs):
        start = pl.multiple_of((place ^ slot) * rows, rows)
        out[...] = total[pl.ds(start, rows), :].astype(out.dtype)


def sum_to_slots(meta, shift, parts):
    rows, width = parts[0].shape
    out_types = (f32, bf16, bf16, bf16)
    return pl.pallas_call(
        functools.partial(sum_to_slots_kernel, shift),
        name="sum_to_slots",
        in_specs=[smem] + [whole(part.shape) for part in parts],
        out_specs=[whole((rows // 4, width))] * 4,
        out_shape=[jax.ShapeDtypeStruct((rows // 4, width), kind) for kind in out_types],
        scratch_shapes=[pltpu.VMEM((rows, width), f32)],
        compiler_params=params(),
    )(meta, *parts)


def sum_parts_kernel(*refs):
    total = refs[0][...].astype(f32)
    for part in refs[1:-1]:
        total = total + part[...].astype(f32)
    refs[-1][...] = total.astype(bf16)


def sum_parts(parts):
    return pl.pallas_call(
        sum_parts_kernel,
        name="sum_parts",
        in_specs=[whole(part.shape) for part in parts],
        out_specs=whole(parts[0].shape),
        out_shape=jax.ShapeDtypeStruct(parts[0].shape, bf16),
        compiler_params=params(),
    )(*parts)


def assemble_kernel(shift, meta, *refs):
    place = meta[5] >> shift & 3
    rows = refs[0].shape[0]
    for slot, part in enumerate(refs[:-1]):
        start = pl.multiple_of((place ^ slot) * rows, rows)
        refs[-1][pl.ds(start, rows), :] = part[...]


def assemble(meta, shift, parts):
    rows, width = parts[0].shape
    return pl.pallas_call(
        functools.partial(assemble_kernel, shift),
        name="assemble",
        in_specs=[smem] + [whole(part.shape) for part in parts],
        out_specs=whole((4 * rows, width)),
        out_shape=jax.ShapeDtypeStruct((4 * rows, width), bf16),
        compiler_params=params(),
    )(meta, *parts)


def sent_each_way(shift, slots):
    return [moved(slot, place << shift) for place, slot in enumerate(slots) if place > 0]


def moved(value, mask):
    devices = lax.axis_size("res") * lax.axis_size("nbr")
    cores = lax.axis_size("nbr")
    pairs = [(source, source ^ (mask * cores)) for source in range(devices)]
    return lax.ppermute(value, ("res", "nbr"), pairs)


def unpack_early_kernel(meta, own, other, grad_out, grad_in, message_out):
    core = meta[4]
    hidden, model = grad_out.shape
    half = model // 2
    for side, source in enumerate((own, other)):
        place = core if side == 0 else 1 - core
        grad_out[pl.ds(pl.multiple_of(place * (hidden // 2), 8), hidden // 2), :] = source[
            : hidden // 2, :
        ].astype(f32)
        rows = pl.ds(pl.multiple_of(place * half, 8), half)
        for part in range(hidden // model):
            start = hidden // 2 + part * half
            grad_in[rows, part * model : (part + 1) * model] = source[start : start + half, :].astype(f32)
        message_out[rows, :] = source[hidden:, :].astype(f32)


def unpack_early(meta, own, other, hidden):
    model = own.shape[1]
    return pl.pallas_call(
        unpack_early_kernel,
        name="unpack_early",
        in_specs=[smem, whole(own.shape), whole(other.shape)],
        out_specs=[whole((hidden, model)), whole((model, hidden)), whole((model, model))],
        out_shape=[
            jax.ShapeDtypeStruct((hidden, model), f32),
            jax.ShapeDtypeStruct((model, hidden), f32),
            jax.ShapeDtypeStruct((model, model), f32),
        ],
        compiler_params=params(),
    )(meta, own, other)


def unpack_late_kernel(
    meta, own, other, grad_self, grad_near, grad_edge, edge_self, edge_near, edge_edge, edge_out, vectors, weights
):
    core = meta[4]
    rows, model = own.shape
    width = edge_self.shape[0]
    mine = pl.multiple_of(core * rows, rows)
    weights[pl.ds(mine, rows), :] = own[...]
    weights[pl.ds(rows - mine, rows), :] = other[...]
    grad_self[...] = weights[:model, :].astype(f32)
    grad_near[...] = weights[model : 2 * model, :].astype(f32)
    start = 2 * model
    for out in (grad_edge, edge_self, edge_near):
        out[...] = weights[start : start + width, :].astype(f32)
        start += width
    edge_edge[...] = weights[start : start + width, :width].astype(f32)
    edge_out[...] = weights[start : start + width, 256 : 256 + width].astype(f32)
    start += width
    vectors[...] = weights[start : start + 32, :].astype(f32)


def unpack_late(meta, own, other, width):
    rows, model = own.shape
    shapes = [(model, model)] * 2 + [(width, model)] * 3 + [(width, width)] * 2 + [(32, model)]
    return pl.pallas_call(
        unpack_late_kernel,
        name="unpack_late",
        in_specs=[smem, whole(own.shape), whole(other.shape)],
        out_specs=[whole(shape) for shape in shapes],
        out_shape=[jax.ShapeDtypeStruct(shape, f32) for shape in shapes],
        scratch_shapes=[pltpu.VMEM((2 * rows, model), bf16)],
        compiler_params=params(),
    )(meta, own, other)


def planes(size):
    return [[4 * block + place for place in range(4)] for block in range(size // 4)]


def columns(size):
    return [[4 * block + place for block in range(size // 4)] for place in range(4)]


def tied(*arrays):
    return lax.optimization_barrier(arrays)


def early_parts(size):
    if size != 16:
        return (
            lambda value: lax.psum(value.astype(f32), "res").astype(bf16),
            lambda value: value,
            lambda value: value,
        )
    return (
        lambda value: lax.psum_scatter(value, "res", axis_index_groups=planes(size), tiled=True),
        lambda value: lax.psum(value, "res", axis_index_groups=columns(size)),
        lambda value: lax.all_gather(value, "res", axis_index_groups=planes(size), tiled=True),
    )


def late_sum(meta, kept, sent, size, value, pieces, early, early_steps):
    received = swapped(sent, 0)
    early = early_steps[1](early)
    value, received = tied(pieces[0](value), received)
    if size != 16:
        total = lax.psum(kept + received.astype(f32), "res").astype(bf16)
        for piece in pieces[1:]:
            value = piece(value)
        return total, value, early_steps[2](early)
    value, kept, *slots = tied(value, *sum_to_slots(meta, 0, [kept, received]))
    value, *received = tied(pieces[1](value), *sent_each_way(0, [kept, *slots]))
    value, kept, *slots = tied(value, *sum_to_slots(meta, 2, [kept, *received]))
    value, *received = tied(pieces[2](value), *sent_each_way(2, [kept, *slots]))
    value, early, mine = tied(value, early, sum_parts([kept, *received]))
    early = early_steps[2](early)
    value, *received = tied(pieces[3](value), *sent_each_way(2, [mine] * 4))
    value, mine = tied(value, assemble(meta, 2, [mine, *received]))
    value, early, *received = tied(pieces[4](value), early, *sent_each_way(0, [mine] * 4))
    return assemble(meta, 0, [mine, *received]), value, early


def joined(table, other, high_side):
    return jnp.where(
        high_side, jnp.concatenate([other, table], axis=0), jnp.concatenate([table, other], axis=0)
    )


def halves(table, high_side):
    half = table.shape[0] // 2
    lower, upper = (table[:half], table[half:])
    return (jnp.where(high_side, upper, lower), jnp.where(high_side, lower, upper))


def sum_blocks(table, device, level):
    keep, send = halves(table, device >> level & 1 == 1)
    return keep + swapped(send.astype(bf16), level).astype(keep.dtype)


def on_device(
    nodes,
    edges,
    neighbours,
    lengths,
    message_receiver_weight,
    message_neighbour_weight,
    message_edge_weight,
    message_hidden_bias,
    message_output_weight,
    gain_one,
    ffn_in,
    ffn_bias,
    ffn_out,
    gain_two,
    edge_update_residue_weight,
    edge_update_neighbour_weight,
    edge_update_edge_weight,
    edge_update_bias,
    edge_out,
    gain_three,
    node_cot,
    edge_cot,
):
    rows, half_k, edge_width = edges.shape
    own_rows, model = nodes.shape
    hidden = ffn_in.shape[1]
    levels = (SPAN // own_rows).bit_length() - 1
    core = lax.axis_index("nbr")
    device = lax.axis_index("res") * lax.axis_size("nbr") + core
    first_row = lax.axis_index("res") * rows
    bucket = first_row // SPAN
    group_start = bucket * SPAN
    local_first = 0 if rows == SPAN else None
    length = jnp.sum(jnp.where(jnp.arange(lengths.shape[0]) == bucket, lengths, 0))
    top = device >> (levels - 1) & 1
    meta = jnp.stack(
        [top, first_row - group_start, group_start, length, core, lax.axis_index("res"), 0, 0]
    ).astype(jnp.int32)

    ids = neighbours.T
    edges_t = edges.transpose(1, 2, 0)
    cot_t = edge_cot.transpose(1, 2, 0)

    table = nodes
    for level in range(levels - 1):
        table = joined(table, swapped(table, level), device >> level & 1 == 1)
    other_table = swapped(table, levels - 1)
    other_cot = swapped(node_cot, 0)

    node_table, slope, packed = message_forward(
        meta,
        table,
        other_table,
        ids,
        edges_t,
        message_receiver_weight,
        message_neighbour_weight,
        message_edge_weight,
        message_hidden_bias,
        local_first,
    )
    block = node_table
    if rows < SPAN:
        block = lax.dynamic_slice_in_dim(node_table, first_row - group_start, rows, 0)
    state, ffn_input, act, ffn_slope, first, second, stats, sums = node_forward(
        block,
        packed,
        swapped(packed, 0),
        message_output_weight,
        gain_one,
        ffn_in,
        ffn_bias,
        ffn_out,
        gain_two,
    )
    states = state
    for level in range(1, levels):
        states = joined(states, swapped(states, level), device >> level & 1 == 1)
    new_edges, partial, back, edge_grads, edge_vectors = edge_layer(
        meta,
        states,
        ids,
        edges_t,
        cot_t,
        edge_update_residue_weight,
        edge_update_neighbour_weight,
        edge_update_edge_weight,
        edge_update_bias,
        edge_out,
        gain_three,
        local_first,
    )
    for level in reversed(range(1, levels)):
        back = sum_blocks(back, device, level)
    grad_first, message_cot, early, node_vectors = node_backward(
        meta,
        node_cot,
        other_cot,
        back,
        swapped(back, 0),
        first,
        second,
        stats,
        ffn_input,
        act,
        ffn_slope,
        sums,
        gain_one,
        ffn_in,
        ffn_out,
        gain_two,
    )
    size = lax.axis_size("res")
    early_steps = early_parts(size)
    early = early_steps[0](early)
    keep, send, kept_weights, sent_weights, spread = message_backward(
        meta,
        node_table,
        message_cot,
        ids,
        edges_t,
        slope,
        message_receiver_weight,
        message_neighbour_weight,
        message_output_weight,
        edge_grads,
        edge_vectors,
        node_vectors,
        local_first,
    )
    early, kept_weights, sent_weights = tied(early, kept_weights, sent_weights)
    kept = keep + swapped(send, levels - 1).astype(f32)
    for level in reversed(range(levels - 1)):
        kept = sum_blocks(kept, device, level)
    pieces = 5 if half_k % 10 == 0 else 1
    count = half_k // 2 // pieces

    def piece(index):
        return lambda values: edge_gradient(index * count, count, values, slope, spread, message_edge_weight)

    late, edge_grad, early = late_sum(
        meta,
        kept_weights,
        sent_weights,
        size,
        partial,
        [piece(index) for index in range(pieces)],
        early,
        early_steps,
    )
    own_first = lax.dynamic_slice_in_dim(grad_first, core * own_rows, own_rows, 0)
    node_grad = own_first + kept
    node_out = lax.dynamic_slice_in_dim(state, core * own_rows, own_rows, 0)
    grad_ffn_out, grad_ffn_in, grad_msg_out = unpack_early(meta, early, swapped(early, 0), hidden)
    (
        grad_msg_self,
        grad_msg_nbr,
        grad_msg_edge,
        grad_edge_self,
        grad_edge_nbr,
        grad_edge_edge,
        grad_edge_out,
        vectors,
    ) = unpack_late(meta, late, swapped(late, 0), edge_width)
    return (
        node_out,
        new_edges.transpose(2, 0, 1),
        node_grad,
        edge_grad.transpose(2, 0, 1),
        grad_msg_self,
        grad_msg_nbr,
        grad_msg_edge,
        vectors[16],
        grad_msg_out,
        vectors[8],
        grad_ffn_in,
        vectors[10 : 10 + hidden // model].reshape(-1),
        grad_ffn_out,
        vectors[9],
        grad_edge_self.T,
        grad_edge_nbr.T,
        grad_edge_edge,
        vectors[0, :edge_width],
        grad_edge_out,
        vectors[1, :edge_width],
    )


def solution(mesh):
    rows = P(("res", "nbr"), None)
    pairs = P("res", "nbr", None)
    placed = (rows, pairs, P("res", "nbr")) + (P(),) * 17 + (rows, pairs)
    return jax.shard_map(
        on_device,
        mesh=mesh,
        in_specs=placed,
        out_specs=(rows, pairs, rows, pairs) + (P(),) * 16,
        check_vma=False,
    )
```

```python
import functools

import jax
import jax.numpy as jnp
from jax import lax
from jax.experimental import pallas as pl
from jax.experimental.pallas import tpu as pltpu
from jax.sharding import PartitionSpec as P

SPAN = 1024
REACH = 32
MASKED = -16384.0
FORWARD_GROUP = 2
EDGE_GROUP = 6
MSG_GROUP = 6
NODE_CHUNK = 256

epsilon = 1e-05
root_half = 0.7071067811865476
inv_root_two_pi = 0.3989422804014327
half_log2_e = 0.7213475204444817

bf16 = jnp.bfloat16
f32 = jnp.float32


def swapped(value, level):
    mask = 2**level
    devices = lax.axis_size("res") * lax.axis_size("nbr")
    pairs = [(source, source ^ mask) for source in range(devices)]
    return lax.ppermute(value, ("res", "nbr"), pairs)


def nn(left_op, right_op):
    return jnp.dot(left_op, right_op, preferred_element_type=f32)


def nt(left_op, right_op):
    return lax.dot_general(
        left_op, right_op, (((1,), (1,)), ((), ())), preferred_element_type=f32
    )


def tn(left_op, right_op):
    return lax.dot_general(
        left_op, right_op, (((0,), (0,)), ((), ())), preferred_element_type=f32
    )


def split(values):
    high = values.astype(bf16)
    return high, (values - high.astype(f32)).astype(bf16)


def twice_gelu_and_slope(values):
    below = 1.0 + lax.erf(values * root_half)
    density = jnp.exp2(values * values * -half_log2_e)
    return values * below, below + values * density * (2.0 * inv_root_two_pi)


def selector(rows, ids):
    places = lax.broadcasted_iota(jnp.int16, (rows, ids.shape[1]), 0)
    return jnp.where(places == ids.astype(jnp.int16), bf16(1), bf16(0))


def group_of(count, wanted):
    return wanted if count % wanted == 0 else 2


def tile_of(rows):
    return min(rows, 256)


def window_of(rows):
    return tile_of(rows) + 2 * REACH


def far_rows(ids, edge):
    return jnp.concatenate([selector(SPAN, ids), edge], axis=0)


def near_rows(ids, edge, first):
    return jnp.concatenate([selector(ids.shape[1] + 2 * REACH, ids - (first - REACH)), edge], axis=0)


def beside(parts):
    return parts[0] if len(parts) == 1 else jnp.concatenate(parts, axis=1)


def tiles(rows):
    width = tile_of(rows)
    return [(tile, slice(tile * width, (tile + 1) * width)) for tile in range(rows // width)]


def window_rows(local_first, rows, tile):
    start = local_first + tile * tile_of(rows)
    if not isinstance(start, int):
        start = pl.multiple_of(start, 128)
    return pl.ds(start, window_of(rows))


def repeat_lanes(column, width):
    return jnp.concatenate([column] * (width // column.shape[1]), axis=1)


def whole(shape):
    return pl.BlockSpec(shape, lambda *_: (0,) * len(shape))


def params(mebibytes=60):
    return pltpu.CompilerParams(vmem_limit_bytes=mebibytes * 2**20)


smem = pl.BlockSpec(memory_space=pltpu.SMEM)


def message_forward_kernel(
    static_first,
    meta,
    lengths,
    own,
    other,
    ids,
    edges,
    receiver,
    neighbour,
    edge_weight,
    bias,
    table,
    slope,
    packed,
    padded,
    far_table,
    near_table,
    base,
    sums,
    counts,
):
    step = pl.program_id(0)
    rows = base.shape[1]
    half = own.shape[0]
    length = lengths[meta[3]]
    local_first = pl.multiple_of(meta[1], 128) if static_first is None else static_first

    @pl.when(step == 0)
    def _():
        high = meta[0]
        table[pl.ds(pl.multiple_of(high * half, half), half), :] = own[...]
        table[pl.ds(pl.multiple_of((1 - high) * half, half), half), :] = other[...]
        places = lax.broadcasted_iota(jnp.int32, (SPAN, 1), 0)
        hidden = jnp.where(places < length, 0.0, MASKED)
        projected = (nn(table[...], neighbour[...]) + hidden).astype(bf16)
        far_table[...] = jnp.concatenate([projected, edge_weight[...]], axis=0).T
        padded[...] = jnp.zeros_like(padded)
        padded[REACH : REACH + SPAN, :] = projected
        for tile, _ in tiles(rows):
            window = padded[window_rows(local_first, rows, tile), :]
            near_table[tile] = jnp.concatenate([window, edge_weight[...]], axis=0).T
        block = table[pl.ds(local_first, rows), :]
        places = lax.broadcasted_iota(jnp.int32, (rows, 1), 0) + local_first
        hidden = jnp.where(places < length, 0.0, MASKED)
        base[...] = (nn(block, receiver[...]) + (bias[...] + hidden)).T
        sums[...] = jnp.zeros_like(sums)
        counts[...] = jnp.zeros_like(counts)

    positions = lax.broadcasted_iota(jnp.int32, (1, rows), 1) + local_first
    group = edges.shape[0]
    near = [ids[pl.ds(group * step + k, 1), :] - meta[2] for k in range(group)]
    counts[...] += jnp.where(positions < length, 1.0, 0.0) * sum(
        jnp.where(place < length, 1.0, 0.0) for place in near
    )
    for tile, lanes in tiles(rows):
        for k in range(0, group, 2):
            near_part = near_rows(near[k][:, lanes], edges[k, :, lanes], local_first + lanes.start)
            far_part = far_rows(near[k + 1][:, lanes], edges[k + 1, :, lanes])
            far_value = nn(far_table[...], far_part)
            near_value = nn(near_table[tile], near_part)
            far_act, far_slope = twice_gelu_and_slope(far_value + base[:, lanes])
            slope[k + 1, :, lanes] = far_slope.astype(bf16)
            near_act, near_slope = twice_gelu_and_slope(near_value + base[:, lanes])
            slope[k, :, lanes] = near_slope.astype(bf16)
            sums[:, lanes] += far_act + near_act

    @pl.when(step == pl.num_programs(0) - 1)
    def _():
        width = sums.shape[0]
        packed[:width, :] = (0.5 * sums[...]).astype(bf16)
        packed[width:, :] = jnp.broadcast_to(counts[...], (16, rows)).astype(bf16)


def message_forward(meta, lengths, own, other, ids, edges, receiver, neighbour, edge_weight, bias, local_first):
    columns_in = edges.shape[0]
    group = group_of(columns_in, FORWARD_GROUP)
    width, rows = edges.shape[1:]
    model = own.shape[1]
    return pl.pallas_call(
        functools.partial(message_forward_kernel, local_first),
        name="message_forward",
        grid=(columns_in // group,),
        in_specs=[
            smem,
            smem,
            whole(own.shape),
            whole(other.shape),
            whole(ids.shape),
            pl.BlockSpec((group, width, rows), lambda i: (i, 0, 0)),
            whole(receiver.shape),
            whole(neighbour.shape),
            whole(edge_weight.shape),
            whole((1, model)),
        ],
        out_specs=[
            whole((SPAN, model)),
            pl.BlockSpec((group, model, rows), lambda i: (i, 0, 0)),
            whole((model + 16, rows)),
        ],
        out_shape=[
            jax.ShapeDtypeStruct((SPAN, model), bf16),
            jax.ShapeDtypeStruct((columns_in, model, rows), bf16),
            jax.ShapeDtypeStruct((model + 16, rows), bf16),
        ],
        scratch_shapes=[
            pltpu.VMEM((SPAN + 2 * REACH, model), bf16),
            pltpu.VMEM((model, SPAN + width), bf16),
            pltpu.VMEM((rows // tile_of(rows), model, window_of(rows) + width), bf16),
            pltpu.VMEM((model, rows), f32),
            pltpu.VMEM((model, rows), f32),
            pltpu.VMEM((1, rows), f32),
        ],
        compiler_params=params(),
    )(meta, lengths, own, other, ids, edges, receiver, neighbour, edge_weight, bias[None])


def normed(values):
    mean_val = jnp.mean(values, -1, keepdims=True)
    centered = values - mean_val
    inv_std = lax.rsqrt(jnp.mean(centered * centered, -1, keepdims=True) + epsilon)
    return centered * inv_std, inv_std


def node_forward_kernel(
    meta,
    nodes,
    mine,
    theirs,
    out_weight,
    gain_one,
    ffn_in,
    ffn_bias,
    ffn_out,
    gain_two,
    state,
    ffn_input,
    act,
    slope,
    first,
    second,
    stats,
    sums,
    own_state,
):
    step = pl.program_id(0)
    rows, width = nodes.shape
    total = mine[...].astype(f32) + theirs[...].astype(f32)
    count = jnp.maximum(total[width : width + 1, :], 1.0)
    ratio = 1.0 / jnp.broadcast_to(count, (128, rows)).T
    high, low = split(total[:width, :])
    sums[...] = high
    message = tn(high, out_weight[...]) + tn(low, out_weight[...])
    first_sum = nodes[...].astype(f32) + message * repeat_lanes(ratio, width)
    first_unit, first_inv = normed(first_sum)
    first[...] = first_unit.astype(bf16)
    first_norm = first_unit * gain_one[...]
    low = first_norm.astype(bf16)
    ffn_input[...] = low
    hidden, grad = twice_gelu_and_slope(nn(low, ffn_in[...]) + ffn_bias[...])
    hidden = (0.5 * hidden).astype(bf16)
    act[...] = hidden
    slope[...] = (0.5 * grad).astype(bf16)
    second_unit, second_inv = normed(first_norm + nn(hidden, ffn_out[...]))
    second[...] = second_unit.astype(bf16)
    out = (second_unit * gain_two[...]).astype(bf16)
    state[...] = out
    store_own_rows(own_state, out, step, meta[4])
    lane = lax.broadcasted_iota(jnp.int32, ratio.shape, 1)
    stats[...] = jnp.where(lane == 0, ratio, jnp.where(lane == 1, first_inv, second_inv))


def store_own_rows(own, values, step, core):
    half, chunk = own.shape[0], values.shape[0]
    if chunk > half:
        own[...] = jnp.where(core == 0, values[:half, :], values[half:, :])
        return
    place = step * chunk

    @pl.when(place // half == core)
    def _():
        own[pl.ds(pl.multiple_of(lax.rem(place, half), chunk), chunk), :] = values


def node_forward(meta, nodes, mine, theirs, out_weight, gain_one, ffn_in, ffn_bias, ffn_out, gain_two):
    rows, model = nodes.shape
    hidden = ffn_in.shape[1]
    chunk = min(rows, NODE_CHUNK)

    def by_rows(width):
        return pl.BlockSpec((chunk, width), lambda i: (i, 0))

    return pl.pallas_call(
        node_forward_kernel,
        name="node_forward",
        grid=(rows // chunk,),
        in_specs=[
            smem,
            by_rows(model),
            pl.BlockSpec((model + 16, chunk), lambda i: (0, i)),
            pl.BlockSpec((model + 16, chunk), lambda i: (0, i)),
            whole(out_weight.shape),
            whole((1, model)),
            whole(ffn_in.shape),
            whole((1, hidden)),
            whole(ffn_out.shape),
            whole((1, model)),
        ],
        out_specs=[
            by_rows(model),
            by_rows(model),
            by_rows(hidden),
            by_rows(hidden),
            by_rows(model),
            by_rows(model),
            by_rows(128),
            pl.BlockSpec((model, chunk), lambda i: (0, i)),
            whole((rows // 2, model)),
        ],
        out_shape=[
            jax.ShapeDtypeStruct((rows, model), bf16),
            jax.ShapeDtypeStruct((rows, model), bf16),
            jax.ShapeDtypeStruct((rows, hidden), bf16),
            jax.ShapeDtypeStruct((rows, hidden), bf16),
            jax.ShapeDtypeStruct((rows, model), bf16),
            jax.ShapeDtypeStruct((rows, model), bf16),
            jax.ShapeDtypeStruct((rows, 128), f32),
            jax.ShapeDtypeStruct((model, rows), bf16),
            jax.ShapeDtypeStruct((rows // 2, model), bf16),
        ],
        compiler_params=params(),
    )(
        meta, nodes, mine, theirs, out_weight, gain_one[None], ffn_in, ffn_bias[None], ffn_out, gain_two[None]
    )


def edge_kernel(
    static_first,
    meta,
    states,
    ids,
    edges,
    cots,
    residue_t,
    neighbour_t,
    edge_weight,
    bias,
    out_weight,
    out_weight_t,
    gain,
    new_edges,
    partial,
    back_table,
    grads,
    squares,
    vectors,
    padded,
    far_table,
    near_table,
    base,
    gains,
    far_sum,
    near_sum,
    own_sum,
    gain_sum,
    grad_edge,
    grad_out,
):
    step = pl.program_id(0)
    width, rows = base.shape
    window = window_of(rows)
    local_first = pl.multiple_of(meta[1], 128) if static_first is None else static_first

    @pl.when(step == 0)
    def _():
        fill = jnp.zeros((width, 256 - width), bf16)
        weight = jnp.concatenate([edge_weight[...], fill], axis=1)
        projected = nt(states[...], neighbour_t[...]).astype(bf16)
        projected = jnp.concatenate([projected, jnp.zeros((SPAN, 256 - width), bf16)], axis=1)
        far_table[...] = jnp.concatenate([projected, weight], axis=0).T[:width, :]
        padded[...] = jnp.zeros_like(padded)
        padded[REACH : REACH + SPAN, :] = projected
        for tile, _ in tiles(rows):
            part = padded[window_rows(local_first, rows, tile), :]
            near_table[tile] = jnp.concatenate([part, weight], axis=0).T[:width, :]
        block = states[pl.ds(local_first, rows), :]
        base[...] = nt(residue_t[...], block) + repeat_lanes(bias[...], rows)
        gains[...] = repeat_lanes(gain[...], rows)
        for total in (far_sum, near_sum, own_sum, gain_sum, grad_edge, grad_out):
            total[...] = jnp.zeros_like(total)

    group = edges.shape[0]
    order = list(range(1, group, 2)) + list(range(0, group, 2))
    found_rows, found_grads = {}, {}
    for side in order:
        near = ids[pl.ds(group * step + side, 1), :] - meta[2]
        edge = edges[side]
        if side % 2 == 0:
            chosen = [
                near_rows(near[:, lanes], edges[side, :, lanes], local_first + lanes.start)
                for _, lanes in tiles(rows)
            ]
            value = jnp.concatenate(
                [nn(near_table[tile], part) for tile, part in enumerate(chosen)], axis=1
            )
        else:
            chosen = far_rows(near, edge)
            value = nn(far_table[...], chosen)
        act, slope = twice_gelu_and_slope(value + base[...])
        act = act.astype(bf16)
        third = edge.astype(f32) + nn(out_weight_t[...], act)
        centered = third - jnp.mean(third, 0, keepdims=True)
        inv_std = lax.rsqrt(jnp.mean(centered * centered, 0, keepdims=True) + epsilon)
        unit = centered * inv_std
        new_edges[side] = (unit * gains[...]).astype(bf16)
        cot = cots[side].astype(f32)
        gain_sum[...] += cot * unit
        scaled = cot * gains[...]
        grad_third = inv_std * (
            scaled
            - jnp.mean(scaled, 0, keepdims=True)
            - unit * jnp.mean(scaled * unit, 0, keepdims=True)
        )
        branch = grad_third.astype(bf16)
        grad_out[...] += nt(act, branch)
        grad_wide = nn(out_weight[...], branch) * slope
        own_sum[...] += grad_wide
        grad_value = grad_wide.astype(bf16)
        partial[side] = (grad_third + nn(edge_weight[...], grad_value)).astype(bf16)
        found_rows[side], found_grads[side] = chosen, grad_value
        if side == order[group // 2 - 1]:
            far_sum[...] += nt(
                beside([found_rows[k] for k in order[: group // 2]]),
                beside([found_grads[k] for k in order[: group // 2]]),
            )
    for tile, lanes in tiles(rows):
        found = nt(
            beside([found_rows[k][tile] for k in range(0, group, 2)]),
            beside([found_grads[k][:, lanes] for k in range(0, group, 2)]),
        )
        near_sum[window_rows(local_first, rows, tile), :] += found[:window, :]
        grad_edge[...] += found[window:, :]

    @pl.when(step == pl.num_programs(0) - 1)
    def _():
        table_high, table_low = split(far_sum[:SPAN, :] + near_sum[REACH : REACH + SPAN, :])
        own_high, own_low = split(own_sum[...])
        back = nn(table_high, neighbour_t[...]) + nn(table_low, neighbour_t[...])
        own_back = tn(own_high, residue_t[...]) + tn(own_low, residue_t[...])
        if rows == SPAN:
            back_table[...] = (back + own_back).astype(bf16)
        else:
            own_rows = pl.ds(local_first, rows)
            back_table[...] = back.astype(bf16)
            back_table[own_rows, :] = (back_table[own_rows, :].astype(f32) + own_back).astype(bf16)
        block = states[pl.ds(local_first, rows), :]
        grad_self = nn(own_high, block) + nn(own_low, block)
        grad_near = tn(table_high, states[...]) + tn(table_low, states[...])
        grads[:width, :] = grad_self
        grads[width:, :] = grad_near
        squares[...] = jnp.zeros_like(squares)
        squares[:, :width] = grad_edge[...] + far_sum[SPAN:, :]
        squares[:, 256 : 256 + width] = 0.5 * grad_out[...]
        vectors[...] = jnp.zeros_like(vectors)
        ones = jnp.ones((16, rows), bf16)
        gain_high, gain_low = split(gain_sum[...])
        vectors[0:1, :width] = (nt(ones, own_high) + nt(ones, own_low))[:1]
        vectors[1:2, :width] = (nt(ones, gain_high) + nt(ones, gain_low))[:1]


def edge_layer(
    meta, states, ids, edges, cots, residue, neighbour, edge_weight, bias, out_weight, out_weight_t, gain, local_first
):
    group = group_of(edges.shape[0], EDGE_GROUP)
    width, rows = edges.shape[1:]
    model = states.shape[1]
    by_pair = pl.BlockSpec((group, width, rows), lambda i: (i, 0, 0))
    square = whole((width, width))
    return pl.pallas_call(
        functools.partial(edge_kernel, local_first),
        name="edge_layer",
        grid=(edges.shape[0] // group,),
        in_specs=[
            smem,
            whole(states.shape),
            whole(ids.shape),
            by_pair,
            by_pair,
            whole((width, model)),
            whole((width, model)),
            square,
            whole((width, 128)),
            square,
            square,
            whole((width, 128)),
        ],
        out_specs=[
            by_pair,
            by_pair,
            whole((SPAN, model)),
            whole((2 * width, model)),
            whole((width, model)),
            whole((8, model)),
        ],
        out_shape=[
            jax.ShapeDtypeStruct(edges.shape, bf16),
            jax.ShapeDtypeStruct(edges.shape, bf16),
            jax.ShapeDtypeStruct((SPAN, model), bf16),
            jax.ShapeDtypeStruct((2 * width, model), f32),
            jax.ShapeDtypeStruct((width, model), f32),
            jax.ShapeDtypeStruct((8, model), f32),
        ],
        scratch_shapes=[
            pltpu.VMEM((SPAN + 2 * REACH, 256), bf16),
            pltpu.VMEM((width, SPAN + width), bf16),
            pltpu.VMEM((rows // tile_of(rows), width, window_of(rows) + width), bf16),
            pltpu.VMEM((width, rows), f32),
            pltpu.VMEM((width, rows), f32),
            pltpu.VMEM((SPAN + width, width), f32),
            pltpu.VMEM((SPAN + 2 * REACH, width), f32),
            pltpu.VMEM((width, rows), f32),
            pltpu.VMEM((width, rows), f32),
            pltpu.VMEM((width, width), f32),
            pltpu.VMEM((width, width), f32),
        ],
        compiler_params=params(),
    )(
        meta,
        states,
        ids,
        edges,
        cots,
        residue.T,
        neighbour.T,
        edge_weight,
        bias,
        out_weight,
        out_weight_t,
        gain,
    )


def norm_back(unit, inv_std, gain, grad_out):
    grad_gain = jnp.sum(grad_out * unit, axis=0, keepdims=True)
    scaled = grad_out * gain
    grad_in = inv_std * (
        scaled
        - jnp.mean(scaled, -1, keepdims=True)
        - unit * jnp.mean(scaled * unit, -1, keepdims=True)
    )
    return grad_in, grad_gain


def node_backward_kernel(
    meta,
    own_cot,
    other_cot,
    mine,
    theirs,
    first,
    second,
    stats,
    ffn_input,
    act,
    slope,
    sums,
    gain_one,
    ffn_in,
    ffn_out,
    gain_two,
    out_weight,
    own_grad,
    spread,
    weights,
    message_out,
    vectors,
    sum_out,
    sum_in,
    sum_message,
):
    step = pl.program_id(0)
    chunk, model = first.shape
    hidden = act.shape[1]
    core = meta[4]
    half = own_cot.shape[0]

    @pl.when(step == 0)
    def _():
        vectors[...] = jnp.zeros_like(vectors)
        sum_out[...] = jnp.zeros_like(sum_out)
        sum_in[...] = jnp.zeros_like(sum_in)
        sum_message[...] = jnp.zeros_like(sum_message)

    if chunk > half:
        mine_first = core == 0
        lower = jnp.where(mine_first, own_cot[...], other_cot[...])
        cot = jnp.concatenate([lower, jnp.where(mine_first, other_cot[...], own_cot[...])], axis=0)
    else:
        row = step * chunk
        inside = pl.ds(pl.multiple_of(lax.rem(row, half), chunk), chunk)
        cot = jnp.where(row // half == core, own_cot[inside, :], other_cot[inside, :])
    total = cot.astype(f32) + (mine[...].astype(f32) + theirs[...].astype(f32))
    second_inv = stats[:, 2:3]
    first_inv = stats[:, 1:2]
    grad_second, gain_two_part = norm_back(second[...].astype(f32), second_inv, gain_two[...], total)
    top = grad_second.astype(bf16)
    grad_hidden = (nt(top, ffn_out[...]) * slope[...].astype(f32)).astype(bf16)
    out_columns = pl.ds(pl.multiple_of(core * (hidden // 2), 128), hidden // 2)
    in_columns = pl.ds(pl.multiple_of(core * (model // 2), 128), model // 2)
    sum_out[...] += tn(act[:, out_columns], top)
    sum_in[...] += tn(ffn_input[:, in_columns], grad_hidden)
    bias_part = jnp.sum(grad_hidden.astype(f32), axis=0, keepdims=True)
    grad_norm = grad_second + nt(grad_hidden, ffn_in[...])
    grad_first, gain_one_part = norm_back(first[...].astype(f32), first_inv, gain_one[...], grad_norm)
    store_own_rows(own_grad, grad_first, step, core)
    message_cot = (grad_first * stats[:, :1]).astype(bf16)
    spread[...] = (0.5 * nt(out_weight[...], message_cot)).astype(bf16)
    sum_message[...] += nn(sums[pl.ds(pl.multiple_of(core * (model // 2), 16), model // 2), :], message_cot)
    vectors[0:1, :] += gain_one_part
    vectors[1:2, :] += gain_two_part
    for part in range(hidden // model):
        vectors[2 + part : 3 + part, :] += bias_part[:, part * model : (part + 1) * model]

    @pl.when(step == pl.num_programs(0) - 1)
    def _():
        weights[: hidden // 2, :] = sum_out[...].astype(bf16)
        for part in range(hidden // model):
            start = hidden // 2 + part * (model // 2)
            weights[start : start + model // 2, :] = sum_in[
                :, part * model : (part + 1) * model
            ].astype(bf16)
        message_out[...] = sum_message[...]


def node_backward(
    meta,
    own_cot,
    other_cot,
    mine,
    theirs,
    first,
    second,
    stats,
    ffn_input,
    act,
    slope,
    sums,
    gain_one,
    ffn_in,
    ffn_out,
    gain_two,
    out_weight,
):
    rows, model = first.shape
    hidden = act.shape[1]
    chunk = min(rows, NODE_CHUNK)

    def by_rows(width):
        return pl.BlockSpec((chunk, width), lambda i: (i, 0))

    by_lanes = pl.BlockSpec((model, chunk), lambda i: (0, i))
    return pl.pallas_call(
        node_backward_kernel,
        name="node_backward",
        grid=(rows // chunk,),
        in_specs=[
            smem,
            whole(own_cot.shape),
            whole(other_cot.shape),
            by_rows(model),
            by_rows(model),
            by_rows(model),
            by_rows(model),
            by_rows(128),
            by_rows(model),
            by_rows(hidden),
            by_rows(hidden),
            by_lanes,
            whole((1, model)),
            whole(ffn_in.shape),
            whole(ffn_out.shape),
            whole((1, model)),
            whole(out_weight.shape),
        ],
        out_specs=[
            whole(own_cot.shape),
            by_lanes,
            whole((hidden, model)),
            whole((model // 2, model)),
            whole((8, model)),
        ],
        out_shape=[
            jax.ShapeDtypeStruct(own_cot.shape, f32),
            jax.ShapeDtypeStruct((model, rows), bf16),
            jax.ShapeDtypeStruct((hidden, model), bf16),
            jax.ShapeDtypeStruct((model // 2, model), f32),
            jax.ShapeDtypeStruct((8, model), f32),
        ],
        scratch_shapes=[
            pltpu.VMEM((hidden // 2, model), f32),
            pltpu.VMEM((model // 2, hidden), f32),
            pltpu.VMEM((model // 2, model), f32),
        ],
        compiler_params=params(),
    )(
        meta,
        own_cot,
        other_cot,
        mine,
        theirs,
        first,
        second,
        stats,
        ffn_input,
        act,
        slope,
        sums,
        gain_one[None],
        ffn_in,
        ffn_out,
        gain_two[None],
        out_weight,
    )


def message_backward_kernel(
    static_first,
    meta,
    table,
    spread,
    ids,
    edges,
    slope,
    receiver,
    neighbour,
    edge_grads,
    squares,
    message_out,
    edge_vectors,
    node_vectors,
    own_grad,
    keep,
    send,
    keep_weights,
    send_weights,
    far_sum,
    near_sum,
    own_sum,
    edge_sum,
    weights,
):
    step = pl.program_id(0)
    model, rows = spread.shape
    group, width = edges.shape[:2]
    half = keep.shape[0]
    window = window_of(rows)
    local_first = pl.multiple_of(meta[1], 128) if static_first is None else static_first

    @pl.when(step == 0)
    def _():
        for total in (far_sum, near_sum, own_sum, edge_sum):
            total[...] = jnp.zeros_like(total)

    near = [ids[pl.ds(group * step + k, 1), :] - meta[2] for k in range(group)]
    grads = [spread[...] * slope[k] for k in range(group)]
    own_sum[...] += sum(grad.astype(f32) for grad in grads)
    far_sum[...] += nt(
        beside([far_rows(near[k], edges[k]) for k in range(1, group, 2)]), beside(grads[1::2])
    )
    for tile, lanes in tiles(rows):
        first = local_first + lanes.start
        part = beside([near_rows(near[k][:, lanes], edges[k, :, lanes], first) for k in range(0, group, 2)])
        found = nt(part, beside([grad[:, lanes] for grad in grads[::2]]))
        near_sum[window_rows(local_first, rows, tile), :] += found[:window, :]
        edge_sum[...] += found[window:, :]

    @pl.when(step == pl.num_programs(0) - 1)
    def _():
        table_sum = (far_sum[:SPAN, :] + near_sum[REACH : REACH + SPAN, :]).astype(bf16)
        own_rows = own_sum[...].T
        own_low = own_rows.astype(bf16)
        nodes_t = table[...].T
        block_t = nodes_t
        if rows < SPAN:
            block_t = table[pl.ds(local_first, rows), :].T
        split_rows = keep_weights.shape[0]
        for core, start in enumerate((0, split_rows)):
            if core == 0:
                weights[:model, :] = nn(block_t, own_low)
                third = edge_sum[...] + far_sum[SPAN:, :]
            else:
                weights[start : start + model, :] = nn(nodes_t, table_sum)
                third = squares[...]
            start += model
            weights[start : start + width, :] = third
            start += width
            weights[start : start + width, :] = edge_grads[core * width : (core + 1) * width, :]
            start += width
            weights[start : start + model // 2, :] = jnp.where(meta[4] == core, message_out[...], 0.0)
            start += model // 2
            if core == 0:
                weights[start:split_rows, :] = jnp.zeros((split_rows - start, model), f32)
        weights[start : start + 8, :] = edge_vectors[...]
        weights[start + 8 : start + 16, :] = 0.5 * node_vectors[...]
        weights[start + 16 :, :] = jnp.broadcast_to(
            jnp.sum(own_rows, axis=0, keepdims=True), (2 * split_rows - start - 16, model)
        )
        mine = pl.multiple_of(meta[4] * split_rows, split_rows)
        keep_weights[...] = weights[pl.ds(mine, split_rows), :]
        send_weights[...] = weights[pl.ds(split_rows - mine, split_rows), :].astype(bf16)
        back = nt(table_sum, neighbour[...])
        own_back = nt(own_low, receiver[...])
        if rows == SPAN:
            far_sum[:SPAN, :] = back + own_back
        else:
            far_sum[:SPAN, :] = back
            far_sum[pl.ds(local_first, rows), :] += own_back
        high = meta[0]
        kept = far_sum[pl.ds(pl.multiple_of(high * half, half), half), :]
        keep[...] = kept + own_grad[...] if own_grad.shape[0] == half else kept
        send[...] = far_sum[pl.ds(pl.multiple_of((1 - high) * half, half), half), :].astype(bf16)


def message_backward(
    meta,
    table,
    spread,
    ids,
    edges,
    slope,
    receiver,
    neighbour,
    edge_grads,
    squares,
    message_out,
    edge_vectors,
    node_vectors,
    own_grad,
    local_first,
):
    group = group_of(edges.shape[0], MSG_GROUP)
    width, rows = edges.shape[1:]
    model = table.shape[1]
    square = whole((model, model))
    split_rows = -(-(model + 2 * width + model // 2 + 24) // 256) * 256
    return pl.pallas_call(
        functools.partial(message_backward_kernel, local_first),
        name="message_backward",
        grid=(edges.shape[0] // group,),
        in_specs=[
            smem,
            whole(table.shape),
            whole(spread.shape),
            whole(ids.shape),
            pl.BlockSpec((group, width, rows), lambda i: (i, 0, 0)),
            pl.BlockSpec((group, model, rows), lambda i: (i, 0, 0)),
            square,
            square,
            whole(edge_grads.shape),
            whole(squares.shape),
            whole(message_out.shape),
            whole(edge_vectors.shape),
            whole(node_vectors.shape),
            whole(own_grad.shape),
        ],
        out_specs=[
            whole((SPAN // 2, model)),
            whole((SPAN // 2, model)),
            whole((split_rows, model)),
            whole((split_rows, model)),
        ],
        out_shape=[
            jax.ShapeDtypeStruct((SPAN // 2, model), f32),
            jax.ShapeDtypeStruct((SPAN // 2, model), bf16),
            jax.ShapeDtypeStruct((split_rows, model), f32),
            jax.ShapeDtypeStruct((split_rows, model), bf16),
        ],
        scratch_shapes=[
            pltpu.VMEM((SPAN + width, model), f32),
            pltpu.VMEM((SPAN + 2 * REACH, model), f32),
            pltpu.VMEM((model, rows), f32),
            pltpu.VMEM((width, model), f32),
            pltpu.VMEM((2 * split_rows, model), f32),
        ],
        compiler_params=params(),
    )(
        meta,
        table,
        spread,
        ids,
        edges,
        slope,
        receiver,
        neighbour,
        edge_grads,
        squares,
        message_out,
        edge_vectors,
        node_vectors,
        own_grad,
    )


def edge_gradient_kernel(partial, slope, spread, edge_weight, *rest):
    out = rest[-1]
    for k in range(out.shape[0]):
        grad_value = spread[...] * slope[k]
        out[k] = partial[k].astype(f32) + nn(edge_weight[...], grad_value)


def edge_gradient(first, count, filled, partial, slope, spread, edge_weight):
    width, rows = partial.shape[1:]
    model = spread.shape[0]

    def pair(size):
        return pl.BlockSpec((2, size, rows), lambda i: (first + i, 0, 0))

    before = [] if filled is None else [filled]
    return pl.pallas_call(
        edge_gradient_kernel,
        name="edge_gradient",
        grid=(count,),
        in_specs=[pair(width), pair(model), whole(spread.shape), whole(edge_weight.shape)]
        + [pl.BlockSpec(memory_space=pl.ANY)] * len(before),
        out_specs=pair(width),
        out_shape=jax.ShapeDtypeStruct(partial.shape, f32),
        input_output_aliases={4: 0} if before else {},
        compiler_params=params(54),
    )(partial, slope, spread, edge_weight, *before)


def sum_to_slots_kernel(shift, meta, *refs):
    parts, outs, total = refs[:-5], refs[-5:-1], refs[-1]
    total[...] = parts[0][...].astype(f32)
    for part in parts[1:]:
        total[...] += part[...].astype(f32)
    place = meta[5] >> shift & 3
    rows = outs[0].shape[0]
    for slot, out in enumerate(outs):
        start = pl.multiple_of((place ^ slot) * rows, rows)
        out[...] = total[pl.ds(start, rows), :].astype(out.dtype)


def sum_to_slots(meta, shift, parts):
    rows, width = parts[0].shape
    out_types = (f32, bf16, bf16, bf16)
    return pl.pallas_call(
        functools.partial(sum_to_slots_kernel, shift),
        name="sum_to_slots",
        in_specs=[smem] + [whole(part.shape) for part in parts],
        out_specs=[whole((rows // 4, width))] * 4,
        out_shape=[jax.ShapeDtypeStruct((rows // 4, width), kind) for kind in out_types],
        scratch_shapes=[pltpu.VMEM((rows, width), f32)],
        compiler_params=params(12),
    )(meta, *parts)


def sum_parts_kernel(*refs):
    total = refs[0][...].astype(f32)
    for part in refs[1:-1]:
        total = total + part[...].astype(f32)
    refs[-1][...] = total.astype(bf16)


def sum_parts(parts):
    return pl.pallas_call(
        sum_parts_kernel,
        name="sum_parts",
        in_specs=[whole(part.shape) for part in parts],
        out_specs=whole(parts[0].shape),
        out_shape=jax.ShapeDtypeStruct(parts[0].shape, bf16),
        compiler_params=params(12),
    )(*parts)


def assemble_kernel(shift, meta, *refs):
    place = meta[5] >> shift & 3
    rows = refs[0].shape[0]
    for slot, part in enumerate(refs[:-1]):
        start = pl.multiple_of((place ^ slot) * rows, rows)
        refs[-1][pl.ds(start, rows), :] = part[...]


def assemble(meta, shift, parts):
    rows, width = parts[0].shape
    return pl.pallas_call(
        functools.partial(assemble_kernel, shift),
        name="assemble",
        in_specs=[smem] + [whole(part.shape) for part in parts],
        out_specs=whole((4 * rows, width)),
        out_shape=jax.ShapeDtypeStruct((4 * rows, width), bf16),
        compiler_params=params(12),
    )(meta, *parts)


def sent_each_way(shift, slots):
    return [moved(slot, place << shift) for place, slot in enumerate(slots) if place > 0]


def moved(value, mask):
    devices = lax.axis_size("res") * lax.axis_size("nbr")
    cores = lax.axis_size("nbr")
    pairs = [(source, source ^ (mask * cores)) for source in range(devices)]
    return lax.ppermute(value, ("res", "nbr"), pairs)


def unpack_early_kernel(side, meta, source, *rest):
    grad_out, grad_in, wide, out_sem, in_sem = rest[-5:]
    place = meta[4] if side == 0 else 1 - meta[4]
    model, hidden = grad_in.shape
    wide[...] = source[...].astype(f32)
    half, quarter = hidden // 2, model // 2
    copies = [
        pltpu.make_async_copy(
            wide.at[:half], grad_out.at[pl.ds(pl.multiple_of(place * half, half), half)], out_sem
        )
    ]
    for part in range(hidden // model):
        start = half + part * quarter
        copies.append(
            pltpu.make_async_copy(
                wide.at[start : start + quarter],
                grad_in.at[
                    pl.ds(pl.multiple_of(place * quarter, quarter), quarter),
                    part * model : (part + 1) * model,
                ],
                in_sem.at[part],
            )
        )
    for copy in copies:
        copy.start()
    for copy in copies:
        copy.wait()


def unpack_early(meta, side, source, before):
    rows, model = source.shape
    anywhere = pl.BlockSpec(memory_space=pl.ANY)
    return pl.pallas_call(
        functools.partial(unpack_early_kernel, side),
        name="unpack_early",
        in_specs=[smem, whole(source.shape)] + [anywhere] * len(before),
        out_specs=[anywhere, anywhere],
        out_shape=[
            jax.ShapeDtypeStruct((rows, model), f32),
            jax.ShapeDtypeStruct((model, rows), f32),
        ],
        scratch_shapes=[
            pltpu.VMEM((rows, model), f32),
            pltpu.SemaphoreType.DMA,
            pltpu.SemaphoreType.DMA((rows // model,)),
        ],
        input_output_aliases={2: 0, 3: 1} if before else {},
        compiler_params=params(),
    )(meta, source, *before)


def unpack_late_kernel(
    meta, own, other, grad_self, grad_near, grad_edge, edge_edge, edge_out, edge_self, edge_near, message_out, *vectors
):
    lower = meta[4] == 0
    model = own.shape[1]
    width = edge_edge.shape[0]
    first = jnp.where(lower, own[...], other[...]).astype(f32)
    second = jnp.where(lower, other[...], own[...]).astype(f32)
    grad_self[...] = first[:model, :]
    grad_near[...] = second[:model, :]
    start = model + width
    grad_edge[...] = first[model:start, :]
    edge_edge[...] = second[model:start, :width]
    edge_out[...] = second[model:start, 256 : 256 + width]
    edge_self[...] = first[start : start + width, :]
    edge_near[...] = second[start : start + width, :]
    start += width
    half = model // 2
    message_out[:half, :] = first[start : start + half, :]
    message_out[half:, :] = second[start : start + half, :]
    start += half
    edge_bias, gain_three, gain_one, gain_two, message_bias, ffn_bias = vectors
    edge_bias[...] = second[start : start + 1, :width]
    gain_three[...] = second[start + 1 : start + 2, :width]
    gain_one[...] = second[start + 8 : start + 9, :]
    gain_two[...] = second[start + 9 : start + 10, :]
    message_bias[...] = second[start + 16 : start + 17, :]
    for part in range(ffn_bias.shape[1] // model):
        row = start + 10 + part
        ffn_bias[:, part * model : (part + 1) * model] = second[row : row + 1, :]


def unpack_late(meta, own, other, width, hidden):
    model = own.shape[1]
    shapes = [(model, model)] * 2 + [(width, model)] + [(width, width)] * 2 + [(width, model)] * 2
    shapes += [(model, model)] + [(1, size) for size in (width, width, model, model, model, hidden)]
    return pl.pallas_call(
        unpack_late_kernel,
        name="unpack_late",
        in_specs=[smem, whole(own.shape), whole(other.shape)],
        out_specs=[whole(shape) for shape in shapes],
        out_shape=[jax.ShapeDtypeStruct(shape, f32) for shape in shapes],
        compiler_params=params(),
    )(meta, own, other)


def planes(size):
    return [[4 * block + place for place in range(4)] for block in range(size // 4)]


def columns(size):
    return [[4 * block + place for block in range(size // 4)] for place in range(4)]


def tied(*arrays):
    return lax.optimization_barrier(arrays)


def weight_sums(meta, early, kept, sent, kept_nodes, nodes, size, pieces):
    received = swapped(sent, 0)
    early = lax.psum(early, "res", axis_index_groups=columns(size))
    value, received, given = tied(pieces[0](None), received, swapped(nodes, 0))
    node_grad = kept_nodes + given.astype(f32)
    value, kept, *slots = tied(value, *sum_to_slots(meta, 0, [kept, received]))
    value, node_grad, *received = tied(pieces[1](value), node_grad, *sent_each_way(0, [kept, *slots]))
    value, kept, *slots = tied(value, *sum_to_slots(meta, 2, [kept, *received]))
    value, *received = tied(pieces[2](value), *sent_each_way(2, [kept, *slots]))
    value, early, late = tied(value, early, sum_parts([kept, *received]))
    early = lax.all_gather(early, "res", axis_index_groups=planes(size), tiled=True)
    value, *received = tied(pieces[3](value), *sent_each_way(2, [late] * 4))
    value, late = tied(value, assemble(meta, 2, [late, *received]))
    value, early, *received = tied(pieces[4](value), early, *sent_each_way(0, [late] * 4))
    return early, assemble(meta, 0, [late, *received]), value, node_grad


def joined(table, other, high_side):
    return jnp.where(
        high_side, jnp.concatenate([other, table], axis=0), jnp.concatenate([table, other], axis=0)
    )


def halves(table, high_side):
    half = table.shape[0] // 2
    lower, upper = (table[:half], table[half:])
    return (jnp.where(high_side, upper, lower), jnp.where(high_side, lower, upper))


def sum_blocks(table, device, level):
    keep, send = halves(table, device >> level & 1 == 1)
    return keep + swapped(send.astype(bf16), level).astype(keep.dtype)


def on_device(
    nodes,
    edges,
    neighbours,
    lengths,
    message_receiver_weight,
    message_neighbour_weight,
    message_edge_weight,
    message_hidden_bias,
    message_output_weight,
    gain_one,
    ffn_in,
    ffn_bias,
    ffn_out,
    gain_two,
    edge_update_residue_weight,
    edge_update_neighbour_weight,
    edge_update_edge_weight,
    edge_update_bias,
    edge_out,
    gain_three,
    node_cot,
    edge_cot,
):
    rows, half_k, edge_width = edges.shape
    own_rows, model = nodes.shape
    hidden = ffn_in.shape[1]
    levels = (SPAN // own_rows).bit_length() - 1
    core = lax.axis_index("nbr")
    device = lax.axis_index("res") * lax.axis_size("nbr") + core
    first_row = lax.axis_index("res") * rows
    bucket = first_row // SPAN
    group_start = bucket * SPAN
    local_first = 0 if rows == SPAN else None
    top = device >> (levels - 1) & 1
    meta = jnp.stack(
        [top, first_row - group_start, group_start, bucket, core, lax.axis_index("res"), 0, 0]
    ).astype(jnp.int32)

    ids = neighbours.T
    edges_t = edges.transpose(1, 2, 0)
    cot_t = edge_cot.transpose(1, 2, 0)

    table = nodes
    for level in range(levels - 1):
        table = joined(table, swapped(table, level), device >> level & 1 == 1)
    other_table = swapped(table, levels - 1)
    other_cot = swapped(node_cot, 0)

    node_table, slope, packed = message_forward(
        meta,
        lengths,
        table,
        other_table,
        ids,
        edges_t,
        message_receiver_weight,
        message_neighbour_weight,
        message_edge_weight,
        message_hidden_bias,
        local_first,
    )
    packed, *edge_parts = tied(
        packed,
        jnp.broadcast_to(edge_update_bias[:, None], (edge_width, 128)),
        edge_out * 0.5,
        edge_out.T * 0.5,
        jnp.broadcast_to(gain_three[:, None], (edge_width, 128)),
    )
    block = node_table
    if rows < SPAN:
        block = lax.dynamic_slice_in_dim(node_table, first_row - group_start, rows, 0)
    state, ffn_input, act, ffn_slope, first, second, stats, sums, node_out = node_forward(
        meta,
        block,
        packed,
        swapped(packed, 0),
        message_output_weight,
        gain_one,
        ffn_in,
        ffn_bias,
        ffn_out,
        gain_two,
    )
    states = state
    for level in range(1, levels):
        states = joined(states, swapped(states, level), device >> level & 1 == 1)
    new_edges, partial, back, edge_grads, squares, edge_vectors = edge_layer(
        meta,
        states,
        ids,
        edges_t,
        cot_t,
        edge_update_residue_weight,
        edge_update_neighbour_weight,
        edge_update_edge_weight,
        *edge_parts,
        local_first,
    )
    for level in reversed(range(1, levels)):
        back = sum_blocks(back, device, level)
    own_grad, spread, early, message_out, node_vectors = node_backward(
        meta,
        node_cot,
        other_cot,
        back,
        swapped(back, 0),
        first,
        second,
        stats,
        ffn_input,
        act,
        ffn_slope,
        sums,
        gain_one,
        ffn_in,
        ffn_out,
        gain_two,
        message_output_weight,
    )
    size = lax.axis_size("res")
    if size == 16:
        early = lax.psum_scatter(early, "res", axis_index_groups=planes(size), tiled=True)
    else:
        early = lax.psum(early.astype(f32), "res").astype(bf16)
    keep, send, kept_weights, sent_weights = message_backward(
        meta,
        node_table,
        spread,
        ids,
        edges_t,
        slope,
        message_receiver_weight,
        message_neighbour_weight,
        edge_grads,
        squares,
        message_out,
        edge_vectors,
        node_vectors,
        own_grad,
        local_first,
    )
    early, kept_weights, sent_weights = tied(early, kept_weights, sent_weights)
    counts = [1, 6, 1, 1, 6] if half_k == 30 else [half_k // 2]
    starts = [sum(counts[:index]) for index in range(len(counts))]

    def piece(start, count):
        return lambda filled: edge_gradient(
            start, count, filled, partial, slope, spread, message_edge_weight
        )

    spans = [piece(*span) for span in zip(starts, counts)]
    if size == 16:
        early, late, edge_grad, node_grad = weight_sums(
            meta, early, kept_weights, sent_weights, keep, send, size, spans
        )
    else:
        late = lax.psum(kept_weights + swapped(sent_weights, 0).astype(f32), "res").astype(bf16)
        edge_grad = None
        for span in spans:
            edge_grad = span(edge_grad)
        node_grad = keep + swapped(send, levels - 1).astype(f32)
        for level in reversed(range(levels - 1)):
            node_grad = sum_blocks(node_grad, device, level)
        if levels > 1:
            node_grad = own_grad + node_grad
    late_other = swapped(late, 0)
    early_other = swapped(early, 0)
    late_other, *halves_out = tied(late_other, *unpack_early(meta, 0, early, []))
    (
        grad_msg_self,
        grad_msg_nbr,
        grad_msg_edge,
        grad_edge_edge,
        grad_edge_out,
        grad_edge_self,
        grad_edge_nbr,
        grad_msg_out,
        grad_edge_bias,
        grad_gain_three,
        grad_gain_one,
        grad_gain_two,
        grad_msg_bias,
        grad_ffn_bias,
    ) = unpack_late(meta, late, late_other, edge_width, hidden)
    grad_msg_out, early_other = tied(grad_msg_out, early_other)
    grad_ffn_out, grad_ffn_in = unpack_early(meta, 1, early_other, halves_out)
    return (
        node_out,
        new_edges.transpose(2, 0, 1),
        node_grad,
        edge_grad.transpose(2, 0, 1),
        grad_msg_self,
        grad_msg_nbr,
        grad_msg_edge,
        grad_msg_bias[0],
        grad_msg_out,
        grad_gain_one[0],
        grad_ffn_in,
        grad_ffn_bias[0],
        grad_ffn_out,
        grad_gain_two[0],
        grad_edge_self.T,
        grad_edge_nbr.T,
        grad_edge_edge,
        grad_edge_bias[0],
        grad_edge_out,
        grad_gain_three[0],
    )


def solution(mesh):
    rows = P(("res", "nbr"), None)
    pairs = P("res", "nbr", None)
    placed = (rows, pairs, P("res", "nbr")) + (P(),) * 17 + (rows, pairs)
    return jax.shard_map(
        on_device,
        mesh=mesh,
        in_specs=placed,
        out_specs=(rows, pairs, rows, pairs) + (P(),) * 16,
        check_vma=False,
    )
```

```python
import functools

import jax
import jax.numpy as jnp
from jax import lax
from jax.experimental import pallas as pl
from jax.experimental.pallas import tpu as pltpu
from jax.sharding import PartitionSpec as P

SPAN = 1024
REACH = 32
MASKED = -16384.0
FORWARD_GROUP = 6
EDGE_GROUP = 6
MSG_GROUP = 6
FORWARD_CHUNK = 512
NODE_CHUNK = 256

epsilon = 1e-05
root_half = 0.7071067811865476
inv_root_two_pi = 0.3989422804014327
half_log2_e = 0.7213475204444817
two_over_root_pi = 1.1283791670955126

bf16 = jnp.bfloat16
f32 = jnp.float32


def swapped(value, level):
    mask = 2**level
    devices = lax.axis_size("res") * lax.axis_size("nbr")
    pairs = [(source, source ^ mask) for source in range(devices)]
    return lax.ppermute(value, ("res", "nbr"), pairs)


def nn(left_op, right_op):
    return jnp.dot(left_op, right_op, preferred_element_type=f32)


def nt(left_op, right_op):
    return lax.dot_general(
        left_op, right_op, (((1,), (1,)), ((), ())), preferred_element_type=f32
    )


def tn(left_op, right_op):
    return lax.dot_general(
        left_op, right_op, (((0,), (0,)), ((), ())), preferred_element_type=f32
    )


def split(values):
    high = values.astype(bf16)
    return high, (values - high.astype(f32)).astype(bf16)


def twice_gelu_and_slope(values):
    below = 1.0 + lax.erf(values * root_half)
    density = jnp.exp2(values * values * -half_log2_e)
    return values * below, below + values * density * (2.0 * inv_root_two_pi)


def scaled_gelu_and_slope(values):
    below = 1.0 + lax.erf(values)
    low = values.astype(bf16)
    density = jnp.exp2(low * low * bf16(-2.0 * half_log2_e))
    return values * below, below.astype(bf16) + low * density * bf16(two_over_root_pi)


def selector(rows, ids):
    places = lax.broadcasted_iota(jnp.int16, (rows, ids.shape[1]), 0)
    return jnp.where(places == ids.astype(jnp.int16), bf16(1), bf16(0))


def group_of(count, wanted):
    return wanted if count % wanted == 0 else 2


def tile_of(rows):
    return min(rows, 256)


def window_of(rows):
    return tile_of(rows) + 2 * REACH


def far_rows(ids, edge):
    return jnp.concatenate([selector(SPAN, ids), edge], axis=0)


def near_rows(ids, edge, first):
    return jnp.concatenate([selector(ids.shape[1] + 2 * REACH, ids - (first - REACH)), edge], axis=0)


def beside(parts):
    return parts[0] if len(parts) == 1 else jnp.concatenate(parts, axis=1)


def tiles(rows):
    width = tile_of(rows)
    return [(tile, slice(tile * width, (tile + 1) * width)) for tile in range(rows // width)]


def window_rows(local_first, rows, tile):
    start = local_first + tile * tile_of(rows)
    if not isinstance(start, int):
        start = pl.multiple_of(start, 128)
    return pl.ds(start, window_of(rows))


def repeat_lanes(column, width):
    return jnp.concatenate([column] * (width // column.shape[1]), axis=1)


def whole(shape):
    return pl.BlockSpec(shape, lambda *_: (0,) * len(shape))


def params(mebibytes=60):
    return pltpu.CompilerParams(vmem_limit_bytes=mebibytes * 2**20)


smem = pl.BlockSpec(memory_space=pltpu.SMEM)


def message_forward_kernel(
    static_first,
    meta,
    lengths,
    own,
    other,
    ids,
    edges,
    receiver,
    neighbour,
    edge_weight,
    bias,
    table,
    slope,
    packed,
    padded,
    far_table,
    near_table,
    base,
    sums,
    counts,
):
    step = pl.program_id(0)
    rows = base.shape[1]
    half = own.shape[0]
    length = lengths[meta[3]]
    local_first = pl.multiple_of(meta[1], 128) if static_first is None else static_first

    @pl.when(step == 0)
    def _():
        high = meta[0]
        table[pl.ds(pl.multiple_of(high * half, half), half), :] = own[...]
        table[pl.ds(pl.multiple_of((1 - high) * half, half), half), :] = other[...]
        places = lax.broadcasted_iota(jnp.int32, (SPAN, 1), 0)
        hidden = jnp.where(places < length, 0.0, MASKED)
        projected = (root_half * nn(table[...], neighbour[...]) + hidden).astype(bf16)
        scaled_weight = (root_half * edge_weight[...].astype(f32)).astype(bf16)
        far_table[...] = jnp.concatenate([projected, scaled_weight], axis=0).T
        padded[...] = jnp.zeros_like(padded)
        padded[REACH : REACH + SPAN, :] = projected
        for tile, _ in tiles(rows):
            window = padded[window_rows(local_first, rows, tile), :]
            near_table[tile] = jnp.concatenate([window, scaled_weight], axis=0).T
        block = table[pl.ds(local_first, rows), :]
        places = lax.broadcasted_iota(jnp.int32, (rows, 1), 0) + local_first
        hidden = jnp.where(places < length, 0.0, MASKED)
        base[...] = (root_half * (nn(block, receiver[...]) + bias[...]) + hidden).T
        sums[...] = jnp.zeros_like(sums)
        counts[...] = jnp.zeros_like(counts)

    positions = lax.broadcasted_iota(jnp.int32, (1, rows), 1) + local_first
    group = edges.shape[0]
    near = [ids[pl.ds(group * step + k, 1), :] - meta[2] for k in range(group)]
    counts[...] += jnp.where(positions < length, 1.0, 0.0) * sum(
        jnp.where(place < length, 1.0, 0.0) for place in near
    )
    for tile, lanes in tiles(rows):
        for k in range(0, group, 2):
            near_part = near_rows(near[k][:, lanes], edges[k, :, lanes], local_first + lanes.start)
            far_part = far_rows(near[k + 1][:, lanes], edges[k + 1, :, lanes])
            far_value = nn(far_table[...], far_part)
            near_value = nn(near_table[tile], near_part)
            far_act, far_slope = scaled_gelu_and_slope(far_value + base[:, lanes])
            slope[k + 1, :, lanes] = far_slope
            near_act, near_slope = scaled_gelu_and_slope(near_value + base[:, lanes])
            slope[k, :, lanes] = near_slope
            sums[:, lanes] += far_act + near_act

    @pl.when(step == pl.num_programs(0) - 1)
    def _():
        width = sums.shape[0]
        packed[:width, :] = (root_half * sums[...]).astype(bf16)
        packed[width:, :] = jnp.broadcast_to(counts[...], (16, rows)).astype(bf16)


def message_forward(meta, lengths, own, other, ids, edges, receiver, neighbour, edge_weight, bias, local_first):
    columns_in = edges.shape[0]
    group = group_of(columns_in, FORWARD_GROUP)
    width, rows = edges.shape[1:]
    model = own.shape[1]
    return pl.pallas_call(
        functools.partial(message_forward_kernel, local_first),
        name="message_forward",
        grid=(columns_in // group,),
        in_specs=[
            smem,
            smem,
            whole(own.shape),
            whole(other.shape),
            whole(ids.shape),
            pl.BlockSpec((group, width, rows), lambda i: (i, 0, 0)),
            whole(receiver.shape),
            whole(neighbour.shape),
            whole(edge_weight.shape),
            whole((1, model)),
        ],
        out_specs=[
            whole((SPAN, model)),
            pl.BlockSpec((group, model, rows), lambda i: (i, 0, 0)),
            whole((model + 16, rows)),
        ],
        out_shape=[
            jax.ShapeDtypeStruct((SPAN, model), bf16),
            jax.ShapeDtypeStruct((columns_in, model, rows), bf16),
            jax.ShapeDtypeStruct((model + 16, rows), bf16),
        ],
        scratch_shapes=[
            pltpu.VMEM((SPAN + 2 * REACH, model), bf16),
            pltpu.VMEM((model, SPAN + width), bf16),
            pltpu.VMEM((rows // tile_of(rows), model, window_of(rows) + width), bf16),
            pltpu.VMEM((model, rows), f32),
            pltpu.VMEM((model, rows), f32),
            pltpu.VMEM((1, rows), f32),
        ],
        compiler_params=params(),
    )(meta, lengths, own, other, ids, edges, receiver, neighbour, edge_weight, bias[None])


def normed(values):
    mean_val = jnp.mean(values, -1, keepdims=True)
    centered = values - mean_val
    inv_std = lax.rsqrt(jnp.mean(centered * centered, -1, keepdims=True) + epsilon)
    return centered * inv_std, inv_std


def node_forward_kernel(
    meta,
    nodes,
    mine,
    theirs,
    out_weight,
    gain_one,
    ffn_in,
    ffn_bias,
    ffn_out,
    gain_two,
    state,
    ffn_input,
    act,
    slope,
    first,
    second,
    stats,
    sums,
    own_state,
    in_here,
    out_here,
    sems,
):
    step = pl.program_id(0)
    rows, width = nodes.shape
    fetches = [
        pltpu.make_async_copy(there, here, sems.at[place])
        for place, (there, here) in enumerate(((ffn_in, in_here), (ffn_out, out_here)))
    ]

    @pl.when(step == 0)
    def _():
        for fetch in fetches:
            fetch.start()

    total = mine[...].astype(f32) + theirs[...].astype(f32)
    count = jnp.maximum(total[width : width + 1, :], 1.0)
    ratio = 1.0 / jnp.broadcast_to(count, (128, rows)).T
    high, low = split(total[:width, :])
    sums[...] = high
    message = tn(high, out_weight[...]) + tn(low, out_weight[...])
    first_sum = nodes[...].astype(f32) + message * repeat_lanes(ratio, width)
    first_unit, first_inv = normed(first_sum)
    first[...] = first_unit.astype(bf16)
    first_norm = first_unit * gain_one[...]
    low = first_norm.astype(bf16)
    ffn_input[...] = own_columns(low, meta[4])

    @pl.when(step == 0)
    def _():
        for fetch in fetches:
            fetch.wait()

    hidden, grad = twice_gelu_and_slope(nn(low, in_here[...]) + ffn_bias[...])
    hidden = (0.5 * hidden).astype(bf16)
    act[...] = own_columns(hidden, meta[4])
    slope[...] = (0.5 * grad).astype(bf16)
    second_unit, second_inv = normed(first_norm + nn(hidden, out_here[...]))
    second[...] = second_unit.astype(bf16)
    out = (second_unit * gain_two[...]).astype(bf16)
    state[...] = out
    store_own_rows(own_state, out, step, meta[4])
    lane = lax.broadcasted_iota(jnp.int32, ratio.shape, 1)
    stats[...] = jnp.where(lane == 0, ratio, jnp.where(lane == 1, first_inv, second_inv))


def own_columns(values, core):
    half = values.shape[1] // 2
    return jnp.where(core == 0, values[:, :half], values[:, half:])


def store_own_rows(own, values, step, core):
    half, chunk = own.shape[0], values.shape[0]
    if chunk > half:
        own[...] = jnp.where(core == 0, values[:half, :], values[half:, :])
        return
    place = step * chunk

    @pl.when(place // half == core)
    def _():
        own[pl.ds(pl.multiple_of(lax.rem(place, half), chunk), chunk), :] = values


def node_forward(meta, nodes, mine, theirs, out_weight, gain_one, ffn_in, ffn_bias, ffn_out, gain_two):
    rows, model = nodes.shape
    hidden = ffn_in.shape[1]
    chunk = min(rows, FORWARD_CHUNK)

    def by_rows(width):
        return pl.BlockSpec((chunk, width), lambda i: (i, 0))

    return pl.pallas_call(
        node_forward_kernel,
        name="node_forward",
        grid=(rows // chunk,),
        in_specs=[
            smem,
            by_rows(model),
            pl.BlockSpec((model + 16, chunk), lambda i: (0, i)),
            pl.BlockSpec((model + 16, chunk), lambda i: (0, i)),
            whole(out_weight.shape),
            whole((1, model)),
            pl.BlockSpec(memory_space=pl.ANY),
            whole((1, hidden)),
            pl.BlockSpec(memory_space=pl.ANY),
            whole((1, model)),
        ],
        out_specs=[
            by_rows(model),
            by_rows(model // 2),
            by_rows(hidden // 2),
            by_rows(hidden),
            by_rows(model),
            by_rows(model),
            by_rows(128),
            pl.BlockSpec((model, chunk), lambda i: (0, i)),
            whole((rows // 2, model)),
        ],
        out_shape=[
            jax.ShapeDtypeStruct((rows, model), bf16),
            jax.ShapeDtypeStruct((rows, model // 2), bf16),
            jax.ShapeDtypeStruct((rows, hidden // 2), bf16),
            jax.ShapeDtypeStruct((rows, hidden), bf16),
            jax.ShapeDtypeStruct((rows, model), bf16),
            jax.ShapeDtypeStruct((rows, model), bf16),
            jax.ShapeDtypeStruct((rows, 128), f32),
            jax.ShapeDtypeStruct((model, rows), bf16),
            jax.ShapeDtypeStruct((rows // 2, model), bf16),
        ],
        scratch_shapes=[
            pltpu.VMEM(ffn_in.shape, bf16),
            pltpu.VMEM(ffn_out.shape, bf16),
            pltpu.SemaphoreType.DMA((2,)),
        ],
        compiler_params=params(),
    )(
        meta, nodes, mine, theirs, out_weight, gain_one[None], ffn_in, ffn_bias[None], ffn_out, gain_two[None]
    )


def edge_kernel(
    static_first,
    meta,
    states,
    ids,
    edges,
    cots,
    residue_t,
    neighbour_t,
    edge_weight,
    bias,
    out_weight,
    out_weight_t,
    gain,
    new_edges,
    partial,
    back_table,
    grads,
    squares,
    vectors,
    padded,
    far_table,
    near_table,
    base,
    gains,
    far_sum,
    near_sum,
    own_sum,
    gain_sum,
    grad_edge,
    grad_out,
):
    step = pl.program_id(0)
    width, rows = base.shape
    window = window_of(rows)
    local_first = pl.multiple_of(meta[1], 128) if static_first is None else static_first

    @pl.when(step == 0)
    def _():
        fill = jnp.zeros((width, 256 - width), bf16)
        weight = jnp.concatenate([edge_weight[...], fill], axis=1)
        projected = nt(states[...], neighbour_t[...]).astype(bf16)
        projected = jnp.concatenate([projected, jnp.zeros((SPAN, 256 - width), bf16)], axis=1)
        far_table[...] = jnp.concatenate([projected, weight], axis=0).T[:width, :]
        padded[...] = jnp.zeros_like(padded)
        padded[REACH : REACH + SPAN, :] = projected
        for tile, _ in tiles(rows):
            part = padded[window_rows(local_first, rows, tile), :]
            near_table[tile] = jnp.concatenate([part, weight], axis=0).T[:width, :]
        block = states[pl.ds(local_first, rows), :]
        base[...] = nt(residue_t[...], block) + repeat_lanes(bias[...], rows)
        gains[...] = repeat_lanes(gain[...], rows)
        for total in (far_sum, near_sum, own_sum, gain_sum, grad_edge, grad_out):
            total[...] = jnp.zeros_like(total)

    group = edges.shape[0]
    order = list(range(1, group, 2)) + list(range(0, group, 2))
    found_rows, found_grads = {}, {}
    for side in order:
        near = ids[pl.ds(group * step + side, 1), :] - meta[2]
        edge = edges[side]
        if side % 2 == 0:
            chosen = [
                near_rows(near[:, lanes], edges[side, :, lanes], local_first + lanes.start)
                for _, lanes in tiles(rows)
            ]
            value = jnp.concatenate(
                [nn(near_table[tile], part) for tile, part in enumerate(chosen)], axis=1
            )
        else:
            chosen = far_rows(near, edge)
            value = nn(far_table[...], chosen)
        act, slope = twice_gelu_and_slope(value + base[...])
        act = act.astype(bf16)
        third = edge.astype(f32) + nn(out_weight_t[...], act)
        centered = third - jnp.mean(third, 0, keepdims=True)
        inv_std = lax.rsqrt(jnp.mean(centered * centered, 0, keepdims=True) + epsilon)
        unit = centered * inv_std
        new_edges[side] = (unit * gains[...]).astype(bf16)
        cot = cots[side].astype(f32)
        gain_sum[...] += cot * unit
        scaled = cot * gains[...]
        grad_third = inv_std * (
            scaled
            - jnp.mean(scaled, 0, keepdims=True)
            - unit * jnp.mean(scaled * unit, 0, keepdims=True)
        )
        branch = grad_third.astype(bf16)
        grad_out[...] += nt(act, branch)
        grad_wide = nn(out_weight[...], branch) * slope
        own_sum[...] += grad_wide
        grad_value = grad_wide.astype(bf16)
        partial[side, :width, :] = branch
        partial[side, width:, :] = grad_value
        found_rows[side], found_grads[side] = chosen, grad_value
        if side == order[group // 2 - 1]:
            far_sum[...] += nt(
                beside([found_rows[k] for k in order[: group // 2]]),
                beside([found_grads[k] for k in order[: group // 2]]),
            )
    for tile, lanes in tiles(rows):
        found = nt(
            beside([found_rows[k][tile] for k in range(0, group, 2)]),
            beside([found_grads[k][:, lanes] for k in range(0, group, 2)]),
        )
        near_sum[window_rows(local_first, rows, tile), :] += found[:window, :]
        grad_edge[...] += found[window:, :]

    @pl.when(step == pl.num_programs(0) - 1)
    def _():
        table_high, table_low = split(far_sum[:SPAN, :] + near_sum[REACH : REACH + SPAN, :])
        own_high, own_low = split(own_sum[...])
        back = nn(table_high, neighbour_t[...]) + nn(table_low, neighbour_t[...])
        own_back = tn(own_high, residue_t[...]) + tn(own_low, residue_t[...])
        if rows == SPAN:
            back_table[...] = (back + own_back).astype(bf16)
        else:
            own_rows = pl.ds(local_first, rows)
            back_table[...] = back.astype(bf16)
            back_table[own_rows, :] = (back_table[own_rows, :].astype(f32) + own_back).astype(bf16)
        block = states[pl.ds(local_first, rows), :]
        grad_self = nn(own_high, block) + nn(own_low, block)
        grad_near = tn(table_high, states[...]) + tn(table_low, states[...])
        grads[:width, :] = grad_self
        grads[width:, :] = grad_near
        squares[...] = jnp.zeros_like(squares)
        squares[:, :width] = grad_edge[...] + far_sum[SPAN:, :]
        squares[:, 256 : 256 + width] = 0.5 * grad_out[...]
        vectors[...] = jnp.zeros_like(vectors)
        ones = jnp.ones((16, rows), bf16)
        gain_high, gain_low = split(gain_sum[...])
        vectors[0:1, :width] = (nt(ones, own_high) + nt(ones, own_low))[:1]
        vectors[1:2, :width] = (nt(ones, gain_high) + nt(ones, gain_low))[:1]


def edge_layer(
    meta, states, ids, edges, cots, residue, neighbour, edge_weight, bias, out_weight, out_weight_t, gain, local_first
):
    group = group_of(edges.shape[0], EDGE_GROUP)
    width, rows = edges.shape[1:]
    model = states.shape[1]
    by_pair = pl.BlockSpec((group, width, rows), lambda i: (i, 0, 0))
    square = whole((width, width))
    return pl.pallas_call(
        functools.partial(edge_kernel, local_first),
        name="edge_layer",
        grid=(edges.shape[0] // group,),
        in_specs=[
            smem,
            whole(states.shape),
            whole(ids.shape),
            by_pair,
            by_pair,
            whole((width, model)),
            whole((width, model)),
            square,
            whole((width, 128)),
            square,
            square,
            whole((width, 128)),
        ],
        out_specs=[
            by_pair,
            pl.BlockSpec((group, 2 * width, rows), lambda i: (i, 0, 0)),
            whole((SPAN, model)),
            whole((2 * width, model)),
            whole((width, model)),
            whole((8, model)),
        ],
        out_shape=[
            jax.ShapeDtypeStruct(edges.shape, bf16),
            jax.ShapeDtypeStruct((edges.shape[0], 2 * width, rows), bf16),
            jax.ShapeDtypeStruct((SPAN, model), bf16),
            jax.ShapeDtypeStruct((2 * width, model), f32),
            jax.ShapeDtypeStruct((width, model), f32),
            jax.ShapeDtypeStruct((8, model), f32),
        ],
        scratch_shapes=[
            pltpu.VMEM((SPAN + 2 * REACH, 256), bf16),
            pltpu.VMEM((width, SPAN + width), bf16),
            pltpu.VMEM((rows // tile_of(rows), width, window_of(rows) + width), bf16),
            pltpu.VMEM((width, rows), f32),
            pltpu.VMEM((width, rows), f32),
            pltpu.VMEM((SPAN + width, width), f32),
            pltpu.VMEM((SPAN + 2 * REACH, width), f32),
            pltpu.VMEM((width, rows), f32),
            pltpu.VMEM((width, rows), f32),
            pltpu.VMEM((width, width), f32),
            pltpu.VMEM((width, width), f32),
        ],
        compiler_params=params(),
    )(
        meta,
        states,
        ids,
        edges,
        cots,
        residue.T,
        neighbour.T,
        edge_weight,
        bias,
        out_weight,
        out_weight_t,
        gain,
    )


def norm_back(unit, inv_std, gain, grad_out):
    grad_gain = jnp.sum(grad_out * unit, axis=0, keepdims=True)
    scaled = grad_out * gain
    grad_in = inv_std * (
        scaled
        - jnp.mean(scaled, -1, keepdims=True)
        - unit * jnp.mean(scaled * unit, -1, keepdims=True)
    )
    return grad_in, grad_gain


def node_backward_kernel(
    meta,
    own_cot,
    other_cot,
    mine,
    theirs,
    first,
    second,
    stats,
    ffn_input,
    act,
    slope,
    sums,
    gain_one,
    ffn_in,
    ffn_out,
    gain_two,
    out_weight,
    own_grad,
    spread,
    weights,
    message_out,
    vectors,
    sum_out,
    sum_in,
    sum_message,
):
    step = pl.program_id(0)
    chunk, model = first.shape
    hidden = slope.shape[1]
    core = meta[4]
    half = own_cot.shape[0]

    @pl.when(step == 0)
    def _():
        vectors[...] = jnp.zeros_like(vectors)
        sum_out[...] = jnp.zeros_like(sum_out)
        sum_in[...] = jnp.zeros_like(sum_in)
        sum_message[...] = jnp.zeros_like(sum_message)

    if chunk > half:
        mine_first = core == 0
        lower = jnp.where(mine_first, own_cot[...], other_cot[...])
        cot = jnp.concatenate([lower, jnp.where(mine_first, other_cot[...], own_cot[...])], axis=0)
    else:
        row = step * chunk
        inside = pl.ds(pl.multiple_of(lax.rem(row, half), chunk), chunk)
        cot = jnp.where(row // half == core, own_cot[inside, :], other_cot[inside, :])
    total = cot.astype(f32) + (mine[...].astype(f32) + theirs[...].astype(f32))
    second_inv = stats[:, 2:3]
    first_inv = stats[:, 1:2]
    grad_second, gain_two_part = norm_back(second[...].astype(f32), second_inv, gain_two[...], total)
    top = grad_second.astype(bf16)
    grad_hidden = (nt(top, ffn_out[...]) * slope[...].astype(f32)).astype(bf16)
    sum_out[...] += tn(act[...], top)
    sum_in[...] += tn(ffn_input[...], grad_hidden)
    bias_part = jnp.sum(grad_hidden.astype(f32), axis=0, keepdims=True)
    grad_norm = grad_second + nt(grad_hidden, ffn_in[...])
    grad_first, gain_one_part = norm_back(first[...].astype(f32), first_inv, gain_one[...], grad_norm)
    store_own_rows(own_grad, grad_first, step, core)
    message_cot = (grad_first * stats[:, :1]).astype(bf16)
    spread[...] = (0.5 * nt(out_weight[...], message_cot)).astype(bf16)
    sum_message[...] += nn(sums[pl.ds(pl.multiple_of(core * (model // 2), 16), model // 2), :], message_cot)
    vectors[0:1, :] += gain_one_part
    vectors[1:2, :] += gain_two_part
    for part in range(hidden // model):
        vectors[2 + part : 3 + part, :] += bias_part[:, part * model : (part + 1) * model]

    @pl.when(step == pl.num_programs(0) - 1)
    def _():
        weights[: hidden // 2, :] = sum_out[...].astype(bf16)
        for part in range(hidden // model):
            start = hidden // 2 + part * (model // 2)
            weights[start : start + model // 2, :] = sum_in[
                :, part * model : (part + 1) * model
            ].astype(bf16)
        message_out[...] = sum_message[...]


def node_backward(
    meta,
    own_cot,
    other_cot,
    mine,
    theirs,
    first,
    second,
    stats,
    ffn_input,
    act,
    slope,
    sums,
    gain_one,
    ffn_in,
    ffn_out,
    gain_two,
    out_weight,
):
    rows, model = first.shape
    hidden = slope.shape[1]
    chunk = min(rows, NODE_CHUNK)

    def by_rows(width):
        return pl.BlockSpec((chunk, width), lambda i: (i, 0))

    by_lanes = pl.BlockSpec((model, chunk), lambda i: (0, i))
    return pl.pallas_call(
        node_backward_kernel,
        name="node_backward",
        grid=(rows // chunk,),
        in_specs=[
            smem,
            whole(own_cot.shape),
            whole(other_cot.shape),
            by_rows(model),
            by_rows(model),
            by_rows(model),
            by_rows(model),
            by_rows(128),
            by_rows(model // 2),
            by_rows(hidden // 2),
            by_rows(hidden),
            by_lanes,
            whole((1, model)),
            whole(ffn_in.shape),
            whole(ffn_out.shape),
            whole((1, model)),
            whole(out_weight.shape),
        ],
        out_specs=[
            whole(own_cot.shape),
            by_lanes,
            whole((hidden, model)),
            whole((model // 2, model)),
            whole((8, model)),
        ],
        out_shape=[
            jax.ShapeDtypeStruct(own_cot.shape, f32),
            jax.ShapeDtypeStruct((model, rows), bf16),
            jax.ShapeDtypeStruct((hidden, model), bf16),
            jax.ShapeDtypeStruct((model // 2, model), f32),
            jax.ShapeDtypeStruct((8, model), f32),
        ],
        scratch_shapes=[
            pltpu.VMEM((hidden // 2, model), f32),
            pltpu.VMEM((model // 2, hidden), f32),
            pltpu.VMEM((model // 2, model), f32),
        ],
        compiler_params=params(),
    )(
        meta,
        own_cot,
        other_cot,
        mine,
        theirs,
        first,
        second,
        stats,
        ffn_input,
        act,
        slope,
        sums,
        gain_one[None],
        ffn_in,
        ffn_out,
        gain_two[None],
        out_weight,
    )


def message_backward_kernel(
    static_first,
    meta,
    table,
    spread,
    ids,
    edges,
    slope,
    receiver,
    neighbour,
    edge_grads,
    squares,
    message_out,
    edge_vectors,
    node_vectors,
    own_grad,
    keep,
    send,
    keep_weights,
    send_weights,
    far_sum,
    near_sum,
    own_sum,
    edge_sum,
    weights,
    table_here,
    receiver_here,
    neighbour_here,
    edge_grads_here,
    squares_here,
    message_out_here,
    own_grad_here,
    sems,
):
    step = pl.program_id(0)
    model, rows = spread.shape
    group, width = edges.shape[:2]
    half = keep.shape[0]
    window = window_of(rows)
    local_first = pl.multiple_of(meta[1], 128) if static_first is None else static_first

    at_the_end = (
        (table, table_here),
        (receiver, receiver_here),
        (neighbour, neighbour_here),
        (edge_grads, edge_grads_here),
        (squares, squares_here),
        (message_out, message_out_here),
        (own_grad, own_grad_here),
    )
    fetches = [
        pltpu.make_async_copy(there, here, sems.at[place]) for place, (there, here) in enumerate(at_the_end)
    ]

    @pl.when(step == 0)
    def _():
        for fetch in fetches:
            fetch.start()
        for total in (far_sum, near_sum, own_sum, edge_sum):
            total[...] = jnp.zeros_like(total)

    near = [ids[pl.ds(group * step + k, 1), :] - meta[2] for k in range(group)]
    grads = [spread[...] * slope[k] for k in range(group)]
    own_sum[...] += sum(grad.astype(f32) for grad in grads)
    far_sum[...] += nt(
        beside([far_rows(near[k], edges[k]) for k in range(1, group, 2)]), beside(grads[1::2])
    )
    for tile, lanes in tiles(rows):
        first = local_first + lanes.start
        part = beside([near_rows(near[k][:, lanes], edges[k, :, lanes], first) for k in range(0, group, 2)])
        found = nt(part, beside([grad[:, lanes] for grad in grads[::2]]))
        near_sum[window_rows(local_first, rows, tile), :] += found[:window, :]
        edge_sum[...] += found[window:, :]

    @pl.when(step == pl.num_programs(0) - 1)
    def _():
        for fetch in fetches:
            fetch.wait()
        table_sum = (far_sum[:SPAN, :] + near_sum[REACH : REACH + SPAN, :]).astype(bf16)
        own_rows = own_sum[...].T
        own_low = own_rows.astype(bf16)
        nodes_t = table_here[...].T
        block_t = nodes_t
        if rows < SPAN:
            block_t = table_here[pl.ds(local_first, rows), :].T
        split_rows = keep_weights.shape[0]
        for core, start in enumerate((0, split_rows)):
            if core == 0:
                weights[:model, :] = nn(block_t, own_low)
                third = edge_sum[...] + far_sum[SPAN:, :]
            else:
                weights[start : start + model, :] = nn(nodes_t, table_sum)
                third = squares_here[...]
            start += model
            weights[start : start + width, :] = third
            start += width
            weights[start : start + width, :] = edge_grads_here[core * width : (core + 1) * width, :]
            start += width
            weights[start : start + model // 2, :] = jnp.where(meta[4] == core, message_out_here[...], 0.0)
            start += model // 2
            if core == 0:
                weights[start:split_rows, :] = jnp.zeros((split_rows - start, model), f32)
        weights[start : start + 8, :] = edge_vectors[...]
        weights[start + 8 : start + 16, :] = 0.5 * node_vectors[...]
        weights[start + 16 :, :] = jnp.broadcast_to(
            jnp.sum(own_rows, axis=0, keepdims=True), (2 * split_rows - start - 16, model)
        )
        mine = pl.multiple_of(meta[4] * split_rows, split_rows)
        keep_weights[...] = weights[pl.ds(mine, split_rows), :]
        send_weights[...] = weights[pl.ds(split_rows - mine, split_rows), :].astype(bf16)
        back = nt(table_sum, neighbour_here[...])
        own_back = nt(own_low, receiver_here[...])
        if rows == SPAN:
            far_sum[:SPAN, :] = back + own_back
        else:
            far_sum[:SPAN, :] = back
            far_sum[pl.ds(local_first, rows), :] += own_back
        high = meta[0]
        kept = far_sum[pl.ds(pl.multiple_of(high * half, half), half), :]
        keep[...] = kept + own_grad_here[...] if own_grad_here.shape[0] == half else kept
        send[...] = far_sum[pl.ds(pl.multiple_of((1 - high) * half, half), half), :].astype(bf16)


def message_backward(
    meta,
    table,
    spread,
    ids,
    edges,
    slope,
    receiver,
    neighbour,
    edge_grads,
    squares,
    message_out,
    edge_vectors,
    node_vectors,
    own_grad,
    local_first,
):
    group = group_of(edges.shape[0], MSG_GROUP)
    width, rows = edges.shape[1:]
    model = table.shape[1]
    anywhere = pl.BlockSpec(memory_space=pl.ANY)
    late = (table, receiver, neighbour, edge_grads, squares, message_out, own_grad)
    split_rows = -(-(model + 2 * width + model // 2 + 24) // 256) * 256
    return pl.pallas_call(
        functools.partial(message_backward_kernel, local_first),
        name="message_backward",
        grid=(edges.shape[0] // group,),
        in_specs=[
            smem,
            anywhere,
            whole(spread.shape),
            whole(ids.shape),
            pl.BlockSpec((group, width, rows), lambda i: (i, 0, 0)),
            pl.BlockSpec((group, model, rows), lambda i: (i, 0, 0)),
            anywhere,
            anywhere,
            anywhere,
            anywhere,
            anywhere,
            whole(edge_vectors.shape),
            whole(node_vectors.shape),
            anywhere,
        ],
        out_specs=[
            whole((SPAN // 2, model)),
            whole((SPAN // 2, model)),
            whole((split_rows, model)),
            whole((split_rows, model)),
        ],
        out_shape=[
            jax.ShapeDtypeStruct((SPAN // 2, model), f32),
            jax.ShapeDtypeStruct((SPAN // 2, model), bf16),
            jax.ShapeDtypeStruct((split_rows, model), f32),
            jax.ShapeDtypeStruct((split_rows, model), bf16),
        ],
        scratch_shapes=[
            pltpu.VMEM((SPAN + width, model), f32),
            pltpu.VMEM((SPAN + 2 * REACH, model), f32),
            pltpu.VMEM((model, rows), f32),
            pltpu.VMEM((width, model), f32),
            pltpu.VMEM((2 * split_rows, model), f32),
        ]
        + [pltpu.VMEM(value.shape, value.dtype) for value in late]
        + [pltpu.SemaphoreType.DMA((len(late),))],
        compiler_params=params(),
    )(
        meta,
        table,
        spread,
        ids,
        edges,
        slope,
        receiver,
        neighbour,
        edge_grads,
        squares,
        message_out,
        edge_vectors,
        node_vectors,
        own_grad,
    )


def edge_gradient_kernel(partial, slope, spread, message_weight, edge_weight, *rest):
    out = rest[-1]
    width = out.shape[1]
    weights = jnp.concatenate([message_weight[...], edge_weight[...]], axis=1)
    for k in range(out.shape[0]):
        grads = jnp.concatenate([spread[...] * slope[k], partial[k, width:, :]], axis=0)
        out[k] = partial[k, :width, :].astype(f32) + nn(weights, grads)


def edge_gradient(first, count, filled, partial, slope, spread, message_weight, edge_weight):
    columns_in, width, rows = partial.shape
    width //= 2
    model = spread.shape[0]

    def pair(size):
        return pl.BlockSpec((2, size, rows), lambda i: (first + i, 0, 0))

    before = [] if filled is None else [filled]
    return pl.pallas_call(
        edge_gradient_kernel,
        name="edge_gradient",
        grid=(count,),
        in_specs=[
            pair(2 * width),
            pair(model),
            whole(spread.shape),
            whole(message_weight.shape),
            whole(edge_weight.shape),
        ]
        + [pl.BlockSpec(memory_space=pl.ANY)] * len(before),
        out_specs=pair(width),
        out_shape=jax.ShapeDtypeStruct((columns_in, width, rows), f32),
        input_output_aliases={5: 0} if before else {},
        compiler_params=params(54),
    )(partial, slope, spread, message_weight, edge_weight, *before)


def sum_to_slots_kernel(shift, meta, *refs):
    parts, outs, total = refs[:-5], refs[-5:-1], refs[-1]
    total[...] = parts[0][...].astype(f32)
    for part in parts[1:]:
        total[...] += part[...].astype(f32)
    place = meta[5] >> shift & 3
    rows = outs[0].shape[0]
    for slot, out in enumerate(outs):
        start = pl.multiple_of((place ^ slot) * rows, rows)
        out[...] = total[pl.ds(start, rows), :].astype(out.dtype)


def sum_to_slots(meta, shift, parts):
    rows, width = parts[0].shape
    out_types = (f32, bf16, bf16, bf16)
    return pl.pallas_call(
        functools.partial(sum_to_slots_kernel, shift),
        name="sum_to_slots",
        in_specs=[smem] + [whole(part.shape) for part in parts],
        out_specs=[whole((rows // 4, width))] * 4,
        out_shape=[jax.ShapeDtypeStruct((rows // 4, width), kind) for kind in out_types],
        scratch_shapes=[pltpu.VMEM((rows, width), f32)],
        compiler_params=params(12),
    )(meta, *parts)


def sum_parts_kernel(*refs):
    total = refs[0][...].astype(f32)
    for part in refs[1:-1]:
        total = total + part[...].astype(f32)
    refs[-1][...] = total.astype(bf16)


def sum_parts(parts):
    return pl.pallas_call(
        sum_parts_kernel,
        name="sum_parts",
        in_specs=[whole(part.shape) for part in parts],
        out_specs=whole(parts[0].shape),
        out_shape=jax.ShapeDtypeStruct(parts[0].shape, bf16),
        compiler_params=params(12),
    )(*parts)


def assemble_kernel(shift, meta, *refs):
    place = meta[5] >> shift & 3
    rows = refs[0].shape[0]
    for slot, part in enumerate(refs[:-1]):
        start = pl.multiple_of((place ^ slot) * rows, rows)
        refs[-1][pl.ds(start, rows), :] = part[...]


def assemble(meta, shift, parts):
    rows, width = parts[0].shape
    return pl.pallas_call(
        functools.partial(assemble_kernel, shift),
        name="assemble",
        in_specs=[smem] + [whole(part.shape) for part in parts],
        out_specs=whole((4 * rows, width)),
        out_shape=jax.ShapeDtypeStruct((4 * rows, width), bf16),
        compiler_params=params(12),
    )(meta, *parts)


def sent_each_way(shift, slots):
    return [moved(slot, place << shift) for place, slot in enumerate(slots) if place > 0]


def moved(value, mask):
    devices = lax.axis_size("res") * lax.axis_size("nbr")
    cores = lax.axis_size("nbr")
    pairs = [(source, source ^ (mask * cores)) for source in range(devices)]
    return lax.ppermute(value, ("res", "nbr"), pairs)


def unpack_early_kernel(side, meta, source, *rest):
    grad_out, grad_in, wide, out_sem, in_sem = rest[-5:]
    place = meta[4] if side == 0 else 1 - meta[4]
    model, hidden = grad_in.shape
    wide[...] = source[...].astype(f32)
    half, quarter = hidden // 2, model // 2
    copies = [
        pltpu.make_async_copy(
            wide.at[:half], grad_out.at[pl.ds(pl.multiple_of(place * half, half), half)], out_sem
        )
    ]
    for part in range(hidden // model):
        start = half + part * quarter
        copies.append(
            pltpu.make_async_copy(
                wide.at[start : start + quarter],
                grad_in.at[
                    pl.ds(pl.multiple_of(place * quarter, quarter), quarter),
                    part * model : (part + 1) * model,
                ],
                in_sem.at[part],
            )
        )
    for copy in copies:
        copy.start()
    for copy in copies:
        copy.wait()


def unpack_early(meta, side, source, before):
    rows, model = source.shape
    anywhere = pl.BlockSpec(memory_space=pl.ANY)
    return pl.pallas_call(
        functools.partial(unpack_early_kernel, side),
        name="unpack_early",
        in_specs=[smem, whole(source.shape)] + [anywhere] * len(before),
        out_specs=[anywhere, anywhere],
        out_shape=[
            jax.ShapeDtypeStruct((rows, model), f32),
            jax.ShapeDtypeStruct((model, rows), f32),
        ],
        scratch_shapes=[
            pltpu.VMEM((rows, model), f32),
            pltpu.SemaphoreType.DMA,
            pltpu.SemaphoreType.DMA((rows // model,)),
        ],
        input_output_aliases={2: 0, 3: 1} if before else {},
        compiler_params=params(),
    )(meta, source, *before)


def unpack_late_kernel(
    meta, own, other, grad_self, grad_near, grad_edge, edge_edge, edge_out, edge_self, edge_near, message_out, *vectors
):
    lower = meta[4] == 0
    model = own.shape[1]
    width = edge_edge.shape[0]
    first = jnp.where(lower, own[...], other[...]).astype(f32)
    second = jnp.where(lower, other[...], own[...]).astype(f32)
    grad_self[...] = first[:model, :]
    grad_near[...] = second[:model, :]
    start = model + width
    grad_edge[...] = first[model:start, :]
    edge_edge[...] = second[model:start, :width]
    edge_out[...] = second[model:start, 256 : 256 + width]
    edge_self[...] = first[start : start + width, :]
    edge_near[...] = second[start : start + width, :]
    start += width
    half = model // 2
    message_out[:half, :] = first[start : start + half, :]
    message_out[half:, :] = second[start : start + half, :]
    start += half
    edge_bias, gain_three, gain_one, gain_two, message_bias, ffn_bias = vectors
    edge_bias[...] = second[start : start + 1, :width]
    gain_three[...] = second[start + 1 : start + 2, :width]
    gain_one[...] = second[start + 8 : start + 9, :]
    gain_two[...] = second[start + 9 : start + 10, :]
    message_bias[...] = second[start + 16 : start + 17, :]
    for part in range(ffn_bias.shape[1] // model):
        row = start + 10 + part
        ffn_bias[:, part * model : (part + 1) * model] = second[row : row + 1, :]


def unpack_late(meta, own, other, width, hidden):
    model = own.shape[1]
    shapes = [(model, model)] * 2 + [(width, model)] + [(width, width)] * 2 + [(width, model)] * 2
    shapes += [(model, model)] + [(1, size) for size in (width, width, model, model, model, hidden)]
    return pl.pallas_call(
        unpack_late_kernel,
        name="unpack_late",
        in_specs=[smem, whole(own.shape), whole(other.shape)],
        out_specs=[whole(shape) for shape in shapes],
        out_shape=[jax.ShapeDtypeStruct(shape, f32) for shape in shapes],
        compiler_params=params(),
    )(meta, own, other)


def planes(size):
    return [[4 * block + place for place in range(4)] for block in range(size // 4)]


def columns(size):
    return [[4 * block + place for block in range(size // 4)] for place in range(4)]


def tied(*arrays):
    return lax.optimization_barrier(arrays)


def weight_sums(meta, early, kept, sent, kept_nodes, nodes, size, pieces):
    received = swapped(sent, 0)
    early = lax.psum(early, "res", axis_index_groups=columns(size))
    value, received, given = tied(pieces[0](None), received, swapped(nodes, 0))
    node_grad = kept_nodes + given.astype(f32)
    value, kept, *slots = tied(value, *sum_to_slots(meta, 0, [kept, received]))
    value, node_grad, *received = tied(pieces[1](value), node_grad, *sent_each_way(0, [kept, *slots]))
    value, kept, *slots = tied(value, *sum_to_slots(meta, 2, [kept, *received]))
    value, *received = tied(pieces[2](value), *sent_each_way(2, [kept, *slots]))
    value, early, late = tied(value, early, sum_parts([kept, *received]))
    early = lax.all_gather(early, "res", axis_index_groups=planes(size), tiled=True)
    value, *received = tied(pieces[3](value), *sent_each_way(2, [late] * 4))
    value, late = tied(value, assemble(meta, 2, [late, *received]))
    value, early, *received = tied(pieces[4](value), early, *sent_each_way(0, [late] * 4))
    return early, assemble(meta, 0, [late, *received]), value, node_grad


def joined(table, other, high_side):
    return jnp.where(
        high_side, jnp.concatenate([other, table], axis=0), jnp.concatenate([table, other], axis=0)
    )


def halves(table, high_side):
    half = table.shape[0] // 2
    lower, upper = (table[:half], table[half:])
    return (jnp.where(high_side, upper, lower), jnp.where(high_side, lower, upper))


def sum_blocks(table, device, level):
    keep, send = halves(table, device >> level & 1 == 1)
    return keep + swapped(send.astype(bf16), level).astype(keep.dtype)


def on_device(
    nodes,
    edges,
    neighbours,
    lengths,
    message_receiver_weight,
    message_neighbour_weight,
    message_edge_weight,
    message_hidden_bias,
    message_output_weight,
    gain_one,
    ffn_in,
    ffn_bias,
    ffn_out,
    gain_two,
    edge_update_residue_weight,
    edge_update_neighbour_weight,
    edge_update_edge_weight,
    edge_update_bias,
    edge_out,
    gain_three,
    node_cot,
    edge_cot,
):
    rows, half_k, edge_width = edges.shape
    own_rows, model = nodes.shape
    hidden = ffn_in.shape[1]
    levels = (SPAN // own_rows).bit_length() - 1
    core = lax.axis_index("nbr")
    device = lax.axis_index("res") * lax.axis_size("nbr") + core
    first_row = lax.axis_index("res") * rows
    bucket = first_row // SPAN
    group_start = bucket * SPAN
    local_first = 0 if rows == SPAN else None
    top = device >> (levels - 1) & 1
    meta = jnp.stack(
        [top, first_row - group_start, group_start, bucket, core, lax.axis_index("res"), 0, 0]
    ).astype(jnp.int32)

    ids = neighbours.T
    edges_t = edges.transpose(1, 2, 0)
    cot_t = edge_cot.transpose(1, 2, 0)

    table = nodes
    for level in range(levels - 1):
        table = joined(table, swapped(table, level), device >> level & 1 == 1)
    other_table = swapped(table, levels - 1)
    other_cot = swapped(node_cot, 0)

    node_table, slope, packed = message_forward(
        meta,
        lengths,
        table,
        other_table,
        ids,
        edges_t,
        message_receiver_weight,
        message_neighbour_weight,
        message_edge_weight,
        message_hidden_bias,
        local_first,
    )
    packed, *edge_parts = tied(
        packed,
        jnp.broadcast_to(edge_update_bias[:, None], (edge_width, 128)),
        edge_out * 0.5,
        edge_out.T * 0.5,
        jnp.broadcast_to(gain_three[:, None], (edge_width, 128)),
    )
    block = node_table
    if rows < SPAN:
        block = lax.dynamic_slice_in_dim(node_table, first_row - group_start, rows, 0)
    state, ffn_input, act, ffn_slope, first, second, stats, sums, node_out = node_forward(
        meta,
        block,
        packed,
        swapped(packed, 0),
        message_output_weight,
        gain_one,
        ffn_in,
        ffn_bias,
        ffn_out,
        gain_two,
    )
    states = state
    for level in range(1, levels):
        states = joined(states, swapped(states, level), device >> level & 1 == 1)
    new_edges, partial, back, edge_grads, squares, edge_vectors = edge_layer(
        meta,
        states,
        ids,
        edges_t,
        cot_t,
        edge_update_residue_weight,
        edge_update_neighbour_weight,
        edge_update_edge_weight,
        *edge_parts,
        local_first,
    )
    for level in reversed(range(1, levels)):
        back = sum_blocks(back, device, level)
    own_grad, spread, early, message_out, node_vectors = node_backward(
        meta,
        node_cot,
        other_cot,
        back,
        swapped(back, 0),
        first,
        second,
        stats,
        ffn_input,
        act,
        ffn_slope,
        sums,
        gain_one,
        ffn_in,
        ffn_out,
        gain_two,
        message_output_weight,
    )
    size = lax.axis_size("res")
    if size == 16:
        early = lax.psum_scatter(early, "res", axis_index_groups=planes(size), tiled=True)
    else:
        early = lax.psum(early.astype(f32), "res").astype(bf16)
    keep, send, kept_weights, sent_weights = message_backward(
        meta,
        node_table,
        spread,
        ids,
        edges_t,
        slope,
        message_receiver_weight,
        message_neighbour_weight,
        edge_grads,
        squares,
        message_out,
        edge_vectors,
        node_vectors,
        own_grad,
        local_first,
    )
    early, kept_weights, sent_weights = tied(early, kept_weights, sent_weights)
    counts = [1, 6, 1, 1, 6] if half_k == 30 else [half_k // 2]
    starts = [sum(counts[:index]) for index in range(len(counts))]

    def piece(start, count):
        return lambda filled: edge_gradient(
            start, count, filled, partial, slope, spread, message_edge_weight, edge_update_edge_weight
        )

    spans = [piece(*span) for span in zip(starts, counts)]
    if size == 16:
        early, late, edge_grad, node_grad = weight_sums(
            meta, early, kept_weights, sent_weights, keep, send, size, spans
        )
    else:
        late = lax.psum(kept_weights + swapped(sent_weights, 0).astype(f32), "res").astype(bf16)
        edge_grad = None
        for span in spans:
            edge_grad = span(edge_grad)
        node_grad = keep + swapped(send, levels - 1).astype(f32)
        for level in reversed(range(levels - 1)):
            node_grad = sum_blocks(node_grad, device, level)
        if levels > 1:
            node_grad = own_grad + node_grad
    late_other = swapped(late, 0)
    early_other = swapped(early, 0)
    late_other, *halves_out = tied(late_other, *unpack_early(meta, 0, early, []))
    (
        grad_msg_self,
        grad_msg_nbr,
        grad_msg_edge,
        grad_edge_edge,
        grad_edge_out,
        grad_edge_self,
        grad_edge_nbr,
        grad_msg_out,
        grad_edge_bias,
        grad_gain_three,
        grad_gain_one,
        grad_gain_two,
        grad_msg_bias,
        grad_ffn_bias,
    ) = unpack_late(meta, late, late_other, edge_width, hidden)
    grad_msg_out, early_other = tied(grad_msg_out, early_other)
    grad_ffn_out, grad_ffn_in = unpack_early(meta, 1, early_other, halves_out)
    return (
        node_out,
        new_edges.transpose(2, 0, 1),
        node_grad,
        edge_grad.transpose(2, 0, 1),
        grad_msg_self,
        grad_msg_nbr,
        grad_msg_edge,
        grad_msg_bias[0],
        grad_msg_out,
        grad_gain_one[0],
        grad_ffn_in,
        grad_ffn_bias[0],
        grad_ffn_out,
        grad_gain_two[0],
        grad_edge_self.T,
        grad_edge_nbr.T,
        grad_edge_edge,
        grad_edge_bias[0],
        grad_edge_out,
        grad_gain_three[0],
    )


def solution(mesh):
    rows = P(("res", "nbr"), None)
    pairs = P("res", "nbr", None)
    placed = (rows, pairs, P("res", "nbr")) + (P(),) * 17 + (rows, pairs)
    return jax.shard_map(
        on_device,
        mesh=mesh,
        in_specs=placed,
        out_specs=(rows, pairs, rows, pairs) + (P(),) * 16,
        check_vma=False,
    )
```

```python
import functools

import jax
import jax.numpy as jnp
from jax import lax
from jax.experimental import pallas as pl
from jax.experimental.pallas import tpu as pltpu
from jax.sharding import PartitionSpec as P

SPAN = 1024
REACH = 32
MASKED = -16384.0
FORWARD_GROUP = 6
EDGE_GROUP = 6
MSG_GROUP = 6
FORWARD_CHUNK = 512
NODE_CHUNK = 256

epsilon = 1e-05
root_half = 0.7071067811865476
inv_root_two_pi = 0.3989422804014327
half_log2_e = 0.7213475204444817
two_over_root_pi = 1.1283791670955126

bf16 = jnp.bfloat16
f32 = jnp.float32


def swapped(value, level):
    mask = 2**level
    devices = lax.axis_size("res") * lax.axis_size("nbr")
    pairs = [(source, source ^ mask) for source in range(devices)]
    return lax.ppermute(value, ("res", "nbr"), pairs)


def nn(left_op, right_op):
    return jnp.dot(left_op, right_op, preferred_element_type=f32)


def nt(left_op, right_op):
    return lax.dot_general(
        left_op, right_op, (((1,), (1,)), ((), ())), preferred_element_type=f32
    )


def tn(left_op, right_op):
    return lax.dot_general(
        left_op, right_op, (((0,), (0,)), ((), ())), preferred_element_type=f32
    )


def split(values):
    high = values.astype(bf16)
    return high, (values - high.astype(f32)).astype(bf16)


def twice_gelu_and_slope(values):
    below = 1.0 + lax.erf(values * root_half)
    density = jnp.exp2(values * values * -half_log2_e)
    return values * below, below + values * density * (2.0 * inv_root_two_pi)


def wide_gelu_and_slope(values):
    below = 1.0 + lax.erf(values)
    density = jnp.exp2(values * values * (-2.0 * half_log2_e))
    return values * below, below + values * density * two_over_root_pi


def scaled_gelu_and_slope(values):
    below = 1.0 + lax.erf(values)
    low = values.astype(bf16)
    density = jnp.exp2(low * low * bf16(-2.0 * half_log2_e))
    return values * below, below.astype(bf16) + low * density * bf16(two_over_root_pi)


def selector(rows, ids):
    places = lax.broadcasted_iota(jnp.int16, (rows, ids.shape[1]), 0)
    return jnp.where(places == ids.astype(jnp.int16), bf16(1), bf16(0))


def group_of(count, wanted):
    return wanted if count % wanted == 0 else 2


def tile_of(rows):
    return min(rows, 256)


def window_of(rows):
    return tile_of(rows) + 2 * REACH


def far_rows(ids, edge):
    return jnp.concatenate([selector(SPAN, ids), edge], axis=0)


def near_rows(ids, edge, first):
    return jnp.concatenate([selector(ids.shape[1] + 2 * REACH, ids - (first - REACH)), edge], axis=0)


def beside(parts):
    return parts[0] if len(parts) == 1 else jnp.concatenate(parts, axis=1)


def tiles(rows):
    width = tile_of(rows)
    return [(tile, slice(tile * width, (tile + 1) * width)) for tile in range(rows // width)]


def window_rows(local_first, rows, tile):
    start = local_first + tile * tile_of(rows)
    if not isinstance(start, int):
        start = pl.multiple_of(start, 128)
    return pl.ds(start, window_of(rows))


def repeat_lanes(column, width):
    return jnp.concatenate([column] * (width // column.shape[1]), axis=1)


def whole(shape):
    return pl.BlockSpec(shape, lambda *_: (0,) * len(shape))


def params(mebibytes=60):
    return pltpu.CompilerParams(vmem_limit_bytes=mebibytes * 2**20)


smem = pl.BlockSpec(memory_space=pltpu.SMEM)


def message_forward_kernel(
    static_first,
    meta,
    lengths,
    own,
    other,
    ids,
    edges,
    receiver,
    neighbour,
    edge_weight,
    bias,
    table,
    slope,
    packed,
    padded,
    far_table,
    near_table,
    base,
    sums,
    counts,
):
    step = pl.program_id(0)
    rows = base.shape[1]
    half = own.shape[0]
    length = lengths[meta[3]]
    local_first = pl.multiple_of(meta[1], 128) if static_first is None else static_first

    @pl.when(step == 0)
    def _():
        high = meta[0]
        table[pl.ds(pl.multiple_of(high * half, half), half), :] = own[...]
        table[pl.ds(pl.multiple_of((1 - high) * half, half), half), :] = other[...]
        places = lax.broadcasted_iota(jnp.int32, (SPAN, 1), 0)
        hidden = jnp.where(places < length, 0.0, MASKED)
        projected = (root_half * nn(table[...], neighbour[...]) + hidden).astype(bf16)
        scaled_weight = (root_half * edge_weight[...].astype(f32)).astype(bf16)
        far_table[...] = jnp.concatenate([projected, scaled_weight], axis=0).T
        padded[...] = jnp.zeros_like(padded)
        padded[REACH : REACH + SPAN, :] = projected
        for tile, _ in tiles(rows):
            window = padded[window_rows(local_first, rows, tile), :]
            near_table[tile] = jnp.concatenate([window, scaled_weight], axis=0).T
        block = table[pl.ds(local_first, rows), :]
        places = lax.broadcasted_iota(jnp.int32, (rows, 1), 0) + local_first
        hidden = jnp.where(places < length, 0.0, MASKED)
        base[...] = (root_half * (nn(block, receiver[...]) + bias[...]) + hidden).T
        sums[...] = jnp.zeros_like(sums)
        counts[...] = jnp.zeros_like(counts)

    positions = lax.broadcasted_iota(jnp.int32, (1, rows), 1) + local_first
    group = edges.shape[0]
    near = [ids[pl.ds(group * step + k, 1), :] - meta[2] for k in range(group)]
    counts[...] += jnp.where(positions < length, 1.0, 0.0) * sum(
        jnp.where(place < length, 1.0, 0.0) for place in near
    )
    for tile, lanes in tiles(rows):
        for k in range(0, group, 2):
            near_part = near_rows(near[k][:, lanes], edges[k, :, lanes], local_first + lanes.start)
            far_part = far_rows(near[k + 1][:, lanes], edges[k + 1, :, lanes])
            far_value = nn(far_table[...], far_part)
            near_value = nn(near_table[tile], near_part)
            far_act, far_slope = scaled_gelu_and_slope(far_value + base[:, lanes])
            slope[k + 1, :, lanes] = far_slope
            near_act, near_slope = scaled_gelu_and_slope(near_value + base[:, lanes])
            slope[k, :, lanes] = near_slope
            sums[:, lanes] += far_act + near_act

    @pl.when(step == pl.num_programs(0) - 1)
    def _():
        width = sums.shape[0]
        packed[:width, :] = (root_half * sums[...]).astype(bf16)
        packed[width:, :] = jnp.broadcast_to(counts[...], (16, rows)).astype(bf16)


def message_forward(meta, lengths, own, other, ids, edges, receiver, neighbour, edge_weight, bias, local_first):
    columns_in = edges.shape[0]
    group = group_of(columns_in, FORWARD_GROUP)
    width, rows = edges.shape[1:]
    model = own.shape[1]
    return pl.pallas_call(
        functools.partial(message_forward_kernel, local_first),
        name="message_forward",
        grid=(columns_in // group,),
        in_specs=[
            smem,
            smem,
            whole(own.shape),
            whole(other.shape),
            whole(ids.shape),
            pl.BlockSpec((group, width, rows), lambda i: (i, 0, 0)),
            whole(receiver.shape),
            whole(neighbour.shape),
            whole(edge_weight.shape),
            whole((1, model)),
        ],
        out_specs=[
            whole((SPAN, model)),
            pl.BlockSpec((group, model, rows), lambda i: (i, 0, 0)),
            whole((model + 16, rows)),
        ],
        out_shape=[
            jax.ShapeDtypeStruct((SPAN, model), bf16),
            jax.ShapeDtypeStruct((columns_in, model, rows), bf16),
            jax.ShapeDtypeStruct((model + 16, rows), bf16),
        ],
        scratch_shapes=[
            pltpu.VMEM((SPAN + 2 * REACH, model), bf16),
            pltpu.VMEM((model, SPAN + width), bf16),
            pltpu.VMEM((rows // tile_of(rows), model, window_of(rows) + width), bf16),
            pltpu.VMEM((model, rows), f32),
            pltpu.VMEM((model, rows), f32),
            pltpu.VMEM((1, rows), f32),
        ],
        compiler_params=params(63),
    )(meta, lengths, own, other, ids, edges, receiver, neighbour, edge_weight, bias[None])


def normed(values):
    mean_val = jnp.mean(values, -1, keepdims=True)
    centered = values - mean_val
    inv_std = lax.rsqrt(jnp.mean(centered * centered, -1, keepdims=True) + epsilon)
    return centered * inv_std, inv_std


def node_forward_kernel(
    meta,
    nodes,
    mine,
    theirs,
    out_weight,
    gain_one,
    ffn_in,
    ffn_bias,
    ffn_out,
    gain_two,
    state,
    ffn_input,
    act,
    slope,
    first,
    second,
    stats,
    sums,
    own_state,
    in_here,
    out_here,
    sems,
):
    step = pl.program_id(0)
    rows, width = nodes.shape
    fetches = [
        pltpu.make_async_copy(there, here, sems.at[place])
        for place, (there, here) in enumerate(((ffn_in, in_here), (ffn_out, out_here)))
    ]

    @pl.when(step == 0)
    def _():
        for fetch in fetches:
            fetch.start()

    total = mine[...].astype(f32) + theirs[...].astype(f32)
    count = jnp.maximum(total[width : width + 1, :], 1.0)
    ratio = 1.0 / jnp.broadcast_to(count, (128, rows)).T
    high, low = split(total[:width, :])
    sums[...] = high
    message = tn(high, out_weight[...]) + tn(low, out_weight[...])
    first_sum = nodes[...].astype(f32) + message * repeat_lanes(ratio, width)
    first_unit, first_inv = normed(first_sum)
    first[...] = first_unit.astype(bf16)
    first_norm = first_unit * gain_one[...]
    low = first_norm.astype(bf16)
    ffn_input[...] = own_columns(low, meta[4])

    @pl.when(step == 0)
    def _():
        for fetch in fetches:
            fetch.wait()

    hidden, grad = twice_gelu_and_slope(nn(low, in_here[...]) + ffn_bias[...])
    hidden = (0.5 * hidden).astype(bf16)
    act[...] = own_columns(hidden, meta[4])
    slope[...] = (0.5 * grad).astype(bf16)
    second_unit, second_inv = normed(first_norm + nn(hidden, out_here[...]))
    second[...] = second_unit.astype(bf16)
    out = (second_unit * gain_two[...]).astype(bf16)
    state[...] = out
    store_own_rows(own_state, out, step, meta[4])
    lane = lax.broadcasted_iota(jnp.int32, ratio.shape, 1)
    stats[...] = jnp.where(lane == 0, ratio, jnp.where(lane == 1, first_inv, second_inv))


def own_columns(values, core):
    half = values.shape[1] // 2
    return jnp.where(core == 0, values[:, :half], values[:, half:])


def store_own_rows(own, values, step, core):
    half, chunk = own.shape[0], values.shape[0]
    if chunk > half:
        own[...] = jnp.where(core == 0, values[:half, :], values[half:, :])
        return
    place = step * chunk

    @pl.when(place // half == core)
    def _():
        own[pl.ds(pl.multiple_of(lax.rem(place, half), chunk), chunk), :] = values


def node_forward(meta, nodes, mine, theirs, out_weight, gain_one, ffn_in, ffn_bias, ffn_out, gain_two):
    rows, model = nodes.shape
    hidden = ffn_in.shape[1]
    chunk = min(rows, FORWARD_CHUNK)

    def by_rows(width):
        return pl.BlockSpec((chunk, width), lambda i: (i, 0))

    return pl.pallas_call(
        node_forward_kernel,
        name="node_forward",
        grid=(rows // chunk,),
        in_specs=[
            smem,
            by_rows(model),
            pl.BlockSpec((model + 16, chunk), lambda i: (0, i)),
            pl.BlockSpec((model + 16, chunk), lambda i: (0, i)),
            whole(out_weight.shape),
            whole((1, model)),
            pl.BlockSpec(memory_space=pl.ANY),
            whole((1, hidden)),
            pl.BlockSpec(memory_space=pl.ANY),
            whole((1, model)),
        ],
        out_specs=[
            by_rows(model),
            by_rows(model // 2),
            by_rows(hidden // 2),
            by_rows(hidden),
            by_rows(model),
            by_rows(model),
            by_rows(128),
            pl.BlockSpec((model, chunk), lambda i: (0, i)),
            whole((rows // 2, model)),
        ],
        out_shape=[
            jax.ShapeDtypeStruct((rows, model), bf16),
            jax.ShapeDtypeStruct((rows, model // 2), bf16),
            jax.ShapeDtypeStruct((rows, hidden // 2), bf16),
            jax.ShapeDtypeStruct((rows, hidden), bf16),
            jax.ShapeDtypeStruct((rows, model), bf16),
            jax.ShapeDtypeStruct((rows, model), bf16),
            jax.ShapeDtypeStruct((rows, 128), f32),
            jax.ShapeDtypeStruct((model, rows), bf16),
            jax.ShapeDtypeStruct((rows // 2, model), bf16),
        ],
        scratch_shapes=[
            pltpu.VMEM(ffn_in.shape, bf16),
            pltpu.VMEM(ffn_out.shape, bf16),
            pltpu.SemaphoreType.DMA((2,)),
        ],
        compiler_params=params(63),
    )(
        meta, nodes, mine, theirs, out_weight, gain_one[None], ffn_in, ffn_bias[None], ffn_out, gain_two[None]
    )


def edge_kernel(
    static_first,
    meta,
    states,
    ids,
    edges,
    cots,
    residue_t,
    neighbour_t,
    edge_weight,
    bias,
    out_weight,
    out_weight_t,
    gain,
    new_edges,
    partial,
    back_table,
    grads,
    squares,
    vectors,
    padded,
    far_table,
    near_table,
    base,
    gains,
    far_sum,
    near_sum,
    own_sum,
    gain_sum,
    grad_edge,
    grad_out,
):
    step = pl.program_id(0)
    width, rows = base.shape
    window = window_of(rows)
    local_first = pl.multiple_of(meta[1], 128) if static_first is None else static_first

    @pl.when(step == 0)
    def _():
        fill = jnp.zeros((width, 256 - width), bf16)
        scaled_weight = (root_half * edge_weight[...].astype(f32)).astype(bf16)
        weight = jnp.concatenate([scaled_weight, fill], axis=1)
        projected = (root_half * nt(states[...], neighbour_t[...])).astype(bf16)
        projected = jnp.concatenate([projected, jnp.zeros((SPAN, 256 - width), bf16)], axis=1)
        far_table[...] = jnp.concatenate([projected, weight], axis=0).T[:width, :]
        padded[...] = jnp.zeros_like(padded)
        padded[REACH : REACH + SPAN, :] = projected
        for tile, _ in tiles(rows):
            part = padded[window_rows(local_first, rows, tile), :]
            near_table[tile] = jnp.concatenate([part, weight], axis=0).T[:width, :]
        block = states[pl.ds(local_first, rows), :]
        base[...] = root_half * (nt(residue_t[...], block) + repeat_lanes(bias[...], rows))
        gains[...] = repeat_lanes(gain[...], rows)
        for total in (far_sum, near_sum, own_sum, gain_sum, grad_edge, grad_out):
            total[...] = jnp.zeros_like(total)

    group = edges.shape[0]
    order = list(range(1, group, 2)) + list(range(0, group, 2))
    found_rows, found_grads = {}, {}
    for side in order:
        near = ids[pl.ds(group * step + side, 1), :] - meta[2]
        edge = edges[side]
        if side % 2 == 0:
            chosen = [
                near_rows(near[:, lanes], edges[side, :, lanes], local_first + lanes.start)
                for _, lanes in tiles(rows)
            ]
            value = jnp.concatenate(
                [nn(near_table[tile], part) for tile, part in enumerate(chosen)], axis=1
            )
        else:
            chosen = far_rows(near, edge)
            value = nn(far_table[...], chosen)
        act, slope = wide_gelu_and_slope(value + base[...])
        act = act.astype(bf16)
        third = edge.astype(f32) + nn(out_weight_t[...], act)
        centered = third - jnp.mean(third, 0, keepdims=True)
        inv_std = lax.rsqrt(jnp.mean(centered * centered, 0, keepdims=True) + epsilon)
        unit = centered * inv_std
        new_edges[side] = (unit * gains[...]).astype(bf16)
        cot = cots[side].astype(f32)
        gain_sum[...] += cot * unit
        scaled = cot * gains[...]
        grad_third = inv_std * (
            scaled
            - jnp.mean(scaled, 0, keepdims=True)
            - unit * jnp.mean(scaled * unit, 0, keepdims=True)
        )
        branch = grad_third.astype(bf16)
        grad_out[...] += nt(act, branch)
        grad_wide = nn(out_weight[...], branch) * slope
        own_sum[...] += grad_wide
        grad_value = grad_wide.astype(bf16)
        partial[side, :width, :] = branch
        partial[side, width:, :] = grad_value
        found_rows[side], found_grads[side] = chosen, grad_value
        if side == order[group // 2 - 1]:
            far_sum[...] += nt(
                beside([found_rows[k] for k in order[: group // 2]]),
                beside([found_grads[k] for k in order[: group // 2]]),
            )
    for tile, lanes in tiles(rows):
        found = nt(
            beside([found_rows[k][tile] for k in range(0, group, 2)]),
            beside([found_grads[k][:, lanes] for k in range(0, group, 2)]),
        )
        near_sum[window_rows(local_first, rows, tile), :] += found[:window, :]
        grad_edge[...] += found[window:, :]

    @pl.when(step == pl.num_programs(0) - 1)
    def _():
        table_high, table_low = split(far_sum[:SPAN, :] + near_sum[REACH : REACH + SPAN, :])
        own_high, own_low = split(own_sum[...])
        back = nn(table_high, neighbour_t[...]) + nn(table_low, neighbour_t[...])
        own_back = tn(own_high, residue_t[...]) + tn(own_low, residue_t[...])
        if rows == SPAN:
            back_table[...] = (back + own_back).astype(bf16)
        else:
            own_rows = pl.ds(local_first, rows)
            back_table[...] = back.astype(bf16)
            back_table[own_rows, :] = (back_table[own_rows, :].astype(f32) + own_back).astype(bf16)
        block = states[pl.ds(local_first, rows), :]
        grad_self = nn(own_high, block) + nn(own_low, block)
        grad_near = tn(table_high, states[...]) + tn(table_low, states[...])
        grads[:width, :] = grad_self
        grads[width:, :] = grad_near
        squares[...] = jnp.zeros_like(squares)
        squares[:, :width] = grad_edge[...] + far_sum[SPAN:, :]
        squares[:, 256 : 256 + width] = root_half * grad_out[...]
        vectors[...] = jnp.zeros_like(vectors)
        ones = jnp.ones((16, rows), bf16)
        gain_high, gain_low = split(gain_sum[...])
        vectors[0:1, :width] = (nt(ones, own_high) + nt(ones, own_low))[:1]
        vectors[1:2, :width] = (nt(ones, gain_high) + nt(ones, gain_low))[:1]


def edge_layer(
    meta, states, ids, edges, cots, residue, neighbour, edge_weight, bias, out_weight, out_weight_t, gain, local_first
):
    group = group_of(edges.shape[0], EDGE_GROUP)
    width, rows = edges.shape[1:]
    model = states.shape[1]
    by_pair = pl.BlockSpec((group, width, rows), lambda i: (i, 0, 0))
    square = whole((width, width))
    return pl.pallas_call(
        functools.partial(edge_kernel, local_first),
        name="edge_layer",
        grid=(edges.shape[0] // group,),
        in_specs=[
            smem,
            whole(states.shape),
            whole(ids.shape),
            by_pair,
            by_pair,
            whole((width, model)),
            whole((width, model)),
            square,
            whole((width, 128)),
            square,
            square,
            whole((width, 128)),
        ],
        out_specs=[
            by_pair,
            pl.BlockSpec((group, 2 * width, rows), lambda i: (i, 0, 0)),
            whole((SPAN, model)),
            whole((2 * width, model)),
            whole((width, model)),
            whole((8, model)),
        ],
        out_shape=[
            jax.ShapeDtypeStruct(edges.shape, bf16),
            jax.ShapeDtypeStruct((edges.shape[0], 2 * width, rows), bf16),
            jax.ShapeDtypeStruct((SPAN, model), bf16),
            jax.ShapeDtypeStruct((2 * width, model), f32),
            jax.ShapeDtypeStruct((width, model), f32),
            jax.ShapeDtypeStruct((8, model), f32),
        ],
        scratch_shapes=[
            pltpu.VMEM((SPAN + 2 * REACH, 256), bf16),
            pltpu.VMEM((width, SPAN + width), bf16),
            pltpu.VMEM((rows // tile_of(rows), width, window_of(rows) + width), bf16),
            pltpu.VMEM((width, rows), f32),
            pltpu.VMEM((width, rows), f32),
            pltpu.VMEM((SPAN + width, width), f32),
            pltpu.VMEM((SPAN + 2 * REACH, width), f32),
            pltpu.VMEM((width, rows), f32),
            pltpu.VMEM((width, rows), f32),
            pltpu.VMEM((width, width), f32),
            pltpu.VMEM((width, width), f32),
        ],
        compiler_params=params(),
    )(
        meta,
        states,
        ids,
        edges,
        cots,
        residue.T,
        neighbour.T,
        edge_weight,
        bias,
        out_weight,
        out_weight_t,
        gain,
    )


def norm_back(unit, inv_std, gain, grad_out):
    grad_gain = jnp.sum(grad_out * unit, axis=0, keepdims=True)
    scaled = grad_out * gain
    grad_in = inv_std * (
        scaled
        - jnp.mean(scaled, -1, keepdims=True)
        - unit * jnp.mean(scaled * unit, -1, keepdims=True)
    )
    return grad_in, grad_gain


def node_backward_kernel(
    meta,
    own_cot,
    other_cot,
    mine,
    theirs,
    first,
    second,
    stats,
    ffn_input,
    act,
    slope,
    sums,
    gain_one,
    ffn_in,
    ffn_out,
    gain_two,
    out_weight,
    own_grad,
    spread,
    weights,
    message_out,
    vectors,
    sum_out,
    sum_in,
    sum_message,
    in_here,
    out_here,
    sems,
):
    step = pl.program_id(0)
    chunk, model = first.shape
    hidden = slope.shape[1]
    core = meta[4]
    half = own_cot.shape[0]

    fetches = [
        pltpu.make_async_copy(there, here, sems.at[place])
        for place, (there, here) in enumerate(((ffn_in, in_here), (out_weight, out_here)))
    ]

    @pl.when(step == 0)
    def _():
        for fetch in fetches:
            fetch.start()
        vectors[...] = jnp.zeros_like(vectors)
        sum_out[...] = jnp.zeros_like(sum_out)
        sum_in[...] = jnp.zeros_like(sum_in)
        sum_message[...] = jnp.zeros_like(sum_message)

    if chunk > half:
        mine_first = core == 0
        lower = jnp.where(mine_first, own_cot[...], other_cot[...])
        cot = jnp.concatenate([lower, jnp.where(mine_first, other_cot[...], own_cot[...])], axis=0)
    else:
        row = step * chunk
        inside = pl.ds(pl.multiple_of(lax.rem(row, half), chunk), chunk)
        cot = jnp.where(row // half == core, own_cot[inside, :], other_cot[inside, :])
    total = cot.astype(f32) + (mine[...].astype(f32) + theirs[...].astype(f32))
    second_inv = stats[:, 2:3]
    first_inv = stats[:, 1:2]
    grad_second, gain_two_part = norm_back(second[...].astype(f32), second_inv, gain_two[...], total)
    top = grad_second.astype(bf16)
    grad_hidden = (nt(top, ffn_out[...]) * slope[...].astype(f32)).astype(bf16)
    sum_out[...] += tn(act[...], top)
    sum_in[...] += tn(ffn_input[...], grad_hidden)
    bias_part = jnp.sum(grad_hidden.astype(f32), axis=0, keepdims=True)

    @pl.when(step == 0)
    def _():
        for fetch in fetches:
            fetch.wait()

    grad_norm = grad_second + nt(grad_hidden, in_here[...])
    grad_first, gain_one_part = norm_back(first[...].astype(f32), first_inv, gain_one[...], grad_norm)
    store_own_rows(own_grad, grad_first, step, core)
    message_cot = (grad_first * stats[:, :1]).astype(bf16)
    spread[...] = (0.5 * nt(out_here[...], message_cot)).astype(bf16)
    sum_message[...] += nn(sums[pl.ds(pl.multiple_of(core * (model // 2), 16), model // 2), :], message_cot)
    vectors[0:1, :] += gain_one_part
    vectors[1:2, :] += gain_two_part
    for part in range(hidden // model):
        vectors[2 + part : 3 + part, :] += bias_part[:, part * model : (part + 1) * model]

    @pl.when(step == pl.num_programs(0) - 1)
    def _():
        weights[: hidden // 2, :] = sum_out[...].astype(bf16)
        for part in range(hidden // model):
            start = hidden // 2 + part * (model // 2)
            weights[start : start + model // 2, :] = sum_in[
                :, part * model : (part + 1) * model
            ].astype(bf16)
        message_out[...] = sum_message[...]


def node_backward(
    meta,
    own_cot,
    other_cot,
    mine,
    theirs,
    first,
    second,
    stats,
    ffn_input,
    act,
    slope,
    sums,
    gain_one,
    ffn_in,
    ffn_out,
    gain_two,
    out_weight,
):
    rows, model = first.shape
    hidden = slope.shape[1]
    chunk = min(rows, NODE_CHUNK)

    def by_rows(width):
        return pl.BlockSpec((chunk, width), lambda i: (i, 0))

    by_lanes = pl.BlockSpec((model, chunk), lambda i: (0, i))
    return pl.pallas_call(
        node_backward_kernel,
        name="node_backward",
        grid=(rows // chunk,),
        in_specs=[
            smem,
            whole(own_cot.shape),
            whole(other_cot.shape),
            by_rows(model),
            by_rows(model),
            by_rows(model),
            by_rows(model),
            by_rows(128),
            by_rows(model // 2),
            by_rows(hidden // 2),
            by_rows(hidden),
            by_lanes,
            whole((1, model)),
            pl.BlockSpec(memory_space=pl.ANY),
            whole(ffn_out.shape),
            whole((1, model)),
            pl.BlockSpec(memory_space=pl.ANY),
        ],
        out_specs=[
            whole(own_cot.shape),
            by_lanes,
            whole((hidden, model)),
            whole((model // 2, model)),
            whole((8, model)),
        ],
        out_shape=[
            jax.ShapeDtypeStruct(own_cot.shape, f32),
            jax.ShapeDtypeStruct((model, rows), bf16),
            jax.ShapeDtypeStruct((hidden, model), bf16),
            jax.ShapeDtypeStruct((model // 2, model), f32),
            jax.ShapeDtypeStruct((8, model), f32),
        ],
        scratch_shapes=[
            pltpu.VMEM((hidden // 2, model), f32),
            pltpu.VMEM((model // 2, hidden), f32),
            pltpu.VMEM((model // 2, model), f32),
            pltpu.VMEM(ffn_in.shape, bf16),
            pltpu.VMEM(out_weight.shape, bf16),
            pltpu.SemaphoreType.DMA((2,)),
        ],
        compiler_params=params(63),
    )(
        meta,
        own_cot,
        other_cot,
        mine,
        theirs,
        first,
        second,
        stats,
        ffn_input,
        act,
        slope,
        sums,
        gain_one[None],
        ffn_in,
        ffn_out,
        gain_two[None],
        out_weight,
    )


def message_backward_kernel(
    static_first,
    meta,
    table,
    spread,
    ids,
    edges,
    slope,
    receiver,
    neighbour,
    edge_grads,
    squares,
    message_out,
    edge_vectors,
    node_vectors,
    own_grad,
    keep,
    send,
    keep_weights,
    send_weights,
    far_sum,
    near_sum,
    own_sum,
    edge_sum,
    weights,
    table_here,
    receiver_here,
    neighbour_here,
    edge_grads_here,
    squares_here,
    message_out_here,
    own_grad_here,
    sems,
):
    step = pl.program_id(0)
    model, rows = spread.shape
    group, width = edges.shape[:2]
    half = keep.shape[0]
    window = window_of(rows)
    local_first = pl.multiple_of(meta[1], 128) if static_first is None else static_first

    at_the_end = (
        (table, table_here),
        (receiver, receiver_here),
        (neighbour, neighbour_here),
        (edge_grads, edge_grads_here),
        (squares, squares_here),
        (message_out, message_out_here),
        (own_grad, own_grad_here),
    )
    fetches = [
        pltpu.make_async_copy(there, here, sems.at[place]) for place, (there, here) in enumerate(at_the_end)
    ]

    @pl.when(step == 0)
    def _():
        for fetch in fetches:
            fetch.start()
        for total in (far_sum, near_sum, own_sum, edge_sum):
            total[...] = jnp.zeros_like(total)

    near = [ids[pl.ds(group * step + k, 1), :] - meta[2] for k in range(group)]
    grads = [spread[...] * slope[k] for k in range(group)]
    own_sum[...] += sum(grad.astype(f32) for grad in grads)
    far_sum[...] += nt(
        beside([far_rows(near[k], edges[k]) for k in range(1, group, 2)]), beside(grads[1::2])
    )
    for tile, lanes in tiles(rows):
        first = local_first + lanes.start
        part = beside([near_rows(near[k][:, lanes], edges[k, :, lanes], first) for k in range(0, group, 2)])
        found = nt(part, beside([grad[:, lanes] for grad in grads[::2]]))
        near_sum[window_rows(local_first, rows, tile), :] += found[:window, :]
        edge_sum[...] += found[window:, :]

    @pl.when(step == pl.num_programs(0) - 1)
    def _():
        for fetch in fetches:
            fetch.wait()
        table_sum = (far_sum[:SPAN, :] + near_sum[REACH : REACH + SPAN, :]).astype(bf16)
        own_rows = own_sum[...].T
        own_low = own_rows.astype(bf16)
        nodes_t = table_here[...].T
        block_t = nodes_t
        if rows < SPAN:
            block_t = table_here[pl.ds(local_first, rows), :].T
        split_rows = keep_weights.shape[0]
        for core, start in enumerate((0, split_rows)):
            if core == 0:
                weights[:model, :] = nn(block_t, own_low)
                third = edge_sum[...] + far_sum[SPAN:, :]
            else:
                weights[start : start + model, :] = nn(nodes_t, table_sum)
                third = squares_here[...]
            start += model
            weights[start : start + width, :] = third
            start += width
            weights[start : start + width, :] = edge_grads_here[core * width : (core + 1) * width, :]
            start += width
            weights[start : start + model // 2, :] = jnp.where(meta[4] == core, message_out_here[...], 0.0)
            start += model // 2
            if core == 0:
                weights[start:split_rows, :] = jnp.zeros((split_rows - start, model), f32)
        weights[start : start + 8, :] = edge_vectors[...]
        weights[start + 8 : start + 16, :] = 0.5 * node_vectors[...]
        weights[start + 16 :, :] = jnp.broadcast_to(
            jnp.sum(own_rows, axis=0, keepdims=True), (2 * split_rows - start - 16, model)
        )
        mine = pl.multiple_of(meta[4] * split_rows, split_rows)
        keep_weights[...] = weights[pl.ds(mine, split_rows), :]
        send_weights[...] = weights[pl.ds(split_rows - mine, split_rows), :].astype(bf16)
        back = nt(table_sum, neighbour_here[...])
        own_back = nt(own_low, receiver_here[...])
        if rows == SPAN:
            far_sum[:SPAN, :] = back + own_back
        else:
            far_sum[:SPAN, :] = back
            far_sum[pl.ds(local_first, rows), :] += own_back
        high = meta[0]
        kept = far_sum[pl.ds(pl.multiple_of(high * half, half), half), :]
        keep[...] = kept + own_grad_here[...] if own_grad_here.shape[0] == half else kept
        send[...] = far_sum[pl.ds(pl.multiple_of((1 - high) * half, half), half), :].astype(bf16)


def message_backward(
    meta,
    table,
    spread,
    ids,
    edges,
    slope,
    receiver,
    neighbour,
    edge_grads,
    squares,
    message_out,
    edge_vectors,
    node_vectors,
    own_grad,
    local_first,
):
    group = group_of(edges.shape[0], MSG_GROUP)
    width, rows = edges.shape[1:]
    model = table.shape[1]
    anywhere = pl.BlockSpec(memory_space=pl.ANY)
    late = (table, receiver, neighbour, edge_grads, squares, message_out, own_grad)
    split_rows = -(-(model + 2 * width + model // 2 + 24) // 256) * 256
    return pl.pallas_call(
        functools.partial(message_backward_kernel, local_first),
        name="message_backward",
        grid=(edges.shape[0] // group,),
        in_specs=[
            smem,
            anywhere,
            whole(spread.shape),
            whole(ids.shape),
            pl.BlockSpec((group, width, rows), lambda i: (i, 0, 0)),
            pl.BlockSpec((group, model, rows), lambda i: (i, 0, 0)),
            anywhere,
            anywhere,
            anywhere,
            anywhere,
            anywhere,
            whole(edge_vectors.shape),
            whole(node_vectors.shape),
            anywhere,
        ],
        out_specs=[
            whole((SPAN // 2, model)),
            whole((SPAN // 2, model)),
            whole((split_rows, model)),
            whole((split_rows, model)),
        ],
        out_shape=[
            jax.ShapeDtypeStruct((SPAN // 2, model), f32),
            jax.ShapeDtypeStruct((SPAN // 2, model), bf16),
            jax.ShapeDtypeStruct((split_rows, model), f32),
            jax.ShapeDtypeStruct((split_rows, model), bf16),
        ],
        scratch_shapes=[
            pltpu.VMEM((SPAN + width, model), f32),
            pltpu.VMEM((SPAN + 2 * REACH, model), f32),
            pltpu.VMEM((model, rows), f32),
            pltpu.VMEM((width, model), f32),
            pltpu.VMEM((2 * split_rows, model), f32),
        ]
        + [pltpu.VMEM(value.shape, value.dtype) for value in late]
        + [pltpu.SemaphoreType.DMA((len(late),))],
        compiler_params=params(),
    )(
        meta,
        table,
        spread,
        ids,
        edges,
        slope,
        receiver,
        neighbour,
        edge_grads,
        squares,
        message_out,
        edge_vectors,
        node_vectors,
        own_grad,
    )


def edge_gradient_kernel(partial, slope, spread, message_weight, edge_weight, *rest):
    out = rest[-1]
    width = out.shape[1]
    weights = jnp.concatenate([message_weight[...], edge_weight[...]], axis=1)
    for k in range(out.shape[0]):
        grads = jnp.concatenate([spread[...] * slope[k], partial[k, width:, :]], axis=0)
        out[k] = partial[k, :width, :].astype(f32) + nn(weights, grads)


def edge_gradient(first, count, filled, partial, slope, spread, message_weight, edge_weight):
    columns_in, width, rows = partial.shape
    width //= 2
    model = spread.shape[0]

    def pair(size):
        return pl.BlockSpec((2, size, rows), lambda i: (first + i, 0, 0))

    before = [] if filled is None else [filled]
    return pl.pallas_call(
        edge_gradient_kernel,
        name="edge_gradient",
        grid=(count,),
        in_specs=[
            pair(2 * width),
            pair(model),
            whole(spread.shape),
            whole(message_weight.shape),
            whole(edge_weight.shape),
        ]
        + [pl.BlockSpec(memory_space=pl.ANY)] * len(before),
        out_specs=pair(width),
        out_shape=jax.ShapeDtypeStruct((columns_in, width, rows), f32),
        input_output_aliases={5: 0} if before else {},
        compiler_params=params(54),
    )(partial, slope, spread, message_weight, edge_weight, *before)


def sum_to_slots_kernel(shift, meta, *refs):
    parts, outs, total = refs[:-5], refs[-5:-1], refs[-1]
    total[...] = parts[0][...].astype(f32)
    for part in parts[1:]:
        total[...] += part[...].astype(f32)
    place = meta[5] >> shift & 3
    rows = outs[0].shape[0]
    for slot, out in enumerate(outs):
        start = pl.multiple_of((place ^ slot) * rows, rows)
        out[...] = total[pl.ds(start, rows), :].astype(out.dtype)


def sum_to_slots(meta, shift, parts):
    rows, width = parts[0].shape
    out_types = (f32, bf16, bf16, bf16)
    return pl.pallas_call(
        functools.partial(sum_to_slots_kernel, shift),
        name="sum_to_slots",
        in_specs=[smem] + [whole(part.shape) for part in parts],
        out_specs=[whole((rows // 4, width))] * 4,
        out_shape=[jax.ShapeDtypeStruct((rows // 4, width), kind) for kind in out_types],
        scratch_shapes=[pltpu.VMEM((rows, width), f32)],
        compiler_params=params(12),
    )(meta, *parts)


def sum_parts_kernel(*refs):
    total = refs[0][...].astype(f32)
    for part in refs[1:-1]:
        total = total + part[...].astype(f32)
    refs[-1][...] = total.astype(bf16)


def sum_parts(parts):
    return pl.pallas_call(
        sum_parts_kernel,
        name="sum_parts",
        in_specs=[whole(part.shape) for part in parts],
        out_specs=whole(parts[0].shape),
        out_shape=jax.ShapeDtypeStruct(parts[0].shape, bf16),
        compiler_params=params(12),
    )(*parts)


def assemble_kernel(shift, meta, *refs):
    place = meta[5] >> shift & 3
    rows = refs[0].shape[0]
    for slot, part in enumerate(refs[:-1]):
        start = pl.multiple_of((place ^ slot) * rows, rows)
        refs[-1][pl.ds(start, rows), :] = part[...]


def assemble(meta, shift, parts):
    rows, width = parts[0].shape
    return pl.pallas_call(
        functools.partial(assemble_kernel, shift),
        name="assemble",
        in_specs=[smem] + [whole(part.shape) for part in parts],
        out_specs=whole((4 * rows, width)),
        out_shape=jax.ShapeDtypeStruct((4 * rows, width), bf16),
        compiler_params=params(12),
    )(meta, *parts)


def sent_each_way(shift, slots):
    return [moved(slot, place << shift) for place, slot in enumerate(slots) if place > 0]


def moved(value, mask):
    devices = lax.axis_size("res") * lax.axis_size("nbr")
    cores = lax.axis_size("nbr")
    pairs = [(source, source ^ (mask * cores)) for source in range(devices)]
    return lax.ppermute(value, ("res", "nbr"), pairs)


def unpack_early_kernel(side, meta, source, *rest):
    grad_out, grad_in, wide, out_sem, in_sem = rest[-5:]
    place = meta[4] if side == 0 else 1 - meta[4]
    model, hidden = grad_in.shape
    wide[...] = source[...].astype(f32)
    half, quarter = hidden // 2, model // 2
    copies = [
        pltpu.make_async_copy(
            wide.at[:half], grad_out.at[pl.ds(pl.multiple_of(place * half, half), half)], out_sem
        )
    ]
    for part in range(hidden // model):
        start = half + part * quarter
        copies.append(
            pltpu.make_async_copy(
                wide.at[start : start + quarter],
                grad_in.at[
                    pl.ds(pl.multiple_of(place * quarter, quarter), quarter),
                    part * model : (part + 1) * model,
                ],
                in_sem.at[part],
            )
        )
    for copy in copies:
        copy.start()
    for copy in copies:
        copy.wait()


def unpack_early(meta, side, source, before):
    rows, model = source.shape
    anywhere = pl.BlockSpec(memory_space=pl.ANY)
    return pl.pallas_call(
        functools.partial(unpack_early_kernel, side),
        name="unpack_early",
        in_specs=[smem, whole(source.shape)] + [anywhere] * len(before),
        out_specs=[anywhere, anywhere],
        out_shape=[
            jax.ShapeDtypeStruct((rows, model), f32),
            jax.ShapeDtypeStruct((model, rows), f32),
        ],
        scratch_shapes=[
            pltpu.VMEM((rows, model), f32),
            pltpu.SemaphoreType.DMA,
            pltpu.SemaphoreType.DMA((rows // model,)),
        ],
        input_output_aliases={2: 0, 3: 1} if before else {},
        compiler_params=params(),
    )(meta, source, *before)


def unpack_late_kernel(
    meta, own, other, grad_self, grad_near, grad_edge, edge_edge, edge_out, edge_self, edge_near, message_out, *vectors
):
    lower = meta[4] == 0
    model = own.shape[1]
    width = edge_edge.shape[0]
    first = jnp.where(lower, own[...], other[...]).astype(f32)
    second = jnp.where(lower, other[...], own[...]).astype(f32)
    grad_self[...] = first[:model, :]
    grad_near[...] = second[:model, :]
    start = model + width
    grad_edge[...] = first[model:start, :]
    edge_edge[...] = second[model:start, :width]
    edge_out[...] = second[model:start, 256 : 256 + width]
    edge_self[...] = first[start : start + width, :]
    edge_near[...] = second[start : start + width, :]
    start += width
    half = model // 2
    message_out[:half, :] = first[start : start + half, :]
    message_out[half:, :] = second[start : start + half, :]
    start += half
    edge_bias, gain_three, gain_one, gain_two, message_bias, ffn_bias = vectors
    edge_bias[...] = second[start : start + 1, :width]
    gain_three[...] = second[start + 1 : start + 2, :width]
    gain_one[...] = second[start + 8 : start + 9, :]
    gain_two[...] = second[start + 9 : start + 10, :]
    message_bias[...] = second[start + 16 : start + 17, :]
    for part in range(ffn_bias.shape[1] // model):
        row = start + 10 + part
        ffn_bias[:, part * model : (part + 1) * model] = second[row : row + 1, :]


def unpack_late(meta, own, other, width, hidden):
    model = own.shape[1]
    shapes = [(model, model)] * 2 + [(width, model)] + [(width, width)] * 2 + [(width, model)] * 2
    shapes += [(model, model)] + [(1, size) for size in (width, width, model, model, model, hidden)]
    return pl.pallas_call(
        unpack_late_kernel,
        name="unpack_late",
        in_specs=[smem, whole(own.shape), whole(other.shape)],
        out_specs=[whole(shape) for shape in shapes],
        out_shape=[jax.ShapeDtypeStruct(shape, f32) for shape in shapes],
        compiler_params=params(),
    )(meta, own, other)


def planes(size):
    return [[4 * block + place for place in range(4)] for block in range(size // 4)]


def columns(size):
    return [[4 * block + place for block in range(size // 4)] for place in range(4)]


def tied(*arrays):
    return lax.optimization_barrier(arrays)


def weight_sums(meta, early, kept, sent, kept_nodes, nodes, size, pieces):
    received = swapped(sent, 0)
    early = lax.psum(early, "res", axis_index_groups=columns(size))
    value, received, given = tied(pieces[0](None), received, swapped(nodes, 0))
    node_grad = kept_nodes + given.astype(f32)
    value, kept, *slots = tied(value, *sum_to_slots(meta, 0, [kept, received]))
    value, node_grad, *received = tied(pieces[1](value), node_grad, *sent_each_way(0, [kept, *slots]))
    value, kept, *slots = tied(value, *sum_to_slots(meta, 2, [kept, *received]))
    value, *received = tied(pieces[2](value), *sent_each_way(2, [kept, *slots]))
    value, early, late = tied(value, early, sum_parts([kept, *received]))
    early = lax.all_gather(early, "res", axis_index_groups=planes(size), tiled=True)
    value, *received = tied(pieces[3](value), *sent_each_way(2, [late] * 4))
    value, late = tied(value, assemble(meta, 2, [late, *received]))
    value, *received = tied(pieces[4](value), *sent_each_way(0, [late] * 4))
    return early, assemble(meta, 0, [late, *received]), value, node_grad


def joined(table, other, high_side):
    return jnp.where(
        high_side, jnp.concatenate([other, table], axis=0), jnp.concatenate([table, other], axis=0)
    )


def halves(table, high_side):
    half = table.shape[0] // 2
    lower, upper = (table[:half], table[half:])
    return (jnp.where(high_side, upper, lower), jnp.where(high_side, lower, upper))


def sum_blocks(table, device, level):
    keep, send = halves(table, device >> level & 1 == 1)
    return keep + swapped(send.astype(bf16), level).astype(keep.dtype)


def on_device(
    nodes,
    edges,
    neighbours,
    lengths,
    message_receiver_weight,
    message_neighbour_weight,
    message_edge_weight,
    message_hidden_bias,
    message_output_weight,
    gain_one,
    ffn_in,
    ffn_bias,
    ffn_out,
    gain_two,
    edge_update_residue_weight,
    edge_update_neighbour_weight,
    edge_update_edge_weight,
    edge_update_bias,
    edge_out,
    gain_three,
    node_cot,
    edge_cot,
):
    rows, half_k, edge_width = edges.shape
    own_rows, model = nodes.shape
    hidden = ffn_in.shape[1]
    levels = (SPAN // own_rows).bit_length() - 1
    core = lax.axis_index("nbr")
    device = lax.axis_index("res") * lax.axis_size("nbr") + core
    first_row = lax.axis_index("res") * rows
    bucket = first_row // SPAN
    group_start = bucket * SPAN
    local_first = 0 if rows == SPAN else None
    top = device >> (levels - 1) & 1
    meta = jnp.stack(
        [top, first_row - group_start, group_start, bucket, core, lax.axis_index("res"), 0, 0]
    ).astype(jnp.int32)

    ids = neighbours.T
    edges_t = edges.transpose(1, 2, 0)
    cot_t = edge_cot.transpose(1, 2, 0)

    table = nodes
    for level in range(levels - 1):
        table = joined(table, swapped(table, level), device >> level & 1 == 1)
    other_table = swapped(table, levels - 1)
    other_cot = swapped(node_cot, 0)

    node_table, slope, packed = message_forward(
        meta,
        lengths,
        table,
        other_table,
        ids,
        edges_t,
        message_receiver_weight,
        message_neighbour_weight,
        message_edge_weight,
        message_hidden_bias,
        local_first,
    )
    packed, *edge_parts = tied(
        packed,
        jnp.broadcast_to(edge_update_bias[:, None], (edge_width, 128)),
        edge_out * 0.5,
        (edge_out.T.astype(f32) * root_half).astype(bf16),
        jnp.broadcast_to(gain_three[:, None], (edge_width, 128)),
    )
    block = node_table
    if rows < SPAN:
        block = lax.dynamic_slice_in_dim(node_table, first_row - group_start, rows, 0)
    state, ffn_input, act, ffn_slope, first, second, stats, sums, node_out = node_forward(
        meta,
        block,
        packed,
        swapped(packed, 0),
        message_output_weight,
        gain_one,
        ffn_in,
        ffn_bias,
        ffn_out,
        gain_two,
    )
    states = state
    for level in range(1, levels):
        states = joined(states, swapped(states, level), device >> level & 1 == 1)
    new_edges, partial, back, edge_grads, squares, edge_vectors = edge_layer(
        meta,
        states,
        ids,
        edges_t,
        cot_t,
        edge_update_residue_weight,
        edge_update_neighbour_weight,
        edge_update_edge_weight,
        *edge_parts,
        local_first,
    )
    for level in reversed(range(1, levels)):
        back = sum_blocks(back, device, level)
    own_grad, spread, early, message_out, node_vectors = node_backward(
        meta,
        node_cot,
        other_cot,
        back,
        swapped(back, 0),
        first,
        second,
        stats,
        ffn_input,
        act,
        ffn_slope,
        sums,
        gain_one,
        ffn_in,
        ffn_out,
        gain_two,
        message_output_weight,
    )
    size = lax.axis_size("res")
    if size == 16:
        early = lax.psum_scatter(early, "res", axis_index_groups=planes(size), tiled=True)
    else:
        early = lax.psum(early.astype(f32), "res").astype(bf16)
    keep, send, kept_weights, sent_weights = message_backward(
        meta,
        node_table,
        spread,
        ids,
        edges_t,
        slope,
        message_receiver_weight,
        message_neighbour_weight,
        edge_grads,
        squares,
        message_out,
        edge_vectors,
        node_vectors,
        own_grad,
        local_first,
    )
    early, kept_weights, sent_weights = tied(early, kept_weights, sent_weights)
    counts = [1, 5, 4, 1, 4] if half_k == 30 else [half_k // 2]
    starts = [sum(counts[:index]) for index in range(len(counts))]

    def piece(start, count):
        return lambda filled: edge_gradient(
            start, count, filled, partial, slope, spread, message_edge_weight, edge_update_edge_weight
        )

    spans = [piece(*span) for span in zip(starts, counts)]
    if size == 16:
        early, late, edge_grad, node_grad = weight_sums(
            meta, early, kept_weights, sent_weights, keep, send, size, spans
        )
    else:
        late = lax.psum(kept_weights + swapped(sent_weights, 0).astype(f32), "res").astype(bf16)
        edge_grad = None
        for span in spans:
            edge_grad = span(edge_grad)
        node_grad = keep + swapped(send, levels - 1).astype(f32)
        for level in reversed(range(levels - 1)):
            node_grad = sum_blocks(node_grad, device, level)
        if levels > 1:
            node_grad = own_grad + node_grad
    late_other = swapped(late, 0)
    (
        grad_msg_self,
        grad_msg_nbr,
        grad_msg_edge,
        grad_edge_edge,
        grad_edge_out,
        grad_edge_self,
        grad_edge_nbr,
        grad_msg_out,
        grad_edge_bias,
        grad_gain_three,
        grad_gain_one,
        grad_gain_two,
        grad_msg_bias,
        grad_ffn_bias,
    ) = unpack_late(meta, late, late_other, edge_width, hidden)
    early, edge_grad, grad_msg_self = tied(early, edge_grad, grad_msg_self)
    early_other, *halves_out = tied(swapped(early, 0), *unpack_early(meta, 0, early, []))
    grad_ffn_out, grad_ffn_in = unpack_early(meta, 1, early_other, halves_out)
    return (
        node_out,
        new_edges.transpose(2, 0, 1),
        node_grad,
        edge_grad.transpose(2, 0, 1),
        grad_msg_self,
        grad_msg_nbr,
        grad_msg_edge,
        grad_msg_bias[0],
        grad_msg_out,
        grad_gain_one[0],
        grad_ffn_in,
        grad_ffn_bias[0],
        grad_ffn_out,
        grad_gain_two[0],
        grad_edge_self.T,
        grad_edge_nbr.T,
        grad_edge_edge,
        grad_edge_bias[0],
        grad_edge_out,
        grad_gain_three[0],
    )


def solution(mesh):
    rows = P(("res", "nbr"), None)
    pairs = P("res", "nbr", None)
    placed = (rows, pairs, P("res", "nbr")) + (P(),) * 17 + (rows, pairs)
    return jax.shard_map(
        on_device,
        mesh=mesh,
        in_specs=placed,
        out_specs=(rows, pairs, rows, pairs) + (P(),) * 16,
        check_vma=False,
    )
```

```python
import functools

import jax
import jax.numpy as jnp
from jax import lax
from jax.experimental import pallas as pl
from jax.experimental.pallas import tpu as pltpu
from jax.sharding import PartitionSpec as P

SPAN = 1024
REACH = 32
MASKED = -16384.0
FORWARD_GROUP = 6
EDGE_GROUP = 6
MSG_GROUP = 6
FORWARD_CHUNK = 512
NODE_CHUNK = 256

epsilon = 1e-05
root_half = 0.7071067811865476
inv_root_two_pi = 0.3989422804014327
half_log2_e = 0.7213475204444817
two_over_root_pi = 1.1283791670955126

bf16 = jnp.bfloat16
f32 = jnp.float32


def swapped(value, level):
    mask = 2**level
    devices = lax.axis_size("res") * lax.axis_size("nbr")
    pairs = [(source, source ^ mask) for source in range(devices)]
    return lax.ppermute(value, ("res", "nbr"), pairs)


def nn(left_op, right_op):
    return jnp.dot(left_op, right_op, preferred_element_type=f32)


def nt(left_op, right_op):
    return lax.dot_general(
        left_op, right_op, (((1,), (1,)), ((), ())), preferred_element_type=f32
    )


def tn(left_op, right_op):
    return lax.dot_general(
        left_op, right_op, (((0,), (0,)), ((), ())), preferred_element_type=f32
    )


def split(values):
    high = values.astype(bf16)
    return high, (values - high.astype(f32)).astype(bf16)


def twice_gelu_and_slope(values):
    below = 1.0 + lax.erf(values * root_half)
    density = jnp.exp2(values * values * -half_log2_e)
    return values * below, below + values * density * (2.0 * inv_root_two_pi)


def wide_gelu_and_slope(values):
    below = 1.0 + lax.erf(values)
    density = jnp.exp2(values * values * (-2.0 * half_log2_e))
    return values * below, below + values * density * two_over_root_pi


def scaled_gelu_and_slope(values):
    below = 1.0 + lax.erf(values)
    low = values.astype(bf16)
    density = jnp.exp2(low * low * bf16(-2.0 * half_log2_e))
    return values * below, below.astype(bf16) + low * density * bf16(two_over_root_pi)


def selector(rows, ids):
    places = lax.broadcasted_iota(jnp.int16, (rows, ids.shape[1]), 0)
    return jnp.where(places == ids.astype(jnp.int16), bf16(1), bf16(0))


def group_of(count, wanted):
    return wanted if count % wanted == 0 else 2


def tile_of(rows):
    return min(rows, 256)


def window_of(rows):
    return tile_of(rows) + 2 * REACH


def far_rows(ids, edge):
    return jnp.concatenate([selector(SPAN, ids), edge], axis=0)


def near_rows(ids, edge, first):
    return jnp.concatenate([selector(ids.shape[1] + 2 * REACH, ids - (first - REACH)), edge], axis=0)


def beside(parts):
    return parts[0] if len(parts) == 1 else jnp.concatenate(parts, axis=1)


def tiles(rows):
    width = tile_of(rows)
    return [(tile, slice(tile * width, (tile + 1) * width)) for tile in range(rows // width)]


def window_rows(local_first, rows, tile):
    start = local_first + tile * tile_of(rows)
    if not isinstance(start, int):
        start = pl.multiple_of(start, 128)
    return pl.ds(start, window_of(rows))


def repeat_lanes(column, width):
    return jnp.concatenate([column] * (width // column.shape[1]), axis=1)


def whole(shape):
    return pl.BlockSpec(shape, lambda *_: (0,) * len(shape))


def params(mebibytes=60):
    return pltpu.CompilerParams(vmem_limit_bytes=mebibytes * 2**20)


smem = pl.BlockSpec(memory_space=pltpu.SMEM)


def message_forward_kernel(
    static_first,
    meta,
    lengths,
    own,
    other,
    ids,
    edges,
    receiver,
    neighbour,
    edge_weight,
    bias,
    table,
    slope,
    packed,
    padded,
    far_table,
    near_table,
    base,
    sums,
    counts,
):
    step = pl.program_id(0)
    rows = base.shape[1]
    half = own.shape[0]
    length = lengths[meta[3]]
    local_first = pl.multiple_of(meta[1], 128) if static_first is None else static_first

    @pl.when(step == 0)
    def _():
        high = meta[0]
        table[pl.ds(pl.multiple_of(high * half, half), half), :] = own[...]
        table[pl.ds(pl.multiple_of((1 - high) * half, half), half), :] = other[...]
        places = lax.broadcasted_iota(jnp.int32, (SPAN, 1), 0)
        hidden = jnp.where(places < length, 0.0, MASKED)
        projected = (root_half * nn(table[...], neighbour[...]) + hidden).astype(bf16)
        scaled_weight = (root_half * edge_weight[...].astype(f32)).astype(bf16)
        far_table[...] = jnp.concatenate([projected, scaled_weight], axis=0).T
        padded[...] = jnp.zeros_like(padded)
        padded[REACH : REACH + SPAN, :] = projected
        for tile, _ in tiles(rows):
            window = padded[window_rows(local_first, rows, tile), :]
            near_table[tile] = jnp.concatenate([window, scaled_weight], axis=0).T
        block = table[pl.ds(local_first, rows), :]
        places = lax.broadcasted_iota(jnp.int32, (rows, 1), 0) + local_first
        hidden = jnp.where(places < length, 0.0, MASKED)
        base[...] = (root_half * (nn(block, receiver[...]) + bias[...]) + hidden).T
        sums[...] = jnp.zeros_like(sums)
        counts[...] = jnp.zeros_like(counts)

    positions = lax.broadcasted_iota(jnp.int32, (1, rows), 1) + local_first
    group = edges.shape[0]
    near = [ids[pl.ds(group * step + k, 1), :] - meta[2] for k in range(group)]
    counts[...] += jnp.where(positions < length, 1.0, 0.0) * sum(
        jnp.where(place < length, 1.0, 0.0) for place in near
    )
    for tile, lanes in tiles(rows):
        for k in range(0, group, 2):
            near_part = near_rows(near[k][:, lanes], edges[k, :, lanes], local_first + lanes.start)
            far_part = far_rows(near[k + 1][:, lanes], edges[k + 1, :, lanes])
            far_value = nn(far_table[...], far_part)
            near_value = nn(near_table[tile], near_part)
            far_act, far_slope = scaled_gelu_and_slope(far_value + base[:, lanes])
            slope[k + 1, :, lanes] = far_slope
            near_act, near_slope = scaled_gelu_and_slope(near_value + base[:, lanes])
            slope[k, :, lanes] = near_slope
            sums[:, lanes] += far_act + near_act

    @pl.when(step == pl.num_programs(0) - 1)
    def _():
        width = sums.shape[0]
        packed[:width, :] = (root_half * sums[...]).astype(bf16)
        packed[width:, :] = jnp.broadcast_to(counts[...], (16, rows)).astype(bf16)


def message_forward(meta, lengths, own, other, ids, edges, receiver, neighbour, edge_weight, bias, local_first):
    columns_in = edges.shape[0]
    group = group_of(columns_in, FORWARD_GROUP)
    width, rows = edges.shape[1:]
    model = own.shape[1]
    return pl.pallas_call(
        functools.partial(message_forward_kernel, local_first),
        name="message_forward",
        grid=(columns_in // group,),
        in_specs=[
            smem,
            smem,
            whole(own.shape),
            whole(other.shape),
            whole(ids.shape),
            pl.BlockSpec((group, width, rows), lambda i: (i, 0, 0)),
            whole(receiver.shape),
            whole(neighbour.shape),
            whole(edge_weight.shape),
            whole((1, model)),
        ],
        out_specs=[
            whole((SPAN, model)),
            pl.BlockSpec((group, model, rows), lambda i: (i, 0, 0)),
            whole((model + 16, rows)),
        ],
        out_shape=[
            jax.ShapeDtypeStruct((SPAN, model), bf16),
            jax.ShapeDtypeStruct((columns_in, model, rows), bf16),
            jax.ShapeDtypeStruct((model + 16, rows), bf16),
        ],
        scratch_shapes=[
            pltpu.VMEM((SPAN + 2 * REACH, model), bf16),
            pltpu.VMEM((model, SPAN + width), bf16),
            pltpu.VMEM((rows // tile_of(rows), model, window_of(rows) + width), bf16),
            pltpu.VMEM((model, rows), f32),
            pltpu.VMEM((model, rows), f32),
            pltpu.VMEM((1, rows), f32),
        ],
        compiler_params=params(63),
    )(meta, lengths, own, other, ids, edges, receiver, neighbour, edge_weight, bias[None])


def normed(values):
    mean_val = jnp.mean(values, -1, keepdims=True)
    centered = values - mean_val
    inv_std = lax.rsqrt(jnp.mean(centered * centered, -1, keepdims=True) + epsilon)
    return centered * inv_std, inv_std


def node_forward_kernel(
    meta,
    nodes,
    mine,
    theirs,
    out_weight,
    gain_one,
    ffn_in,
    ffn_bias,
    ffn_out,
    gain_two,
    state,
    ffn_input,
    act,
    slope,
    first,
    second,
    stats,
    sums,
    own_state,
    in_here,
    out_here,
    sems,
):
    step = pl.program_id(0)
    rows, width = nodes.shape
    fetches = [
        pltpu.make_async_copy(there, here, sems.at[place])
        for place, (there, here) in enumerate(((ffn_in, in_here), (ffn_out, out_here)))
    ]

    @pl.when(step == 0)
    def _():
        for fetch in fetches:
            fetch.start()

    total = mine[...].astype(f32) + theirs[...].astype(f32)
    count = jnp.maximum(total[width : width + 1, :], 1.0)
    ratio = 1.0 / jnp.broadcast_to(count, (128, rows)).T
    high, low = split(total[:width, :])
    sums[...] = high
    message = tn(high, out_weight[...]) + tn(low, out_weight[...])
    first_sum = nodes[...].astype(f32) + message * repeat_lanes(ratio, width)
    first_unit, first_inv = normed(first_sum)
    first[...] = first_unit.astype(bf16)
    first_norm = first_unit * gain_one[...]
    low = first_norm.astype(bf16)
    ffn_input[...] = own_columns(low, meta[4])

    @pl.when(step == 0)
    def _():
        for fetch in fetches:
            fetch.wait()

    hidden, grad = twice_gelu_and_slope(nn(low, in_here[...]) + ffn_bias[...])
    hidden = (0.5 * hidden).astype(bf16)
    act[...] = own_columns(hidden, meta[4])
    slope[...] = (0.5 * grad).astype(bf16)
    second_unit, second_inv = normed(first_norm + nn(hidden, out_here[...]))
    second[...] = second_unit.astype(bf16)
    out = (second_unit * gain_two[...]).astype(bf16)
    state[...] = out
    store_own_rows(own_state, out, step, meta[4])
    lane = lax.broadcasted_iota(jnp.int32, ratio.shape, 1)
    stats[...] = jnp.where(lane == 0, ratio, jnp.where(lane == 1, first_inv, second_inv))


def own_columns(values, core):
    half = values.shape[1] // 2
    return jnp.where(core == 0, values[:, :half], values[:, half:])


def store_own_rows(own, values, step, core):
    half, chunk = own.shape[0], values.shape[0]
    if chunk > half:
        own[...] = jnp.where(core == 0, values[:half, :], values[half:, :])
        return
    place = step * chunk

    @pl.when(place // half == core)
    def _():
        own[pl.ds(pl.multiple_of(lax.rem(place, half), chunk), chunk), :] = values


def node_forward(meta, nodes, mine, theirs, out_weight, gain_one, ffn_in, ffn_bias, ffn_out, gain_two):
    rows, model = nodes.shape
    hidden = ffn_in.shape[1]
    chunk = min(rows, FORWARD_CHUNK)

    def by_rows(width):
        return pl.BlockSpec((chunk, width), lambda i: (i, 0))

    return pl.pallas_call(
        node_forward_kernel,
        name="node_forward",
        grid=(rows // chunk,),
        in_specs=[
            smem,
            by_rows(model),
            pl.BlockSpec((model + 16, chunk), lambda i: (0, i)),
            pl.BlockSpec((model + 16, chunk), lambda i: (0, i)),
            whole(out_weight.shape),
            whole((1, model)),
            pl.BlockSpec(memory_space=pl.ANY),
            whole((1, hidden)),
            pl.BlockSpec(memory_space=pl.ANY),
            whole((1, model)),
        ],
        out_specs=[
            by_rows(model),
            by_rows(model // 2),
            by_rows(hidden // 2),
            by_rows(hidden),
            by_rows(model),
            by_rows(model),
            by_rows(128),
            pl.BlockSpec((model, chunk), lambda i: (0, i)),
            whole((rows // 2, model)),
        ],
        out_shape=[
            jax.ShapeDtypeStruct((rows, model), bf16),
            jax.ShapeDtypeStruct((rows, model // 2), bf16),
            jax.ShapeDtypeStruct((rows, hidden // 2), bf16),
            jax.ShapeDtypeStruct((rows, hidden), bf16),
            jax.ShapeDtypeStruct((rows, model), bf16),
            jax.ShapeDtypeStruct((rows, model), bf16),
            jax.ShapeDtypeStruct((rows, 128), f32),
            jax.ShapeDtypeStruct((model, rows), bf16),
            jax.ShapeDtypeStruct((rows // 2, model), bf16),
        ],
        scratch_shapes=[
            pltpu.VMEM(ffn_in.shape, bf16),
            pltpu.VMEM(ffn_out.shape, bf16),
            pltpu.SemaphoreType.DMA((2,)),
        ],
        compiler_params=params(63),
    )(
        meta, nodes, mine, theirs, out_weight, gain_one[None], ffn_in, ffn_bias[None], ffn_out, gain_two[None]
    )


def edge_kernel(
    static_first,
    meta,
    states,
    ids,
    edges,
    cots,
    residue_t,
    neighbour_t,
    edge_weight,
    bias,
    out_weight,
    out_weight_t,
    gain,
    new_edges,
    partial,
    back_table,
    grads,
    squares,
    vectors,
    padded,
    far_table,
    near_table,
    base,
    gains,
    far_sum,
    near_sum,
    own_sum,
    gain_sum,
    grad_edge,
    grad_out,
):
    step = pl.program_id(0)
    width, rows = base.shape
    window = window_of(rows)
    local_first = pl.multiple_of(meta[1], 128) if static_first is None else static_first

    @pl.when(step == 0)
    def _():
        fill = jnp.zeros((width, 256 - width), bf16)
        scaled_weight = (root_half * edge_weight[...].astype(f32)).astype(bf16)
        weight = jnp.concatenate([scaled_weight, fill], axis=1)
        projected = (root_half * nt(states[...], neighbour_t[...])).astype(bf16)
        projected = jnp.concatenate([projected, jnp.zeros((SPAN, 256 - width), bf16)], axis=1)
        far_table[...] = jnp.concatenate([projected, weight], axis=0).T[:width, :]
        padded[...] = jnp.zeros_like(padded)
        padded[REACH : REACH + SPAN, :] = projected
        for tile, _ in tiles(rows):
            part = padded[window_rows(local_first, rows, tile), :]
            near_table[tile] = jnp.concatenate([part, weight], axis=0).T[:width, :]
        block = states[pl.ds(local_first, rows), :]
        base[...] = root_half * (nt(residue_t[...], block) + repeat_lanes(bias[...], rows))
        gains[...] = repeat_lanes(gain[...], rows)
        for total in (far_sum, near_sum, own_sum, gain_sum, grad_edge, grad_out):
            total[...] = jnp.zeros_like(total)

    group = edges.shape[0]
    order = list(range(1, group, 2)) + list(range(0, group, 2))
    found_rows, found_grads = {}, {}
    for side in order:
        near = ids[pl.ds(group * step + side, 1), :] - meta[2]
        edge = edges[side]
        if side % 2 == 0:
            chosen = [
                near_rows(near[:, lanes], edges[side, :, lanes], local_first + lanes.start)
                for _, lanes in tiles(rows)
            ]
            value = jnp.concatenate(
                [nn(near_table[tile], part) for tile, part in enumerate(chosen)], axis=1
            )
        else:
            chosen = far_rows(near, edge)
            value = nn(far_table[...], chosen)
        act, slope = wide_gelu_and_slope(value + base[...])
        act = act.astype(bf16)
        third = edge.astype(f32) + nn(out_weight_t[...], act)
        centered = third - jnp.mean(third, 0, keepdims=True)
        inv_std = lax.rsqrt(jnp.mean(centered * centered, 0, keepdims=True) + epsilon)
        unit = centered * inv_std
        new_edges[side] = (unit * gains[...]).astype(bf16)
        cot = cots[side].astype(f32)
        gain_sum[...] += cot * unit
        scaled = cot * gains[...]
        grad_third = inv_std * (
            scaled
            - jnp.mean(scaled, 0, keepdims=True)
            - unit * jnp.mean(scaled * unit, 0, keepdims=True)
        )
        branch = grad_third.astype(bf16)
        grad_out[...] += nt(act, branch)
        grad_wide = nn(out_weight[...], branch) * slope
        own_sum[...] += grad_wide
        grad_value = grad_wide.astype(bf16)
        partial[side, :width, :] = branch
        partial[side, width:, :] = grad_value
        found_rows[side], found_grads[side] = chosen, grad_value
        if side == order[group // 2 - 1]:
            far_sum[...] += nt(
                beside([found_rows[k] for k in order[: group // 2]]),
                beside([found_grads[k] for k in order[: group // 2]]),
            )
    for tile, lanes in tiles(rows):
        found = nt(
            beside([found_rows[k][tile] for k in range(0, group, 2)]),
            beside([found_grads[k][:, lanes] for k in range(0, group, 2)]),
        )
        near_sum[window_rows(local_first, rows, tile), :] += found[:window, :]
        grad_edge[...] += found[window:, :]

    @pl.when(step == pl.num_programs(0) - 1)
    def _():
        table_high, table_low = split(far_sum[:SPAN, :] + near_sum[REACH : REACH + SPAN, :])
        own_high, own_low = split(own_sum[...])
        back = nn(table_high, neighbour_t[...]) + nn(table_low, neighbour_t[...])
        own_back = tn(own_high, residue_t[...]) + tn(own_low, residue_t[...])
        if rows == SPAN:
            back_table[...] = (back + own_back).astype(bf16)
        else:
            own_rows = pl.ds(local_first, rows)
            back_table[...] = back.astype(bf16)
            back_table[own_rows, :] = (back_table[own_rows, :].astype(f32) + own_back).astype(bf16)
        block = states[pl.ds(local_first, rows), :]
        grad_self = nn(own_high, block) + nn(own_low, block)
        grad_near = tn(table_high, states[...]) + tn(table_low, states[...])
        grads[:width, :] = grad_self
        grads[width:, :] = grad_near
        squares[...] = jnp.zeros_like(squares)
        squares[:, :width] = grad_edge[...] + far_sum[SPAN:, :]
        squares[:, 256 : 256 + width] = root_half * grad_out[...]
        vectors[...] = jnp.zeros_like(vectors)
        ones = jnp.ones((16, rows), bf16)
        gain_high, gain_low = split(gain_sum[...])
        vectors[0:1, :width] = (nt(ones, own_high) + nt(ones, own_low))[:1]
        vectors[1:2, :width] = (nt(ones, gain_high) + nt(ones, gain_low))[:1]


def edge_layer(
    meta, states, ids, edges, cots, residue, neighbour, edge_weight, bias, out_weight, out_weight_t, gain, local_first
):
    group = group_of(edges.shape[0], EDGE_GROUP)
    width, rows = edges.shape[1:]
    model = states.shape[1]
    by_pair = pl.BlockSpec((group, width, rows), lambda i: (i, 0, 0))
    square = whole((width, width))
    return pl.pallas_call(
        functools.partial(edge_kernel, local_first),
        name="edge_layer",
        grid=(edges.shape[0] // group,),
        in_specs=[
            smem,
            whole(states.shape),
            whole(ids.shape),
            by_pair,
            by_pair,
            whole((width, model)),
            whole((width, model)),
            square,
            whole((width, 128)),
            square,
            square,
            whole((width, 128)),
        ],
        out_specs=[
            by_pair,
            pl.BlockSpec((group, 2 * width, rows), lambda i: (i, 0, 0)),
            whole((SPAN, model)),
            whole((2 * width, model)),
            whole((width, model)),
            whole((8, model)),
        ],
        out_shape=[
            jax.ShapeDtypeStruct(edges.shape, bf16),
            jax.ShapeDtypeStruct((edges.shape[0], 2 * width, rows), bf16),
            jax.ShapeDtypeStruct((SPAN, model), bf16),
            jax.ShapeDtypeStruct((2 * width, model), f32),
            jax.ShapeDtypeStruct((width, model), f32),
            jax.ShapeDtypeStruct((8, model), f32),
        ],
        scratch_shapes=[
            pltpu.VMEM((SPAN + 2 * REACH, 256), bf16),
            pltpu.VMEM((width, SPAN + width), bf16),
            pltpu.VMEM((rows // tile_of(rows), width, window_of(rows) + width), bf16),
            pltpu.VMEM((width, rows), f32),
            pltpu.VMEM((width, rows), f32),
            pltpu.VMEM((SPAN + width, width), f32),
            pltpu.VMEM((SPAN + 2 * REACH, width), f32),
            pltpu.VMEM((width, rows), f32),
            pltpu.VMEM((width, rows), f32),
            pltpu.VMEM((width, width), f32),
            pltpu.VMEM((width, width), f32),
        ],
        compiler_params=params(),
    )(
        meta,
        states,
        ids,
        edges,
        cots,
        residue.T,
        neighbour.T,
        edge_weight,
        bias,
        out_weight,
        out_weight_t,
        gain,
    )


def norm_back(unit, inv_std, gain, grad_out):
    grad_gain = jnp.sum(grad_out * unit, axis=0, keepdims=True)
    scaled = grad_out * gain
    grad_in = inv_std * (
        scaled
        - jnp.mean(scaled, -1, keepdims=True)
        - unit * jnp.mean(scaled * unit, -1, keepdims=True)
    )
    return grad_in, grad_gain


def node_backward_kernel(
    meta,
    own_cot,
    other_cot,
    mine,
    theirs,
    first,
    second,
    stats,
    ffn_input,
    act,
    slope,
    sums,
    gain_one,
    ffn_in,
    ffn_out,
    gain_two,
    out_weight,
    own_grad,
    spread,
    weights,
    message_out,
    vectors,
    sum_out,
    sum_in,
    sum_message,
    in_here,
    out_here,
    sems,
):
    step = pl.program_id(0)
    chunk, model = first.shape
    hidden = slope.shape[1]
    core = meta[4]
    half = own_cot.shape[0]

    fetches = [
        pltpu.make_async_copy(there, here, sems.at[place])
        for place, (there, here) in enumerate(((ffn_in, in_here), (out_weight, out_here)))
    ]

    @pl.when(step == 0)
    def _():
        for fetch in fetches:
            fetch.start()
        vectors[...] = jnp.zeros_like(vectors)
        sum_out[...] = jnp.zeros_like(sum_out)
        sum_in[...] = jnp.zeros_like(sum_in)
        sum_message[...] = jnp.zeros_like(sum_message)

    if chunk > half:
        mine_first = core == 0
        lower = jnp.where(mine_first, own_cot[...], other_cot[...])
        cot = jnp.concatenate([lower, jnp.where(mine_first, other_cot[...], own_cot[...])], axis=0)
    else:
        row = step * chunk
        inside = pl.ds(pl.multiple_of(lax.rem(row, half), chunk), chunk)
        cot = jnp.where(row // half == core, own_cot[inside, :], other_cot[inside, :])
    total = cot.astype(f32) + (mine[...].astype(f32) + theirs[...].astype(f32))
    second_inv = stats[:, 2:3]
    first_inv = stats[:, 1:2]
    grad_second, gain_two_part = norm_back(second[...].astype(f32), second_inv, gain_two[...], total)
    top = grad_second.astype(bf16)
    grad_hidden = (nt(top, ffn_out[...]) * slope[...].astype(f32)).astype(bf16)
    sum_out[...] += tn(act[...], top)
    sum_in[...] += tn(ffn_input[...], grad_hidden)
    bias_part = jnp.sum(grad_hidden.astype(f32), axis=0, keepdims=True)

    @pl.when(step == 0)
    def _():
        for fetch in fetches:
            fetch.wait()

    grad_norm = grad_second + nt(grad_hidden, in_here[...])
    grad_first, gain_one_part = norm_back(first[...].astype(f32), first_inv, gain_one[...], grad_norm)
    store_own_rows(own_grad, grad_first, step, core)
    message_cot = (grad_first * stats[:, :1]).astype(bf16)
    spread[...] = (0.5 * nt(out_here[...], message_cot)).astype(bf16)
    sum_message[...] += nn(sums[pl.ds(pl.multiple_of(core * (model // 2), 16), model // 2), :], message_cot)
    vectors[0:1, :] += gain_one_part
    vectors[1:2, :] += gain_two_part
    for part in range(hidden // model):
        vectors[2 + part : 3 + part, :] += bias_part[:, part * model : (part + 1) * model]

    @pl.when(step == pl.num_programs(0) - 1)
    def _():
        weights[: hidden // 2, :] = sum_out[...].astype(bf16)
        for part in range(hidden // model):
            start = hidden // 2 + part * (model // 2)
            weights[start : start + model // 2, :] = sum_in[
                :, part * model : (part + 1) * model
            ].astype(bf16)
        message_out[...] = sum_message[...]


def node_backward(
    meta,
    own_cot,
    other_cot,
    mine,
    theirs,
    first,
    second,
    stats,
    ffn_input,
    act,
    slope,
    sums,
    gain_one,
    ffn_in,
    ffn_out,
    gain_two,
    out_weight,
):
    rows, model = first.shape
    hidden = slope.shape[1]
    chunk = min(rows, NODE_CHUNK)

    def by_rows(width):
        return pl.BlockSpec((chunk, width), lambda i: (i, 0))

    by_lanes = pl.BlockSpec((model, chunk), lambda i: (0, i))
    return pl.pallas_call(
        node_backward_kernel,
        name="node_backward",
        grid=(rows // chunk,),
        in_specs=[
            smem,
            whole(own_cot.shape),
            whole(other_cot.shape),
            by_rows(model),
            by_rows(model),
            by_rows(model),
            by_rows(model),
            by_rows(128),
            by_rows(model // 2),
            by_rows(hidden // 2),
            by_rows(hidden),
            by_lanes,
            whole((1, model)),
            pl.BlockSpec(memory_space=pl.ANY),
            whole(ffn_out.shape),
            whole((1, model)),
            pl.BlockSpec(memory_space=pl.ANY),
        ],
        out_specs=[
            whole(own_cot.shape),
            by_lanes,
            whole((hidden, model)),
            whole((model // 2, model)),
            whole((8, model)),
        ],
        out_shape=[
            jax.ShapeDtypeStruct(own_cot.shape, f32),
            jax.ShapeDtypeStruct((model, rows), bf16),
            jax.ShapeDtypeStruct((hidden, model), bf16),
            jax.ShapeDtypeStruct((model // 2, model), f32),
            jax.ShapeDtypeStruct((8, model), f32),
        ],
        scratch_shapes=[
            pltpu.VMEM((hidden // 2, model), f32),
            pltpu.VMEM((model // 2, hidden), f32),
            pltpu.VMEM((model // 2, model), f32),
            pltpu.VMEM(ffn_in.shape, bf16),
            pltpu.VMEM(out_weight.shape, bf16),
            pltpu.SemaphoreType.DMA((2,)),
        ],
        compiler_params=params(63),
    )(
        meta,
        own_cot,
        other_cot,
        mine,
        theirs,
        first,
        second,
        stats,
        ffn_input,
        act,
        slope,
        sums,
        gain_one[None],
        ffn_in,
        ffn_out,
        gain_two[None],
        out_weight,
    )


def message_backward_kernel(
    static_first,
    meta,
    table,
    spread,
    ids,
    edges,
    slope,
    receiver,
    neighbour,
    edge_grads,
    squares,
    message_out,
    edge_vectors,
    node_vectors,
    own_grad,
    keep,
    send,
    keep_weights,
    send_weights,
    far_sum,
    near_sum,
    own_sum,
    edge_sum,
    weights,
    table_here,
    receiver_here,
    neighbour_here,
    edge_grads_here,
    squares_here,
    message_out_here,
    own_grad_here,
    sems,
):
    step = pl.program_id(0)
    model, rows = spread.shape
    group, width = edges.shape[:2]
    half = keep.shape[0]
    window = window_of(rows)
    local_first = pl.multiple_of(meta[1], 128) if static_first is None else static_first

    at_the_end = (
        (table, table_here),
        (receiver, receiver_here),
        (neighbour, neighbour_here),
        (edge_grads, edge_grads_here),
        (squares, squares_here),
        (message_out, message_out_here),
        (own_grad, own_grad_here),
    )
    fetches = [
        pltpu.make_async_copy(there, here, sems.at[place]) for place, (there, here) in enumerate(at_the_end)
    ]

    @pl.when(step == 0)
    def _():
        for fetch in fetches:
            fetch.start()
        for total in (far_sum, near_sum, own_sum, edge_sum):
            total[...] = jnp.zeros_like(total)

    near = [ids[pl.ds(group * step + k, 1), :] - meta[2] for k in range(group)]
    grads = [spread[...] * slope[k] for k in range(group)]
    own_sum[...] += sum(grad.astype(f32) for grad in grads)
    far_sum[...] += nt(
        beside([far_rows(near[k], edges[k]) for k in range(1, group, 2)]), beside(grads[1::2])
    )
    for tile, lanes in tiles(rows):
        first = local_first + lanes.start
        part = beside([near_rows(near[k][:, lanes], edges[k, :, lanes], first) for k in range(0, group, 2)])
        found = nt(part, beside([grad[:, lanes] for grad in grads[::2]]))
        near_sum[window_rows(local_first, rows, tile), :] += found[:window, :]
        edge_sum[...] += found[window:, :]

    @pl.when(step == pl.num_programs(0) - 1)
    def _():
        for fetch in fetches:
            fetch.wait()
        table_sum = (far_sum[:SPAN, :] + near_sum[REACH : REACH + SPAN, :]).astype(bf16)
        own_rows = own_sum[...].T
        own_low = own_rows.astype(bf16)
        nodes_t = table_here[...].T
        block_t = nodes_t
        if rows < SPAN:
            block_t = table_here[pl.ds(local_first, rows), :].T
        split_rows = keep_weights.shape[0]
        for core, start in enumerate((0, split_rows)):
            if core == 0:
                weights[:model, :] = nn(block_t, own_low)
                third = edge_sum[...] + far_sum[SPAN:, :]
            else:
                weights[start : start + model, :] = nn(nodes_t, table_sum)
                third = squares_here[...]
            start += model
            weights[start : start + width, :] = third
            start += width
            weights[start : start + width, :] = edge_grads_here[core * width : (core + 1) * width, :]
            start += width
            weights[start : start + model // 2, :] = jnp.where(meta[4] == core, message_out_here[...], 0.0)
            start += model // 2
            if core == 0:
                weights[start:split_rows, :] = jnp.zeros((split_rows - start, model), f32)
        weights[start : start + 8, :] = edge_vectors[...]
        weights[start + 8 : start + 16, :] = 0.5 * node_vectors[...]
        weights[start + 16 :, :] = jnp.broadcast_to(
            jnp.sum(own_rows, axis=0, keepdims=True), (2 * split_rows - start - 16, model)
        )
        mine = pl.multiple_of(meta[4] * split_rows, split_rows)
        keep_weights[...] = weights[pl.ds(mine, split_rows), :]
        send_weights[...] = weights[pl.ds(split_rows - mine, split_rows), :].astype(bf16)
        back = nt(table_sum, neighbour_here[...])
        own_back = nt(own_low, receiver_here[...])
        if rows == SPAN:
            far_sum[:SPAN, :] = back + own_back
        else:
            far_sum[:SPAN, :] = back
            far_sum[pl.ds(local_first, rows), :] += own_back
        high = meta[0]
        kept = far_sum[pl.ds(pl.multiple_of(high * half, half), half), :]
        keep[...] = kept + own_grad_here[...] if own_grad_here.shape[0] == half else kept
        send[...] = far_sum[pl.ds(pl.multiple_of((1 - high) * half, half), half), :].astype(bf16)


def message_backward(
    meta,
    table,
    spread,
    ids,
    edges,
    slope,
    receiver,
    neighbour,
    edge_grads,
    squares,
    message_out,
    edge_vectors,
    node_vectors,
    own_grad,
    local_first,
):
    group = group_of(edges.shape[0], MSG_GROUP)
    width, rows = edges.shape[1:]
    model = table.shape[1]
    anywhere = pl.BlockSpec(memory_space=pl.ANY)
    late = (table, receiver, neighbour, edge_grads, squares, message_out, own_grad)
    split_rows = -(-(model + 2 * width + model // 2 + 24) // 256) * 256
    return pl.pallas_call(
        functools.partial(message_backward_kernel, local_first),
        name="message_backward",
        grid=(edges.shape[0] // group,),
        in_specs=[
            smem,
            anywhere,
            whole(spread.shape),
            whole(ids.shape),
            pl.BlockSpec((group, width, rows), lambda i: (i, 0, 0)),
            pl.BlockSpec((group, model, rows), lambda i: (i, 0, 0)),
            anywhere,
            anywhere,
            anywhere,
            anywhere,
            anywhere,
            whole(edge_vectors.shape),
            whole(node_vectors.shape),
            anywhere,
        ],
        out_specs=[
            whole((SPAN // 2, model)),
            whole((SPAN // 2, model)),
            whole((split_rows, model)),
            whole((split_rows, model)),
        ],
        out_shape=[
            jax.ShapeDtypeStruct((SPAN // 2, model), f32),
            jax.ShapeDtypeStruct((SPAN // 2, model), bf16),
            jax.ShapeDtypeStruct((split_rows, model), f32),
            jax.ShapeDtypeStruct((split_rows, model), bf16),
        ],
        scratch_shapes=[
            pltpu.VMEM((SPAN + width, model), f32),
            pltpu.VMEM((SPAN + 2 * REACH, model), f32),
            pltpu.VMEM((model, rows), f32),
            pltpu.VMEM((width, model), f32),
            pltpu.VMEM((2 * split_rows, model), f32),
        ]
        + [pltpu.VMEM(value.shape, value.dtype) for value in late]
        + [pltpu.SemaphoreType.DMA((len(late),))],
        compiler_params=params(),
    )(
        meta,
        table,
        spread,
        ids,
        edges,
        slope,
        receiver,
        neighbour,
        edge_grads,
        squares,
        message_out,
        edge_vectors,
        node_vectors,
        own_grad,
    )


def edge_gradient_kernel(partial, slope, spread, message_weight, edge_weight, *rest):
    out = rest[-1]
    width = out.shape[1]
    weights = jnp.concatenate([message_weight[...], edge_weight[...]], axis=1)
    for k in range(out.shape[0]):
        grads = jnp.concatenate([spread[...] * slope[k], partial[k, width:, :]], axis=0)
        out[k] = partial[k, :width, :].astype(f32) + nn(weights, grads)


def edge_gradient(first, count, filled, partial, slope, spread, message_weight, edge_weight):
    columns_in, width, rows = partial.shape
    width //= 2
    model = spread.shape[0]

    def pair(size):
        return pl.BlockSpec((2, size, rows), lambda i: (first + i, 0, 0))

    before = [] if filled is None else [filled]
    return pl.pallas_call(
        edge_gradient_kernel,
        name="edge_gradient",
        grid=(count,),
        in_specs=[
            pair(2 * width),
            pair(model),
            whole(spread.shape),
            whole(message_weight.shape),
            whole(edge_weight.shape),
        ]
        + [pl.BlockSpec(memory_space=pl.ANY)] * len(before),
        out_specs=pair(width),
        out_shape=jax.ShapeDtypeStruct((columns_in, width, rows), f32),
        input_output_aliases={5: 0} if before else {},
        compiler_params=params(54),
    )(partial, slope, spread, message_weight, edge_weight, *before)


def sum_to_slots_kernel(shift, meta, *refs):
    parts, outs, total = refs[:-5], refs[-5:-1], refs[-1]
    total[...] = parts[0][...].astype(f32)
    for part in parts[1:]:
        total[...] += part[...].astype(f32)
    place = meta[5] >> shift & 3
    rows = outs[0].shape[0]
    for slot, out in enumerate(outs):
        start = pl.multiple_of((place ^ slot) * rows, rows)
        out[...] = total[pl.ds(start, rows), :].astype(out.dtype)


def sum_to_slots(meta, shift, parts):
    rows, width = parts[0].shape
    out_types = (f32, bf16, bf16, bf16)
    return pl.pallas_call(
        functools.partial(sum_to_slots_kernel, shift),
        name="sum_to_slots",
        in_specs=[smem] + [whole(part.shape) for part in parts],
        out_specs=[whole((rows // 4, width))] * 4,
        out_shape=[jax.ShapeDtypeStruct((rows // 4, width), kind) for kind in out_types],
        scratch_shapes=[pltpu.VMEM((rows, width), f32)],
        compiler_params=params(12),
    )(meta, *parts)


def sum_parts_kernel(*refs):
    total = refs[0][...].astype(f32)
    for part in refs[1:-1]:
        total = total + part[...].astype(f32)
    refs[-1][...] = total.astype(bf16)


def sum_parts(parts):
    return pl.pallas_call(
        sum_parts_kernel,
        name="sum_parts",
        in_specs=[whole(part.shape) for part in parts],
        out_specs=whole(parts[0].shape),
        out_shape=jax.ShapeDtypeStruct(parts[0].shape, bf16),
        compiler_params=params(12),
    )(*parts)


def assemble_kernel(shift, meta, *refs):
    place = meta[5] >> shift & 3
    rows = refs[0].shape[0]
    for slot, part in enumerate(refs[:-1]):
        start = pl.multiple_of((place ^ slot) * rows, rows)
        refs[-1][pl.ds(start, rows), :] = part[...]


def assemble(meta, shift, parts):
    rows, width = parts[0].shape
    return pl.pallas_call(
        functools.partial(assemble_kernel, shift),
        name="assemble",
        in_specs=[smem] + [whole(part.shape) for part in parts],
        out_specs=whole((4 * rows, width)),
        out_shape=jax.ShapeDtypeStruct((4 * rows, width), bf16),
        compiler_params=params(12),
    )(meta, *parts)


def sent_each_way(shift, slots):
    return [moved(slot, place << shift) for place, slot in enumerate(slots) if place > 0]


def moved(value, mask):
    devices = lax.axis_size("res") * lax.axis_size("nbr")
    cores = lax.axis_size("nbr")
    pairs = [(source, source ^ (mask * cores)) for source in range(devices)]
    return lax.ppermute(value, ("res", "nbr"), pairs)


def unpack_early_kernel(side, meta, source, *rest):
    grad_out, grad_in, wide, out_sem, in_sem = rest[-5:]
    place = meta[4] if side == 0 else 1 - meta[4]
    model, hidden = grad_in.shape
    wide[...] = source[...].astype(f32)
    half, quarter = hidden // 2, model // 2
    copies = [
        pltpu.make_async_copy(
            wide.at[:half], grad_out.at[pl.ds(pl.multiple_of(place * half, half), half)], out_sem
        )
    ]
    for part in range(hidden // model):
        start = half + part * quarter
        copies.append(
            pltpu.make_async_copy(
                wide.at[start : start + quarter],
                grad_in.at[
                    pl.ds(pl.multiple_of(place * quarter, quarter), quarter),
                    part * model : (part + 1) * model,
                ],
                in_sem.at[part],
            )
        )
    for copy in copies:
        copy.start()
    for copy in copies:
        copy.wait()


def unpack_early(meta, side, source, before):
    rows, model = source.shape
    anywhere = pl.BlockSpec(memory_space=pl.ANY)
    return pl.pallas_call(
        functools.partial(unpack_early_kernel, side),
        name="unpack_early",
        in_specs=[smem, whole(source.shape)] + [anywhere] * len(before),
        out_specs=[anywhere, anywhere],
        out_shape=[
            jax.ShapeDtypeStruct((rows, model), f32),
            jax.ShapeDtypeStruct((model, rows), f32),
        ],
        scratch_shapes=[
            pltpu.VMEM((rows, model), f32),
            pltpu.SemaphoreType.DMA,
            pltpu.SemaphoreType.DMA((rows // model,)),
        ],
        input_output_aliases={2: 0, 3: 1} if before else {},
        compiler_params=params(),
    )(meta, source, *before)


def unpack_late_kernel(
    meta, own, other, grad_self, grad_near, grad_edge, edge_edge, edge_out, edge_self, edge_near, message_out, *vectors
):
    lower = meta[4] == 0
    model = own.shape[1]
    width = edge_edge.shape[0]
    first = jnp.where(lower, own[...], other[...]).astype(f32)
    second = jnp.where(lower, other[...], own[...]).astype(f32)
    grad_self[...] = first[:model, :]
    grad_near[...] = second[:model, :]
    start = model + width
    grad_edge[...] = first[model:start, :]
    edge_edge[...] = second[model:start, :width]
    edge_out[...] = second[model:start, 256 : 256 + width]
    edge_self[...] = first[start : start + width, :]
    edge_near[...] = second[start : start + width, :]
    start += width
    half = model // 2
    message_out[:half, :] = first[start : start + half, :]
    message_out[half:, :] = second[start : start + half, :]
    start += half
    edge_bias, gain_three, gain_one, gain_two, message_bias, ffn_bias = vectors
    edge_bias[...] = second[start : start + 1, :width]
    gain_three[...] = second[start + 1 : start + 2, :width]
    gain_one[...] = second[start + 8 : start + 9, :]
    gain_two[...] = second[start + 9 : start + 10, :]
    message_bias[...] = second[start + 16 : start + 17, :]
    for part in range(ffn_bias.shape[1] // model):
        row = start + 10 + part
        ffn_bias[:, part * model : (part + 1) * model] = second[row : row + 1, :]


def unpack_late(meta, own, other, width, hidden):
    model = own.shape[1]
    shapes = [(model, model)] * 2 + [(width, model)] + [(width, width)] * 2 + [(width, model)] * 2
    shapes += [(model, model)] + [(1, size) for size in (width, width, model, model, model, hidden)]
    return pl.pallas_call(
        unpack_late_kernel,
        name="unpack_late",
        in_specs=[smem, whole(own.shape), whole(other.shape)],
        out_specs=[whole(shape) for shape in shapes],
        out_shape=[jax.ShapeDtypeStruct(shape, f32) for shape in shapes],
        compiler_params=params(),
    )(meta, own, other)


def planes(size):
    return [[4 * block + place for place in range(4)] for block in range(size // 4)]


def columns(size):
    return [[4 * block + place for block in range(size // 4)] for place in range(4)]


def tied(*arrays):
    return lax.optimization_barrier(arrays)


def weight_sums(meta, early, kept, sent, kept_nodes, nodes, size, pieces):
    received = swapped(sent, 0)
    early = lax.psum(early, "res", axis_index_groups=columns(size))
    value, received, given = tied(pieces[0](None), received, swapped(nodes, 0))
    node_grad = kept_nodes + given.astype(f32)
    value, kept, *slots = tied(value, *sum_to_slots(meta, 0, [kept, received]))
    value, node_grad, *received = tied(pieces[1](value), node_grad, *sent_each_way(0, [kept, *slots]))
    value, kept, *slots = tied(value, *sum_to_slots(meta, 2, [kept, *received]))
    value, *received = tied(pieces[2](value), *sent_each_way(2, [kept, *slots]))
    value, early, late = tied(value, early, sum_parts([kept, *received]))
    early = lax.all_gather(early, "res", axis_index_groups=planes(size), tiled=True)
    value, *received = tied(pieces[3](value), *sent_each_way(2, [late] * 4))
    value, late = tied(value, assemble(meta, 2, [late, *received]))
    value, *received = tied(pieces[4](value), *sent_each_way(0, [late] * 4))
    return early, assemble(meta, 0, [late, *received]), value, node_grad


def joined(table, other, high_side):
    return jnp.where(
        high_side, jnp.concatenate([other, table], axis=0), jnp.concatenate([table, other], axis=0)
    )


def halves(table, high_side):
    half = table.shape[0] // 2
    lower, upper = (table[:half], table[half:])
    return (jnp.where(high_side, upper, lower), jnp.where(high_side, lower, upper))


def sum_blocks(table, device, level):
    keep, send = halves(table, device >> level & 1 == 1)
    return keep + swapped(send.astype(bf16), level).astype(keep.dtype)


def on_device(
    nodes,
    edges,
    neighbours,
    lengths,
    message_receiver_weight,
    message_neighbour_weight,
    message_edge_weight,
    message_hidden_bias,
    message_output_weight,
    gain_one,
    ffn_in,
    ffn_bias,
    ffn_out,
    gain_two,
    edge_update_residue_weight,
    edge_update_neighbour_weight,
    edge_update_edge_weight,
    edge_update_bias,
    edge_out,
    gain_three,
    node_cot,
    edge_cot,
):
    rows, half_k, edge_width = edges.shape
    own_rows, model = nodes.shape
    hidden = ffn_in.shape[1]
    levels = (SPAN // own_rows).bit_length() - 1
    core = lax.axis_index("nbr")
    device = lax.axis_index("res") * lax.axis_size("nbr") + core
    first_row = lax.axis_index("res") * rows
    bucket = first_row // SPAN
    group_start = bucket * SPAN
    local_first = 0 if rows == SPAN else None
    top = device >> (levels - 1) & 1
    meta = jnp.stack(
        [top, first_row - group_start, group_start, bucket, core, lax.axis_index("res"), 0, 0]
    ).astype(jnp.int32)

    ids = neighbours.T
    edges_t = edges.transpose(1, 2, 0)
    cot_t = edge_cot.transpose(1, 2, 0)

    table = nodes
    for level in range(levels - 1):
        table = joined(table, swapped(table, level), device >> level & 1 == 1)
    other_table = swapped(table, levels - 1)
    other_cot = swapped(node_cot, 0)

    node_table, slope, packed = message_forward(
        meta,
        lengths,
        table,
        other_table,
        ids,
        edges_t,
        message_receiver_weight,
        message_neighbour_weight,
        message_edge_weight,
        message_hidden_bias,
        local_first,
    )
    theirs, *edge_parts = tied(
        swapped(packed, 0),
        jnp.broadcast_to(edge_update_bias[:, None], (edge_width, 128)),
        edge_out * 0.5,
        (edge_out.T.astype(f32) * root_half).astype(bf16),
        jnp.broadcast_to(gain_three[:, None], (edge_width, 128)),
    )
    block = node_table
    if rows < SPAN:
        block = lax.dynamic_slice_in_dim(node_table, first_row - group_start, rows, 0)
    state, ffn_input, act, ffn_slope, first, second, stats, sums, node_out = node_forward(
        meta,
        block,
        packed,
        theirs,
        message_output_weight,
        gain_one,
        ffn_in,
        ffn_bias,
        ffn_out,
        gain_two,
    )
    states = state
    for level in range(1, levels):
        states = joined(states, swapped(states, level), device >> level & 1 == 1)
    new_edges, partial, back, edge_grads, squares, edge_vectors = edge_layer(
        meta,
        states,
        ids,
        edges_t,
        cot_t,
        edge_update_residue_weight,
        edge_update_neighbour_weight,
        edge_update_edge_weight,
        *edge_parts,
        local_first,
    )
    for level in reversed(range(1, levels)):
        back = sum_blocks(back, device, level)
    own_grad, spread, early, message_out, node_vectors = node_backward(
        meta,
        node_cot,
        other_cot,
        back,
        swapped(back, 0),
        first,
        second,
        stats,
        ffn_input,
        act,
        ffn_slope,
        sums,
        gain_one,
        ffn_in,
        ffn_out,
        gain_two,
        message_output_weight,
    )
    size = lax.axis_size("res")
    if size == 16:
        early = lax.psum_scatter(early, "res", axis_index_groups=planes(size), tiled=True)
    else:
        early = lax.psum(early.astype(f32), "res").astype(bf16)
    keep, send, kept_weights, sent_weights = message_backward(
        meta,
        node_table,
        spread,
        ids,
        edges_t,
        slope,
        message_receiver_weight,
        message_neighbour_weight,
        edge_grads,
        squares,
        message_out,
        edge_vectors,
        node_vectors,
        own_grad,
        local_first,
    )
    early, kept_weights, sent_weights = tied(early, kept_weights, sent_weights)
    counts = [1, 5, 4, 1, 4] if half_k == 30 else [half_k // 2]
    starts = [sum(counts[:index]) for index in range(len(counts))]

    def piece(start, count):
        return lambda filled: edge_gradient(
            start, count, filled, partial, slope, spread, message_edge_weight, edge_update_edge_weight
        )

    spans = [piece(*span) for span in zip(starts, counts)]
    if size == 16:
        early, late, edge_grad, node_grad = weight_sums(
            meta, early, kept_weights, sent_weights, keep, send, size, spans
        )
    else:
        late = lax.psum(kept_weights + swapped(sent_weights, 0).astype(f32), "res").astype(bf16)
        edge_grad = None
        for span in spans:
            edge_grad = span(edge_grad)
        node_grad = keep + swapped(send, levels - 1).astype(f32)
        for level in reversed(range(levels - 1)):
            node_grad = sum_blocks(node_grad, device, level)
        if levels > 1:
            node_grad = own_grad + node_grad
    late_other = swapped(late, 0)
    (
        grad_msg_self,
        grad_msg_nbr,
        grad_msg_edge,
        grad_edge_edge,
        grad_edge_out,
        grad_edge_self,
        grad_edge_nbr,
        grad_msg_out,
        grad_edge_bias,
        grad_gain_three,
        grad_gain_one,
        grad_gain_two,
        grad_msg_bias,
        grad_ffn_bias,
    ) = unpack_late(meta, late, late_other, edge_width, hidden)
    early, edge_grad, grad_msg_self = tied(early, edge_grad, grad_msg_self)
    early_other, *halves_out = tied(swapped(early, 0), *unpack_early(meta, 0, early, []))
    grad_ffn_out, grad_ffn_in = unpack_early(meta, 1, early_other, halves_out)
    return (
        node_out,
        new_edges.transpose(2, 0, 1),
        node_grad,
        edge_grad.transpose(2, 0, 1),
        grad_msg_self,
        grad_msg_nbr,
        grad_msg_edge,
        grad_msg_bias[0],
        grad_msg_out,
        grad_gain_one[0],
        grad_ffn_in,
        grad_ffn_bias[0],
        grad_ffn_out,
        grad_gain_two[0],
        grad_edge_self.T,
        grad_edge_nbr.T,
        grad_edge_edge,
        grad_edge_bias[0],
        grad_edge_out,
        grad_gain_three[0],
    )


def solution(mesh):
    rows = P(("res", "nbr"), None)
    pairs = P("res", "nbr", None)
    placed = (rows, pairs, P("res", "nbr")) + (P(),) * 17 + (rows, pairs)
    return jax.shard_map(
        on_device,
        mesh=mesh,
        in_specs=placed,
        out_specs=(rows, pairs, rows, pairs) + (P(),) * 16,
        check_vma=False,
    )
```
